32 devices in a mesh: dp: 16 (over z, y, core), fsdp: 2 (over x).
Axes of the slice: x: 2, y: 2, z: 4, core: 2. Of those that a mesh axis runs over, the one named last changes fastest.
Arguments:
- frames: bfloat16 [4096, 1024], P(('dp', 'fsdp')), may hold values from -6 to 6
- lengths: int32 [32, 4], P(('dp', 'fsdp')), may hold values from 1 to 80, 112 in all within a row
- cotangent: bfloat16 [4096, 1024], P(('dp', 'fsdp')), may hold values from -6 to 6
- conv_kernel: bfloat16 [1024, 8192], P(('dp', 'fsdp')), may hold values from -0.125 to 0.125
- conv_bias: bfloat16 [1024], P(('dp', 'fsdp')), may hold values from -1.75 to 1.75
- norm_one_gain: bfloat16 [1024], P(('dp', 'fsdp')), may hold values from 0.5 to 1.5
- norm_one_bias: bfloat16 [1024], P(('dp', 'fsdp')), may hold values from -1.75 to 1.75
- query_weight: bfloat16 [1024, 1024], P(('dp', 'fsdp')), may hold values from -0.25 to 0.25
- query_bias: bfloat16 [1024], P(('dp', 'fsdp')), may hold values from -3 to 3
- key_weight: bfloat16 [1024, 1024], P(('dp', 'fsdp')), may hold values from -0.25 to 0.25
- value_weight: bfloat16 [1024, 1024], P(('dp', 'fsdp')), may hold values from -0.1875 to 0.1875
- value_bias: bfloat16 [1024], P(('dp', 'fsdp')), may hold values from -1.75 to 1.75
- out_weight: bfloat16 [1024, 1024], P(('dp', 'fsdp')), may hold values from -0.5 to 0.5
- out_bias: bfloat16 [1024], P(('dp', 'fsdp')), may hold values from -1.75 to 1.75
- norm_two_gain: bfloat16 [1024], P(('dp', 'fsdp')), may hold values from 0.5 to 1.5
- norm_two_bias: bfloat16 [1024], P(('dp', 'fsdp')), may hold values from -1.75 to 1.75
- up_weight: bfloat16 [1024, 4096], P(('dp', 'fsdp')), may hold values from -0.1875 to 0.1875
- up_bias: bfloat16 [4096], P(('dp', 'fsdp')), may hold values from -1.75 to 1.75
- down_weight: bfloat16 [4096, 1024], P(('dp', 'fsdp')), may hold values from -0.09375 to 0.09375
- down_bias: bfloat16 [1024], P(('dp', 'fsdp')), may hold values from -1.75 to 1.75
Outputs:
- output: bfloat16 [4096, 1024], P(('dp', 'fsdp'))
- frames_grad: float32 [4096, 1024], P(('dp', 'fsdp'))
- conv_kernel_grad: float32 [1024, 8192], P(('dp', 'fsdp'))
- conv_bias_grad: float32 [1024], P(('dp', 'fsdp'))
- norm_one_gain_grad: float32 [1024], P(('dp', 'fsdp'))
- norm_one_bias_grad: float32 [1024], P(('dp', 'fsdp'))
- query_weight_grad: float32 [1024, 1024], P(('dp', 'fsdp'))
- query_bias_grad: float32 [1024], P(('dp', 'fsdp'))
- key_weight_grad: float32 [1024, 1024], P(('dp', 'fsdp'))
- value_weight_grad: float32 [1024, 1024], P(('dp', 'fsdp'))
- value_bias_grad: float32 [1024], P(('dp', 'fsdp'))
- out_weight_grad: float32 [1024, 1024], P(('dp', 'fsdp'))
- out_bias_grad: float32 [1024], P(('dp', 'fsdp'))
- norm_two_gain_grad: float32 [1024], P(('dp', 'fsdp'))
- norm_two_bias_grad: float32 [1024], P(('dp', 'fsdp'))
- up_weight_grad: float32 [1024, 4096], P(('dp', 'fsdp'))
- up_bias_grad: float32 [4096], P(('dp', 'fsdp'))
- down_weight_grad: float32 [4096, 1024], P(('dp', 'fsdp'))
- down_bias_grad: float32 [1024], P(('dp', 'fsdp'))
The draws below stay inside these ranges and needn't reach their ends.
Inputs may be any that keep to these rules, and one draw needn't show every extreme that they name: `lengths`: row j lists the utterances of frame block j from its first slot on; they fill the first 112 slots, the rest is padding, and the longest is exactly 80.
All inputs are finite; a program needn't handle non-finite values.
Results may differ from the reference program's by a relative error of at most 0.015.
Values may be sent and summed in bfloat16 or wider, within the bound.
No kernel may reach another device: no remote copies, remote signals or barrier semaphores. Data moves between devices by JAX's collectives and lax.ppermute only.
A program may use at most 512 MiB of HBM per device.

```python
import math
from functools import partial
import jax
import jax.numpy as jnp
import numpy as np
from jax import lax

D = 1024
FF = 4096
HEAD_DIM = 64
GROUPS = 16
KW = 128
TOK_DEV = 128
UTT = 4
TOKENS = 4096
N_DP = 16
N_FSDP = 2


def block_scale(own_key, extent, shards, low, high):
    factor_of = 1.0
    for position, blocks in shards:
        heights = jax.random.uniform(jax.random.fold_in(jax.random.fold_in(own_key, 6), position), (blocks,), jnp.float32, low / len(shards), high / len(shards))
        factor_of = factor_of * jnp.repeat(jnp.exp(heights), extent[position] // blocks).reshape((-1,) + (1,) * (len(extent) - 1 - position))
    return factor_of


def split_up(number_of, total, bound, slope):
    weights = [(1 << 20) // math.isqrt(standing ** slope) + 1 for standing in range(2, number_of + 1)]
    rest, holding = total - bound - (number_of - 1), [1] * (number_of - 1)
    while rest > 0:
        candidates = [i for i in range(number_of - 1) if holding[i] < bound]
        mass, budget = sum([weights[i] for i in candidates]), rest
        for i in candidates:
            addition = min(bound - holding[i], max(1, budget * weights[i] // mass), rest)
            holding[i] = holding[i] + addition
            rest = rest - addition
    return np.array([bound] + holding)


def uneven(rng, number_of, total, bound, skew):
    if number_of == 2:
        one = jax.random.randint(rng, (), max(1, total - bound), min(bound, total - 1) + 1)
        return jnp.stack([one, total - one])
    tallies = jnp.asarray(split_up(number_of, total, bound, skew), jnp.int32)
    twos = (number_of - 1) // 2
    giver, taker = tallies[1:1 + 2 * twos:2], tallies[2:2 + 2 * twos:2]
    slack = jnp.minimum(giver - 1, bound - taker)
    passed = jax.random.randint(jax.random.fold_in(rng, 1), (twos,), 0, 1 << 20) % (slack + 1)
    tallies = tallies.at[1:1 + 2 * twos:2].set(giver - passed).at[2:2 + 2 * twos:2].set(taker + passed)
    return tallies[jax.random.permutation(jax.random.fold_in(rng, 2), number_of)]


def normal_values(rng, dims, scale, reach, cuts=(), held_as=jnp.bfloat16):
    entries = scale * jax.random.normal(rng, dims, jnp.float32)
    if cuts:
        entries = entries * block_scale(rng, dims, cuts, -0.22, 0.18)
    return jnp.clip(entries, -reach, reach).astype(held_as)


def setup_inputs(seed: int = 0) -> dict:
    key_list = jax.random.split(jax.random.key(seed), 21)
    return {
        "frames": normal_values(key_list[0], (TOKENS, D), 1.0, 6.0, ((0, 32),)),
        "lengths": jax.vmap(lambda own: uneven(own, UTT, 7 * TOK_DEV // 8, 5 * TOK_DEV // 8, 2))(jax.random.split(key_list[1], (N_DP * N_FSDP))).reshape((N_DP * N_FSDP, UTT)).astype(jnp.int32),
        "cotangent": normal_values(key_list[2], (TOKENS, D), 1.0, 6.0, ((0, 32),)),
        "conv_kernel": normal_values(key_list[3], (D, KW * (D // GROUPS)), (KW * (D // GROUPS) // 4) ** -0.5, 0.125, ((0, 32),)),
        "conv_bias": normal_values(key_list[4], (D,), 0.3, 1.75, ((0, 32),)),
        "norm_one_gain": jnp.clip(1.0 + 0.1 * jax.random.normal(key_list[5], (D,), jnp.float32), 0.5, 1.5).astype(jnp.bfloat16),
        "norm_one_bias": normal_values(key_list[6], (D,), 0.3, 1.75, ((0, 32),)),
        "query_weight": normal_values(key_list[7], (D, D), (D // 2) ** -0.5, 0.25, ((0, 32),)),
        "query_bias": normal_values(key_list[8], (D,), 0.5, 3.0, ((0, 32),)),
        "key_weight": normal_values(key_list[9], (D, D), (D // 2) ** -0.5, 0.25, ((0, 32),)),
        "value_weight": normal_values(key_list[10], (D, D), D ** -0.5, 0.1875, ((0, 32),)),
        "value_bias": normal_values(key_list[11], (D,), 0.3, 1.75, ((0, 32),)),
        "out_weight": normal_values(key_list[12], (D, D), (D // 8) ** -0.5, 0.5, ((0, 32),)),
        "out_bias": normal_values(key_list[13], (D,), 0.3, 1.75, ((0, 32),)),
        "norm_two_gain": jnp.clip(1.0 + 0.1 * jax.random.normal(key_list[14], (D,), jnp.float32), 0.5, 1.5).astype(jnp.bfloat16),
        "norm_two_bias": normal_values(key_list[15], (D,), 0.3, 1.75, ((0, 32),)),
        "up_weight": normal_values(key_list[16], (D, FF), D ** -0.5, 0.1875, ((0, 32),)),
        "up_bias": normal_values(key_list[17], (FF,), 0.3, 1.75, ((0, 32),)),
        "down_weight": normal_values(key_list[18], (FF, D), FF ** -0.5, 0.09375, ((0, 32),)),
        "down_bias": normal_values(key_list[19], (D,), 0.3, 1.75, ((0, 32),)),
    }


norm_eps = 1e-05
score_scale = 0.125

@jax.custom_vjp
def low(v):
    return lax.optimization_barrier(v.astype(jnp.bfloat16)).astype(jnp.float32)

@jax.custom_vjp
def low_back(v):
    return v

def low_keep(v):
    return (low(v), None)

def low_pass(kept, grad):
    return (grad,)

def back_keep(v):
    return (v, None)

def back_low(kept, grad):
    return (low(grad),)
low.defvjp(low_keep, low_pass)
low_back.defvjp(back_keep, back_low)

def matmul_high(left, right):
    return jnp.dot(left, right, precision=lax.Precision.HIGHEST)

def layer_norm(rows, scale_vec, shift_vec):
    row_mean = lax.optimization_barrier(jnp.mean(rows, axis=-1, keepdims=True))
    centred = rows - row_mean
    spread = lax.optimization_barrier(jnp.mean(centred * centred, axis=-1, keepdims=True))
    return centred * lax.rsqrt(spread + norm_eps) * scale_vec + shift_vec

def gelu_exact(values):
    return jax.nn.gelu(values, approximate=False)

def unfold(source, segment, first_tap, tap_count, flipped):
    rows_count = source.shape[0]
    model_width = source.shape[1]
    half_width = KW // 2
    padded = jnp.pad(source, ((half_width, half_width), (0, 0)))
    seg_padded = jnp.pad(segment, (half_width, half_width), constant_values=-1)
    pieces = []
    for tap_index in range(first_tap, first_tap + tap_count):
        offset = KW - tap_index if flipped else tap_index
        same_seg = seg_padded[offset:offset + rows_count] == segment
        pieces.append(jnp.where(same_seg[:, None], padded[offset:offset + rows_count], jnp.zeros((), source.dtype)))
    stacked = jnp.stack(pieces, axis=1)
    grouped = stacked.reshape(rows_count, tap_count, GROUPS, model_width // GROUPS)
    return grouped.transpose(0, 2, 1, 3).reshape(rows_count, GROUPS, tap_count * (model_width // GROUPS))

def conv_part(source, segment, kernel_block, first_tap, tap_count):
    unfolded = unfold(source, segment, first_tap, tap_count, False)
    channels = source.shape[1] // GROUPS
    weights = kernel_block.reshape(GROUPS, channels, tap_count * channels)
    return jnp.einsum('tgi,goi->tgo', unfolded, weights, precision=lax.Precision.HIGHEST)

def block_forward(source, segment, params):
    conv_kernel, conv_bias, gain_one, shift_one, query_weight, query_bias, key_weight, value_weight, value_bias, out_weight, out_bias, gain_two, shift_two, up_weight, up_bias, down_weight, down_bias = params
    rows_count, model_width = source.shape
    channels = model_width // GROUPS
    tap_count = KW // 8
    conv_pre = jnp.zeros((rows_count, GROUPS, channels), jnp.float32)
    for block_index in range(8):
        first_tap = block_index * tap_count
        kernel_block = conv_kernel[:, first_tap * channels:(first_tap + tap_count) * channels]
        part_fn = jax.checkpoint(partial(conv_part, first_tap=first_tap, tap_count=tap_count))
        conv_pre = conv_pre + part_fn(source, segment, kernel_block)
    conv_act = low_back(conv_pre.reshape(rows_count, model_width)) + conv_bias
    hidden_zero = source + gelu_exact(conv_act)
    normed_one = low(layer_norm(hidden_zero, gain_one, shift_one))
    query = low(low_back(matmul_high(normed_one, query_weight)) + query_bias)
    key = low(low_back(matmul_high(normed_one, key_weight)))
    value = low(low_back(matmul_high(normed_one, value_weight)) + value_bias)
    head_count = model_width // HEAD_DIM
    query_h = query.reshape(rows_count, head_count, HEAD_DIM)
    key_h = key.reshape(rows_count, head_count, HEAD_DIM)
    value_h = value.reshape(rows_count, head_count, HEAD_DIM)
    raw_scores = low_back(jnp.einsum('qhd,khd->hqk', query_h, key_h, precision=lax.Precision.HIGHEST) * score_scale)
    related = segment[:, None] == segment[None, :]
    scores = jnp.where(related[None], raw_scores, -1000000000.0)
    row_top = lax.optimization_barrier(jnp.max(scores, axis=-1, keepdims=True))
    expd = jnp.exp(scores - row_top)
    probs = expd / lax.optimization_barrier(jnp.sum(expd, axis=-1, keepdims=True))
    probs_low = low(probs)
    mixed = jnp.einsum('hqk,khd->qhd', probs_low, value_h, precision=lax.Precision.HIGHEST)
    mixed = low(low_back(mixed.reshape(rows_count, model_width)))
    hidden_one = hidden_zero + low_back(matmul_high(mixed, out_weight)) + out_bias
    normed_two = low(layer_norm(hidden_one, gain_two, shift_two))
    up_pre = low_back(matmul_high(normed_two, up_weight)) + up_bias
    activated = low(gelu_exact(up_pre))
    return hidden_one + low_back(matmul_high(activated, down_weight)) + down_bias

def reference(frames, lengths, cotangent, conv_kernel, conv_bias, norm_one_gain, norm_one_bias, query_weight, query_bias, key_weight, value_weight, value_bias, out_weight, out_bias, norm_two_gain, norm_two_bias, up_weight, up_bias, down_weight, down_bias):
    params = tuple((p.astype(jnp.float32) for p in (conv_kernel, conv_bias, norm_one_gain, norm_one_bias, query_weight, query_bias, key_weight, value_weight, value_bias, out_weight, out_bias, norm_two_gain, norm_two_bias, up_weight, up_bias, down_weight, down_bias)))
    device_count = N_DP * N_FSDP
    ends = jnp.cumsum(lengths, axis=1)
    positions = jnp.arange(TOK_DEV, dtype=jnp.int32)
    segment = lax.optimization_barrier(jnp.sum((positions[None, :, None] >= ends[:, None, :]).astype(jnp.int32), axis=2)).astype(jnp.int32)
    valid = (segment < UTT).astype(jnp.float32)
    group_count = device_count // 8
    blocks_in = frames.astype(jnp.float32).reshape(group_count, 8, TOK_DEV, D)
    blocks_grad = (cotangent.astype(jnp.float32).reshape(device_count, TOK_DEV, D) * valid[:, :, None]).reshape(group_count, 8, TOK_DEV, D)
    blocks_seg = segment.reshape(group_count, 8, TOK_DEV)

    def group_step(totals, item):
        source, grad_in, seg_block = item

        def whole(src, prm):
            return jax.vmap(block_forward, in_axes=(0, 0, None))(src, seg_block, prm)
        hidden, pull = jax.vjp(whole, source, params)
        src_grad, prm_grad = pull(grad_in)
        totals = jax.tree.map(jnp.add, totals, prm_grad)
        return (totals, (hidden.astype(jnp.bfloat16), src_grad))
    zeros = jax.tree.map(jnp.zeros_like, params)
    totals, (hidden, src_grad) = lax.scan(group_step, zeros, (blocks_in, blocks_grad, blocks_seg))
    return (hidden.reshape(TOKENS, D), src_grad.reshape(TOKENS, D), totals[0], totals[1], totals[2], totals[3], totals[4], totals[5], totals[6], totals[7], totals[8], totals[9], totals[10], totals[11], totals[12], totals[13], totals[14], totals[15], totals[16])
```

```python
import functools

import jax
import jax.numpy as jnp
import numpy as np
from jax import lax
from jax.experimental import pallas as pl
from jax.experimental.pallas import tpu as pltpu
from jax.sharding import Mesh
from jax.sharding import PartitionSpec as P

HEAD_DIM = 64
GROUPS = 16
KW = 128


norm_eps = 1e-05
score_scale = 0.125


def layer_norm(rows, scale_vec, shift_vec):
    row_mean = jnp.mean(rows, axis=-1, keepdims=True)
    centred = rows - row_mean
    spread = jnp.mean(centred * centred, axis=-1, keepdims=True)
    return centred * lax.rsqrt(spread + norm_eps) * scale_vec + shift_vec


def gelu_exact(values):
    return jax.nn.gelu(values, approximate=False)


def unfold(source, segment, first_tap, tap_count, flipped):
    rows_count, model_width = source.shape
    half_width = KW // 2
    channels = model_width // GROUPS
    padded = jnp.pad(source, ((half_width, half_width), (0, 0))).reshape(
        rows_count + KW, GROUPS, channels
    )
    seg_padded = jnp.pad(segment, (half_width, half_width), constant_values=-1)
    offsets = [
        KW - tap_index if flipped else tap_index
        for tap_index in range(first_tap, first_tap + tap_count)
    ]
    shifted = jnp.stack([padded[offset : offset + rows_count] for offset in offsets], axis=2)
    same_seg = jnp.stack(
        [seg_padded[offset : offset + rows_count] == segment for offset in offsets], axis=1
    )
    kept_taps = jnp.where(same_seg[:, None, :, None], shifted, jnp.zeros((), source.dtype))
    return kept_taps.reshape(rows_count, GROUPS, tap_count * channels)


def conv_forward(source, segment, conv_kernel):
    rows_count, model_width = source.shape
    channels = model_width // GROUPS
    tap_count = KW // 8
    summed = jnp.zeros((rows_count, GROUPS, channels), jnp.float32)
    for block_index in range(8):
        first_tap = block_index * tap_count
        unfolded = unfold(source, segment, first_tap, tap_count, False)
        kernel_block = conv_kernel[:, first_tap * channels : (first_tap + tap_count) * channels]
        kernel_block = kernel_block.reshape(GROUPS, channels, tap_count * channels)
        summed = summed + jnp.einsum(
            "tgi,goi->tgo", unfolded, kernel_block, preferred_element_type=jnp.float32
        )
    return summed.reshape(rows_count, model_width)


def conv_backward(source, segment, conv_kernel, grad_low):
    rows_count, model_width = source.shape
    channels = model_width // GROUPS
    tap_count = KW // 8
    grad_groups = grad_low.reshape(rows_count, GROUPS, channels)
    kernel_pieces = []
    input_grad = jnp.zeros((rows_count, GROUPS, channels), jnp.float32)
    for block_index in range(8):
        first_tap = block_index * tap_count
        unfolded = unfold(source, segment, first_tap, tap_count, False)
        kernel_term = jnp.einsum(
            "tgo,tgi->goi", grad_groups, unfolded, preferred_element_type=jnp.float32
        )
        kernel_pieces.append(kernel_term.reshape(model_width, tap_count * channels))
        turned = unfold(grad_low, segment, first_tap, tap_count, True).reshape(
            rows_count, GROUPS, tap_count, channels
        )
        kernel_block = conv_kernel[:, first_tap * channels : (first_tap + tap_count) * channels]
        kernel_block = kernel_block.reshape(GROUPS, channels, tap_count, channels)
        input_grad = input_grad + jnp.einsum(
            "tgko,gokc->tgc", turned, kernel_block, preferred_element_type=jnp.float32
        )
    return (kernel_pieces, input_grad.reshape(rows_count, model_width))


def sum_kernel_half(piece):
    return lax.psum_scatter(piece, ("dp", "fsdp"), scatter_dimension=0, tiled=True)


def attention_scores(query_h, key_h, related):
    scores = (
        jnp.einsum("qhd,khd->hqk", query_h, key_h, preferred_element_type=jnp.float32) * score_scale
    )
    return jnp.where(related[None], scores, -1000000000.0)


def local_plain(
    frames,
    lengths,
    cotangent,
    conv_kernel,
    conv_bias,
    norm_one_gain,
    norm_one_bias,
    query_weight,
    query_bias,
    key_weight,
    value_weight,
    value_bias,
    out_weight,
    out_bias,
    norm_two_gain,
    norm_two_bias,
    up_weight,
    up_bias,
    down_weight,
    down_bias,
):
    rows_count, model_width = frames.shape
    head_count = model_width // HEAD_DIM
    ends = jnp.cumsum(lengths[0])
    positions = lax.broadcasted_iota(jnp.int32, (rows_count, ends.shape[0]), 0)
    segment = jnp.sum((positions >= ends[None, :]).astype(jnp.int32), axis=1)
    valid = (segment < ends.shape[0]).astype(jnp.float32)
    related = segment[:, None] == segment[None, :]
    conv_set = (conv_kernel, conv_bias, norm_one_gain, norm_one_bias)
    attn_set = (
        query_weight,
        key_weight,
        value_weight,
        out_weight,
        query_bias,
        value_bias,
        out_bias,
    )
    ffn_set = (up_weight, down_weight, up_bias, down_bias, norm_two_gain, norm_two_bias)
    source_f = frames.astype(jnp.float32)
    conv_full = (
        lax.all_gather(conv_set[0], ("dp", "fsdp"), axis=0, tiled=True),
        lax.all_gather(conv_set[1], ("dp", "fsdp"), axis=0, tiled=True),
        lax.all_gather(conv_set[2], ("dp", "fsdp"), axis=0, tiled=True),
        lax.all_gather(conv_set[3], ("dp", "fsdp"), axis=0, tiled=True),
    )
    kernel_full, conv_bias_full, gain_one, shift_one = conv_full
    conv_act = conv_forward(frames, segment, kernel_full) + conv_bias_full.astype(jnp.float32)
    conv_gelu, conv_pull = jax.vjp(gelu_exact, conv_act)
    hidden_zero = source_f + conv_gelu
    normed_one, norm_one_pull = jax.vjp(
        layer_norm, hidden_zero, gain_one.astype(jnp.float32), shift_one.astype(jnp.float32)
    )
    normed_one_low = normed_one.astype(jnp.bfloat16)
    attn_full = (
        lax.all_gather(attn_set[0], ("dp", "fsdp"), axis=0, tiled=True),
        lax.all_gather(attn_set[1], ("dp", "fsdp"), axis=0, tiled=True),
        lax.all_gather(attn_set[2], ("dp", "fsdp"), axis=0, tiled=True),
        lax.all_gather(attn_set[3], ("dp", "fsdp"), axis=0, tiled=True),
        lax.all_gather(attn_set[4], ("dp", "fsdp"), axis=0, tiled=True),
        lax.all_gather(attn_set[5], ("dp", "fsdp"), axis=0, tiled=True),
        lax.all_gather(attn_set[6], ("dp", "fsdp"), axis=0, tiled=True),
    )
    query_full, key_full, value_full, out_full, query_bias_full, value_bias_full, out_bias_full = (
        attn_full
    )
    query_low = (
        jnp.dot(normed_one_low, query_full, preferred_element_type=jnp.float32)
        + query_bias_full.astype(jnp.float32)
    ).astype(jnp.bfloat16)
    key_low = jnp.dot(normed_one_low, key_full, preferred_element_type=jnp.float32).astype(
        jnp.bfloat16
    )
    value_low = (
        jnp.dot(normed_one_low, value_full, preferred_element_type=jnp.float32)
        + value_bias_full.astype(jnp.float32)
    ).astype(jnp.bfloat16)
    query_h = query_low.reshape(rows_count, head_count, HEAD_DIM)
    key_h = key_low.reshape(rows_count, head_count, HEAD_DIM)
    value_h = value_low.reshape(rows_count, head_count, HEAD_DIM)
    scores = attention_scores(query_h, key_h, related)
    row_top = jnp.max(scores, axis=-1, keepdims=True)
    expd = jnp.exp(scores - row_top)
    row_total = jnp.sum(expd, axis=-1, keepdims=True)
    probs = expd / row_total
    logsum = row_top + jnp.log(row_total)
    mixed = jnp.einsum(
        "hqk,khd->qhd", probs.astype(jnp.bfloat16), value_h, preferred_element_type=jnp.float32
    )
    mixed_low = mixed.reshape(rows_count, model_width).astype(jnp.bfloat16)
    hidden_one = (
        hidden_zero
        + jnp.dot(mixed_low, out_full, preferred_element_type=jnp.float32)
        + out_bias_full.astype(jnp.float32)
    )
    ffn_full = (
        lax.all_gather(ffn_set[0], ("dp", "fsdp"), axis=0, tiled=True),
        lax.all_gather(ffn_set[1], ("dp", "fsdp"), axis=0, tiled=True),
        lax.all_gather(ffn_set[2], ("dp", "fsdp"), axis=0, tiled=True),
        lax.all_gather(ffn_set[3], ("dp", "fsdp"), axis=0, tiled=True),
        lax.all_gather(ffn_set[4], ("dp", "fsdp"), axis=0, tiled=True),
        lax.all_gather(ffn_set[5], ("dp", "fsdp"), axis=0, tiled=True),
    )
    up_full, down_full, up_bias_full, down_bias_full, gain_two, shift_two = ffn_full
    normed_two, norm_two_pull = jax.vjp(
        layer_norm, hidden_one, gain_two.astype(jnp.float32), shift_two.astype(jnp.float32)
    )
    normed_two_low = normed_two.astype(jnp.bfloat16)
    up_pre = jnp.dot(
        normed_two_low, up_full, preferred_element_type=jnp.float32
    ) + up_bias_full.astype(jnp.float32)
    activated, gelu_pull = jax.vjp(gelu_exact, up_pre)
    activated_low = activated.astype(jnp.bfloat16)
    hidden_two = (
        hidden_one
        + jnp.dot(activated_low, down_full, preferred_element_type=jnp.float32)
        + down_bias_full.astype(jnp.float32)
    )
    output = hidden_two.astype(jnp.bfloat16)
    ffn_back = (
        lax.all_gather(ffn_set[0], ("dp", "fsdp"), axis=0, tiled=True),
        lax.all_gather(ffn_set[1], ("dp", "fsdp"), axis=0, tiled=True),
        lax.all_gather(ffn_set[2], ("dp", "fsdp"), axis=0, tiled=True),
        lax.all_gather(ffn_set[3], ("dp", "fsdp"), axis=0, tiled=True),
        lax.all_gather(ffn_set[4], ("dp", "fsdp"), axis=0, tiled=True),
        lax.all_gather(ffn_set[5], ("dp", "fsdp"), axis=0, tiled=True),
    )
    up_back, down_back = (ffn_back[0], ffn_back[1])
    grad_out = cotangent.astype(jnp.float32) * valid[:, None]
    grad_out_low = grad_out.astype(jnp.bfloat16)
    down_weight_term = jnp.einsum(
        "tf,td->fd", activated_low, grad_out_low, preferred_element_type=jnp.float32
    )
    down_bias_term = jnp.sum(grad_out, axis=0)
    down_sums = (
        lax.psum_scatter(down_weight_term, ("dp", "fsdp"), scatter_dimension=0, tiled=True),
        lax.psum_scatter(down_bias_term, ("dp", "fsdp"), scatter_dimension=0, tiled=True),
    )
    act_grad = jnp.einsum("td,fd->tf", grad_out_low, down_back, preferred_element_type=jnp.float32)
    up_grad = gelu_pull(act_grad)[0]
    up_grad_low = up_grad.astype(jnp.bfloat16)
    up_bias_term = jnp.sum(up_grad, axis=0)
    up_weight_term = jnp.einsum(
        "td,tf->df", normed_two_low, up_grad_low, preferred_element_type=jnp.float32
    )
    normed_two_grad = jnp.einsum(
        "tf,df->td", up_grad_low, up_back, preferred_element_type=jnp.float32
    )
    norm_two_input, gain_two_term, shift_two_term = norm_two_pull(normed_two_grad)
    hidden_one_grad = grad_out + norm_two_input
    up_sums = (
        lax.psum_scatter(up_weight_term, ("dp", "fsdp"), scatter_dimension=0, tiled=True),
        lax.psum_scatter(up_bias_term, ("dp", "fsdp"), scatter_dimension=0, tiled=True),
        lax.psum_scatter(gain_two_term, ("dp", "fsdp"), scatter_dimension=0, tiled=True),
        lax.psum_scatter(shift_two_term, ("dp", "fsdp"), scatter_dimension=0, tiled=True),
    )
    attn_back = (
        lax.all_gather(attn_set[0], ("dp", "fsdp"), axis=0, tiled=True),
        lax.all_gather(attn_set[1], ("dp", "fsdp"), axis=0, tiled=True),
        lax.all_gather(attn_set[2], ("dp", "fsdp"), axis=0, tiled=True),
        lax.all_gather(attn_set[3], ("dp", "fsdp"), axis=0, tiled=True),
        lax.all_gather(attn_set[4], ("dp", "fsdp"), axis=0, tiled=True),
        lax.all_gather(attn_set[5], ("dp", "fsdp"), axis=0, tiled=True),
        lax.all_gather(attn_set[6], ("dp", "fsdp"), axis=0, tiled=True),
    )
    query_back, key_back, value_back, out_back = (
        attn_back[0],
        attn_back[1],
        attn_back[2],
        attn_back[3],
    )
    attn_grad_low = hidden_one_grad.astype(jnp.bfloat16)
    out_bias_term = jnp.sum(hidden_one_grad, axis=0)
    out_weight_term = jnp.einsum(
        "tc,td->cd", mixed_low, attn_grad_low, preferred_element_type=jnp.float32
    )
    mixed_grad = jnp.einsum(
        "td,cd->tc", attn_grad_low, out_back, preferred_element_type=jnp.float32
    ).astype(jnp.bfloat16)
    mixed_grad_h = mixed_grad.reshape(rows_count, head_count, HEAD_DIM)
    probs_again = jnp.exp(attention_scores(query_h, key_h, related) - logsum)
    prob_grad = jnp.einsum(
        "qhd,khd->hqk", mixed_grad_h, value_h, preferred_element_type=jnp.float32
    )
    value_grad = jnp.einsum(
        "hqk,qhd->khd",
        probs_again.astype(jnp.bfloat16),
        mixed_grad_h,
        preferred_element_type=jnp.float32,
    )
    score_grad = probs_again * (
        prob_grad - jnp.sum(probs_again * prob_grad, axis=-1, keepdims=True)
    )
    score_low = score_grad.astype(jnp.bfloat16)
    query_grad = (
        jnp.einsum("hqk,khd->qhd", score_low, key_h, preferred_element_type=jnp.float32)
        * score_scale
    ).reshape(rows_count, model_width)
    key_grad = (
        jnp.einsum("hqk,qhd->khd", score_low, query_h, preferred_element_type=jnp.float32)
        * score_scale
    ).reshape(rows_count, model_width)
    value_grad = value_grad.reshape(rows_count, model_width)
    query_bias_term = jnp.sum(query_grad, axis=0)
    value_bias_term = jnp.sum(value_grad, axis=0)
    query_grad_low = query_grad.astype(jnp.bfloat16)
    key_grad_low = key_grad.astype(jnp.bfloat16)
    value_grad_low = value_grad.astype(jnp.bfloat16)
    query_weight_term = jnp.einsum(
        "tc,td->cd", normed_one_low, query_grad_low, preferred_element_type=jnp.float32
    )
    key_weight_term = jnp.einsum(
        "tc,td->cd", normed_one_low, key_grad_low, preferred_element_type=jnp.float32
    )
    value_weight_term = jnp.einsum(
        "tc,td->cd", normed_one_low, value_grad_low, preferred_element_type=jnp.float32
    )
    normed_one_grad = jnp.einsum(
        "td,cd->tc", query_grad_low, query_back, preferred_element_type=jnp.float32
    )
    normed_one_grad = normed_one_grad + jnp.einsum(
        "td,cd->tc", key_grad_low, key_back, preferred_element_type=jnp.float32
    )
    normed_one_grad = normed_one_grad + jnp.einsum(
        "td,cd->tc", value_grad_low, value_back, preferred_element_type=jnp.float32
    )
    norm_one_input, gain_one_term, shift_one_term = norm_one_pull(normed_one_grad)
    hidden_zero_grad = hidden_one_grad + norm_one_input
    conv_grad = conv_pull(hidden_zero_grad)[0]
    conv_bias_term = jnp.sum(conv_grad, axis=0)
    conv_grad_low = conv_grad.astype(jnp.bfloat16)
    attn_sums = (
        lax.psum_scatter(query_weight_term, ("dp", "fsdp"), scatter_dimension=0, tiled=True),
        lax.psum_scatter(key_weight_term, ("dp", "fsdp"), scatter_dimension=0, tiled=True),
        lax.psum_scatter(value_weight_term, ("dp", "fsdp"), scatter_dimension=0, tiled=True),
        lax.psum_scatter(out_weight_term, ("dp", "fsdp"), scatter_dimension=0, tiled=True),
        lax.psum_scatter(query_bias_term, ("dp", "fsdp"), scatter_dimension=0, tiled=True),
        lax.psum_scatter(value_bias_term, ("dp", "fsdp"), scatter_dimension=0, tiled=True),
        lax.psum_scatter(out_bias_term, ("dp", "fsdp"), scatter_dimension=0, tiled=True),
        lax.psum_scatter(conv_bias_term, ("dp", "fsdp"), scatter_dimension=0, tiled=True),
        lax.psum_scatter(gain_one_term, ("dp", "fsdp"), scatter_dimension=0, tiled=True),
        lax.psum_scatter(shift_one_term, ("dp", "fsdp"), scatter_dimension=0, tiled=True),
    )
    conv_back = (
        lax.all_gather(conv_set[0], ("dp", "fsdp"), axis=0, tiled=True),
        lax.all_gather(conv_set[1], ("dp", "fsdp"), axis=0, tiled=True),
        lax.all_gather(conv_set[2], ("dp", "fsdp"), axis=0, tiled=True),
        lax.all_gather(conv_set[3], ("dp", "fsdp"), axis=0, tiled=True),
    )
    kernel_pieces, frames_conv_grad = conv_backward(frames, segment, conv_back[0], conv_grad_low)
    kernel_halves = []
    for half_index in range(2):
        half_term = jnp.concatenate(kernel_pieces[half_index * 4 : (half_index + 1) * 4], axis=1)
        kernel_halves.append(sum_kernel_half(half_term))
    kernel_grad_out = jnp.concatenate(kernel_halves, axis=1)
    frames_grad = hidden_zero_grad + frames_conv_grad
    return (
        output,
        frames_grad,
        kernel_grad_out,
        attn_sums[7],
        attn_sums[8],
        attn_sums[9],
        attn_sums[0],
        attn_sums[4],
        attn_sums[1],
        attn_sums[2],
        attn_sums[5],
        attn_sums[3],
        attn_sums[6],
        up_sums[2],
        up_sums[3],
        up_sums[0],
        up_sums[1],
        down_sums[0],
        down_sums[1],
    )


NT = (((1,), (1,)), ((), ()))
TN = (((0,), (0,)), ((), ()))
BF, F32 = jnp.bfloat16, jnp.float32


def f32(v):
    return v.astype(jnp.float32)


def low(v):
    return v.astype(jnp.bfloat16)


def dot(a, b):
    return jnp.dot(a, b, preferred_element_type=jnp.float32)


def dot_nt(a, b):
    return lax.dot_general(a, b, NT, preferred_element_type=jnp.float32)


def dot_tn(a, b):
    return lax.dot_general(a, b, TN, preferred_element_type=jnp.float32)


SMEM = pl.BlockSpec(memory_space=pltpu.SMEM)
VMEM = pl.BlockSpec(memory_space=pltpu.VMEM)
ANY = pl.BlockSpec(memory_space=pl.ANY)
HBM = pl.BlockSpec(memory_space=pltpu.HBM)


def shape(dims, dtype=BF):
    return jax.ShapeDtypeStruct(dims, dtype)


def in_hbm(v):
    return pltpu.with_memory_space_constraint(v, pltpu.HBM)


def out_hbm(v):
    return pltpu.HBM(v.shape, v.dtype)


def estimate(cost):
    return pl.CostEstimate(flops=int(cost * 1e9), bytes_accessed=1 << 10, transcendentals=0)


def tie(v, *after):
    def body(*refs):
        pass

    return pl.pallas_call(
        body,
        in_specs=[ANY] * (1 + len(after)),
        out_specs=ANY,
        out_shape=shape(v.shape, v.dtype),
        input_output_aliases={0: 0},
        cost_estimate=estimate(0.1),
    )(v, *after)


def run_copies(plan, sems):
    copies = [pltpu.make_async_copy(a, b, sems.at[i]) for i, (a, b) in enumerate(plan)]
    for copy in copies:
        copy.start()
    for copy in copies:
        copy.wait()


def whole_call(kernel, ins, in_specs, outs, out_specs, scratch=(), cost=0.05, after=(), plan=None, vmem=12):
    many = isinstance(outs, (list, tuple))
    out_list, out_specs = (list(outs), list(out_specs)) if many else ([outs], [out_specs])
    staged_in = [i for i, sp in enumerate(in_specs) if sp is None]
    staged_out = [i for i, sp in enumerate(out_specs) if sp is None]
    stages = [pltpu.VMEM(ins[i].shape, ins[i].dtype) for i in staged_in]
    stages += [pltpu.VMEM(out_list[i].shape, out_list[i].dtype) for i in staged_out]
    n_in, n_out, n_stage = len(ins), len(out_list), len(stages)

    def body(*refs):
        given, made = list(refs[:n_in]), list(refs[n_in + len(after) : n_in + len(after) + n_out])
        rest = refs[n_in + len(after) + n_out :]
        stage, own, sems = rest[:n_stage], rest[n_stage:-1], rest[-1]
        first, last = [], []
        for ref, i in zip(stage, staged_in):
            first.append((given[i], ref))
            given[i] = ref
        for ref, i in zip(stage[len(staged_in) :], staged_out):
            last.append((ref, made[i]))
            made[i] = ref
        groups = plan(*given, *made, *own) if plan is not None else []
        copies = [pltpu.make_async_copy(a, b, sems.at[i]) for i, (a, b) in enumerate(first + sum(groups, []))]
        for copy in copies:
            copy.start()
        for copy in copies[: len(first)]:
            copy.wait()
        ends = [len(first) + sum(len(g) for g in groups[:i]) for i in range(len(groups) + 1)]

        def ready(group):
            for copy in copies[ends[group] : ends[group + 1]]:
                copy.wait()

        kernel(*given, *made, *own, *([ready] if groups else []))
        run_copies(last, sems)

    result = pl.pallas_call(
        body,
        in_specs=[HBM if sp is None else sp for sp in in_specs] + [ANY] * len(after),
        out_specs=[HBM if sp is None else sp for sp in out_specs],
        out_shape=[out_hbm(v) if sp is None else pltpu.VMEM(v.shape, v.dtype) if sp is VMEM else v for v, sp in zip(out_list, out_specs)],
        scratch_shapes=stages + list(scratch) + [pltpu.SemaphoreType.DMA((64,))],
        compiler_params=pltpu.CompilerParams(vmem_limit_bytes=vmem << 20),
        cost_estimate=estimate(cost),
    )(*[in_hbm(v) if sp is None or sp is ANY else v for v, sp in zip(ins, in_specs)], *after)
    return result if many else result[0]


def left(dims):
    return lax.broadcasted_iota(jnp.int32, dims, 1) < 64


def turn(v):
    return pltpu.roll(v, 64, 1)


def cross(a, b):
    lo = left(a.shape)
    return jnp.where(lo, a, turn(b)), jnp.where(lo, turn(a), b)


def pack_kernel(f_ref, s_ref, o_ref):
    small = low(s_ref[...])
    for g in range(8):
        tile = slice(128 * g, 128 * g + 128)
        p, q = cross(f32(f_ref[0:64, tile]), f32(f_ref[64:128, tile]))
        o_ref[2 * g, 0:64, :] = low(p)
        o_ref[2 * g + 1, 0:64, :] = low(q)
    for g in range(16):
        o_ref[g, 64:80, :] = small


def first_kernel(lens_ref, *refs):
    vectors, bias_ref = refs[0:9], refs[9]
    q_ref, k_ref, v_ref, o_ref, mine_ref, theirs_ref, out_ref, small_ref = refs[10:18]
    c = lax.axis_index("c")
    for j, ref in enumerate((q_ref, k_ref, v_ref)):
        for t in range(4):
            even, odd = cross(f32(ref[:, 256 * t : 256 * t + 128]), f32(ref[:, 256 * t + 128 : 256 * t + 256]))
            tile = slice(128 * t, 128 * t + 128)
            mine_ref[j, :, tile] = low(jnp.where(c == 0, even, odd))
            theirs_ref[j, :, tile] = low(jnp.where(c == 0, odd, even))
    for h in range(2):
        out_ref[h] = o_ref[:, 512 * h : 512 * h + 512]
    small_ref[...] = jnp.zeros_like(small_ref)
    for i, ref in enumerate(vectors):
        small_ref[i : i + 1, 0:32] = f32(ref[...]).reshape(1, 32)
    bias = f32(bias_ref[...]).reshape(1, 128)
    lane = lax.broadcasted_iota(jnp.int32, (1, 128), 1)
    for k in range(4):
        row = pltpu.roll(bias, 128 - 32 * k, 1) if k else bias
        small_ref[9 + k : 10 + k, :] = jnp.where(lane < 32, row, 0.0)
    small_ref[13:14, 0:4] = lens_ref[...].astype(jnp.float32)


def ffn_prep_kernel(lens_ref, u_ref, cot_ref, up_ref, g_ref, g_send_ref):
    valid = jnp.sum(lens_ref[...], axis=1, keepdims=True)
    for z in range(4):
        for k in range(8):
            at = 128 * (8 * z + k)
            up_ref[k, :, 128 * z : 128 * z + 128] = u_ref[:, at : at + 128]
    slot = lax.broadcasted_iota(jnp.int32, (128, 1024), 0)
    g_ref[...] = jnp.where(slot < valid, cot_ref[...], jnp.zeros_like(cot_ref))
    g_send_ref[...] = g_ref[...]


def vector_kernel(meta_ref, mine_ref, theirs_ref, vec_ref, up_ref, qv_ref):
    c, x = meta_ref[3], meta_ref[2]
    lane = lax.broadcasted_iota(jnp.int32, (16, 128), 1)
    tiles = []
    for t in range(8):
        tile = jnp.zeros((16, 128), jnp.float32)
        for k in range(4):
            part = jnp.where(x == k % 2, f32(mine_ref[2 * t + k // 2]), f32(theirs_ref[2 * t + k // 2]))
            tile = jnp.where(lane // 32 == k, pltpu.roll(part, 32 * k, 1) if k else part, tile)
        tiles.append(tile)
        vec_ref[:, 128 * t : 128 * t + 128] = tile
    for z in range(4):
        own = jnp.where(meta_ref[1] == 0, tiles[2 * z], tiles[2 * z + 1])
        own = jnp.where(c == 0, own, turn(own))
        own = jnp.where(x == 0, own, pltpu.roll(own, 96, 1))
        up = own[9:10, :]
        for k in range(1, 4):
            up = jnp.where(lane[0:1] // 32 == k, pltpu.roll(own[9 + k : 10 + k, :], 32 * k, 1), up)
        up_ref[0:1, 128 * z : 128 * z + 128] = up
    for t in range(4):
        even, odd = cross(tiles[2 * t], tiles[2 * t + 1])
        qv_ref[:, 128 * t : 128 * t + 128] = jnp.where(c == 0, even, odd)[3:5]


NB = 8
GROUP = 2
ROWS = 208


def starts_of(lens_ref, block):
    starts = [jnp.int32(0)]
    for i in range(4):
        starts.append(starts[-1] + lens_ref[block * 4 + i])
    return starts + [jnp.int32(128)]


def spread(block, starts, buf, out):
    v = f32(block)
    turned, lo = turn(v), left((64, 128))
    buf[80:144, :] = jnp.where(lo, v, turned)
    buf[144:208, :] = jnp.where(lo, turned, v)
    row = lax.broadcasted_iota(jnp.int32, (224, 128), 0)
    acc = jnp.zeros((224, 128), jnp.float32)
    for i in range(5):
        gap = 16 * (i + 1)
        keep = (row >= starts[i] + gap) & (row < starts[i + 1] + gap)
        acc = jnp.where(keep, buf[80 - gap : 304 - gap, :], acc)
    out[0:224, :] = acc


def fill_taps(spread_rows, wide, taps, b, shift):
    wide[0:224, :] = jnp.where(left((224, 128)), spread_rows[0:224, :], spread_rows[1:225, :])
    for p in range(8):
        off = 2 * p + shift
        taps[ROWS * b : ROWS * b + ROWS, 128 * p : 128 * p + 128] = low(wide[off : off + ROWS, :])


def fill_regions(starts, reg):
    row = lax.broadcasted_iota(jnp.int32, (336, 128), 0) - 64
    region = jnp.zeros((336, 128), jnp.int32)
    for i in range(1, 5):
        region = region + (row >= starts[i] + 16 * i).astype(jnp.int32)
    reg[...] = jnp.where((row >= 0) & (row < ROWS), region, -1)


def merge(y, b, reg, total, outs, starts):
    lo = left((224, 128))
    mine = jnp.where(lo, reg[64:288, :], reg[48:272, :])
    acc = jnp.zeros((224, 128), jnp.float32)
    for m in range(4):
        first = ROWS * b + 32 * m
        acc = acc + jnp.where(reg[32 * m : 32 * m + 224, :] == mine, y[first : first + 224, 128 * m : 128 * m + 128], 0.0)
    total[...] = acc
    part = total[0:ROWS, :] + turn(total[16 : ROWS + 16, :])
    outs[0:ROWS, :] = jnp.where(left((ROWS, 128)), part, turn(part))
    lo = left((64, 128))
    slot = lax.broadcasted_iota(jnp.int32, (64, 128), 0) + jnp.where(lo, 0, 64)
    packed = jnp.zeros((64, 128), jnp.float32)
    for i in range(5):
        gap = 16 * (i + 1)
        keep = (slot >= starts[i]) & (slot < starts[i + 1])
        packed = jnp.where(keep, jnp.where(lo, outs[gap : gap + 64, :], outs[gap + 64 : gap + 128, :]), packed)
    return low(packed)


def conv_body(lens_ref, src_ref, w, out_ref, scratch, shift):
    bufs, rows, wides, taps, regs, y, totals, outs = scratch
    blocks = [starts_of(lens_ref, pl.program_id(0) * NB + b) for b in range(NB)]
    for g in range(NB // GROUP):
        for b in range(GROUP * g, GROUP * g + GROUP):
            k = b % 2
            spread(src_ref[b, 0:64, :], blocks[b], bufs.at[k], rows.at[k])
            fill_taps(rows.at[k], wides.at[k], taps, b, shift)
        part = slice(ROWS * GROUP * g, ROWS * GROUP * (g + 1))
        y[64 + part.start : 64 + part.stop, :] = dot_nt(taps[part, :], w[...])
        if g > 0:
            merge_group(g - 1, blocks, y, regs, totals, outs, out_ref)
    merge_group(NB // GROUP - 1, blocks, y, regs, totals, outs, out_ref)


def merge_group(g, blocks, y, regs, totals, outs, out_ref):
    for b in range(GROUP * g, GROUP * g + GROUP):
        k = b % 2
        fill_regions(blocks[b], regs.at[k])
        out_ref[b] = merge(y, b, regs.at[k], totals.at[k], outs.at[k], blocks[b])


def conv_fwd_kernel(lens_ref, meta_ref, src_ref, own_ref, other_ref, out_ref, w, *scratch):
    @pl.when(pl.program_id(0) == 0)
    def _():
        x = meta_ref[2]
        for m in range(8):
            cols = slice(1024 * m, 1024 * m + 1024)
            w[pl.ds(pl.multiple_of(64 * m + 32 * x, 32), 32), :] = own_ref[:, cols]
            w[pl.ds(pl.multiple_of(64 * m + 32 * (1 - x), 32), 32), :] = other_ref[:, cols]

    conv_body(lens_ref, src_ref, w, out_ref, scratch, 0)


def conv_back_kernel(lens_ref, meta_ref, src_ref, own_ref, other_ref, out_ref, w, *scratch):
    @pl.when(pl.program_id(0) == 0)
    def _():
        x = meta_ref[2]
        for t in range(64):
            cols = slice(128 * t, 128 * t + 128)
            a, b = f32(own_ref[:, cols]), f32(other_ref[:, cols])
            pair = jnp.concatenate([jnp.where(x == 0, a, b), jnp.where(x == 0, b, a)], axis=0).T
            place = 127 - (2 * t + 1)
            m, j = place // 16, place % 16
            w[64 * m : 64 * m + 64, 64 * j : 64 * j + 64] = low(pair[64:128])
            w[64 * m : 64 * m + 64, 64 * j + 64 : 64 * j + 128] = low(pair[0:64])

    conv_body(lens_ref, src_ref, w, out_ref, scratch, 1)


def conv_grad_kernel(lens_ref, meta_ref, src_ref, g_ref, keep_ref, send_ref, acc, gt, buf, rows, wide, taps, reg, pair, regs):
    step = pl.program_id(0)
    for b in range(NB):
        starts = starts_of(lens_ref, step * NB + b)
        spread(src_ref[b, 0:64, :], starts, buf, rows)
        fill_taps(rows, wide, taps, b, 0)
        fill_regions(starts, reg)
        spread(g_ref[b, 0:64, :], starts, buf, rows.at[64:288])
        lo = left((320, 128))
        pair[16:336, :] = jnp.where(lo, rows[16:336, :], rows[0:320, :])
        regs[16:336, :] = jnp.where(lo, reg[16:336, :], reg[0:320, :])
        mine = reg[64 : 64 + ROWS, :]
        for m in range(4):
            first = 128 - 32 * m
            keep = regs[first : first + ROWS, :] == mine
            gt[ROWS * b : ROWS * b + ROWS, 128 * m : 128 * m + 128] = low(jnp.where(keep, pair[first : first + ROWS, :], 0.0))
    term = dot_tn(gt[...], taps[...])

    @pl.when(step == 0)
    def _():
        acc[...] = term

    @pl.when(step > 0)
    def _():
        acc[...] += term

    @pl.when(step == pl.num_programs(0) - 1)
    def _():
        x = meta_ref[2]
        for m in range(8):
            cols = slice(1024 * m, 1024 * m + 1024)
            keep_ref[:, cols] = acc[pl.ds(pl.multiple_of(64 * m + 32 * x, 32), 32), :]
            send_ref[:, cols] = low(acc[pl.ds(pl.multiple_of(64 * m + 32 * (1 - x), 32), 32), :])


def conv_call(kernel, lens, meta, arrays, outs, out_specs, scratch, after=(), cost=30):
    blocks = arrays[0].shape[0]
    in_specs = [
        pl.BlockSpec((NB, *a.shape[1:]), lambda i, l, m: (i, 0, 0)) if a.ndim == 3 else pl.BlockSpec(a.shape, lambda i, l, m: (0, 0))
        for a in arrays
    ]
    count = 2 + len(arrays)

    def body(*refs):
        kernel(*refs[:count], *refs[count + len(after) :])

    return pl.pallas_call(
        body,
        grid_spec=pltpu.PrefetchScalarGridSpec(
            num_scalar_prefetch=2, grid=(blocks // NB,), in_specs=in_specs + [ANY] * len(after), out_specs=out_specs, scratch_shapes=scratch
        ),
        out_shape=outs,
        compiler_params=pltpu.CompilerParams(vmem_limit_bytes=20 << 20),
        cost_estimate=estimate(cost),
    )(lens, meta, *[a if a.ndim == 3 else in_hbm(a) for a in arrays], *after)


def conv_pass(kernel, lens, meta, src, own, other, after=(), cost=30):
    scratch = [
        pltpu.VMEM((512, 1024), BF), pltpu.VMEM((2, 304, 128), F32), pltpu.VMEM((2, 232, 128), F32), pltpu.VMEM((2, 224, 128), F32),
        pltpu.VMEM((ROWS * NB, 1024), BF), pltpu.VMEM((2, 336, 128), jnp.int32), pltpu.VMEM((128 + ROWS * NB, 512), F32),
        pltpu.VMEM((2, 224, 128), F32), pltpu.VMEM((2, ROWS, 128), F32),
    ]
    spec = pl.BlockSpec((NB, 64, 128), lambda i, l, m: (i, 0, 0))
    return conv_call(kernel, lens, meta, (src, own, other), shape((src.shape[0], 64, 128)), spec, scratch, after, cost)


def conv_grads(lens, meta, src, grad, after=(), cost=30):
    scratch = [
        pltpu.VMEM((512, 1024), F32), pltpu.VMEM((ROWS * NB, 512), BF), pltpu.VMEM((304, 128), F32), pltpu.VMEM((336, 128), F32),
        pltpu.VMEM((224, 128), F32), pltpu.VMEM((ROWS * NB, 1024), BF), pltpu.VMEM((336, 128), jnp.int32), pltpu.VMEM((336, 128), F32),
        pltpu.VMEM((336, 128), jnp.int32),
    ]
    spec = pl.BlockSpec((32, 8192), lambda i, l, m: (0, 0))
    return conv_call(conv_grad_kernel, lens, meta, (src, grad), [out_hbm(shape((32, 8192), F32)), out_hbm(shape((32, 8192)))], [spec, spec], scratch, after, cost)


INV_SQRT2 = 0.7071067811865476
INV_SQRT_2PI = 0.3989422804014327


def gelu_cdf(v):
    return 0.5 + 0.5 * lax.erf(v * INV_SQRT2)


def gelu_slope(v, cdf):
    return cdf + v * (jnp.exp(-0.5 * v * v) * INV_SQRT_2PI)


def normed(v):
    centred = v - jnp.mean(v, axis=-1, keepdims=True)
    scale = lax.rsqrt(jnp.mean(centred * centred, axis=-1, keepdims=True) + norm_eps)
    return centred * scale, scale


def norm_pull(unit, scale, gain, grad):
    grad_unit = grad * gain
    mean_grad = jnp.mean(grad_unit, axis=-1, keepdims=True)
    mean_both = jnp.mean(grad_unit * unit, axis=-1, keepdims=True)
    return scale * (grad_unit - mean_grad - unit * mean_both)


def column_sum(v):
    return jnp.sum(v, axis=0, keepdims=True)


def norm_one_kernel(c_ref, f_ref, vec_ref, act_ref, zero_ref, zero_out_ref, n_ref):
    for g in range(8):
        tile = slice(128 * g, 128 * g + 128)
        a, b = cross(f32(c_ref[2 * g]), f32(c_ref[2 * g + 1]))
        act_ref[0:64, tile] = a + vec_ref[0:1, tile]
        act_ref[64:128, tile] = b + vec_ref[0:1, tile]
    for i in range(4):
        rows = slice(32 * i, 32 * i + 32)
        act = act_ref[rows, :]
        zero = f32(f_ref[rows, :]) + act * gelu_cdf(act)
        zero_ref[rows, :] = zero
        zero_out_ref[rows, :] = zero
        n_ref[rows, :] = low(normed(zero)[0] * vec_ref[1:2, :] + vec_ref[2:3, :])


def norm_two_kernel(zero_ref, keep_ref, got_ref, vec_ref, one_ref, n_ref):
    for i in range(4):
        rows = slice(32 * i, 32 * i + 32)
        one = zero_ref[rows, :] + vec_ref[5:6, :] + keep_ref[rows, :] + f32(got_ref[rows, :])
        one_ref[rows, :] = one
        n_ref[rows, :] = low(normed(one)[0] * vec_ref[6:7, :] + vec_ref[7:8, :])


def norm_two_back_kernel(keep_ref, got_ref, got_y_ref, got_d_ref, one_ref, g_ref, vec_ref, grad_ref, low_ref, sum_ref):
    sums = [jnp.zeros((1, 1024), jnp.float32) for _ in range(4)]
    for i in range(4):
        rows = slice(32 * i, 32 * i + 32)
        grad = keep_ref[rows, :] + f32(got_ref[rows, :]) + f32(got_y_ref[rows, :]) + f32(got_d_ref[rows, :])
        unit, scale = normed(one_ref[rows, :])
        out = f32(g_ref[rows, :])
        total = out + norm_pull(unit, scale, vec_ref[6:7, :], grad)
        grad_ref[rows, :] = total
        low_ref[rows, :] = low(total)
        for k, v in enumerate((total, grad * unit, grad, out)):
            sums[k] = sums[k] + column_sum(v)
    for k in range(4):
        sum_ref[k : k + 1, :] = sums[k]


def norm_one_back_kernel(meta_ref, keep_ref, got_ref, zero_ref, act_ref, one_grad_ref, vec_ref, two_ref, qv_ref, up_ref, grad_ref, pack_ref, conv):
    c, x = meta_ref[3], meta_ref[2]
    sums = [jnp.zeros((1, 1024), jnp.float32) for _ in range(3)]
    for i in range(4):
        rows = slice(32 * i, 32 * i + 32)
        grad = keep_ref[rows, :] + f32(got_ref[rows, :])
        unit, scale = normed(zero_ref[rows, :])
        total = one_grad_ref[rows, :] + norm_pull(unit, scale, vec_ref[1:2, :], grad)
        grad_ref[rows, :] = total
        act = act_ref[rows, :]
        conv_grad = total * gelu_slope(act, gelu_cdf(act))
        conv[rows, :] = conv_grad
        for k, v in enumerate((conv_grad, grad * unit, grad)):
            sums[k] = sums[k] + column_sum(v)
    lane = lax.broadcasted_iota(jnp.int32, (1, 128), 1)
    for g in range(8):
        tile = slice(128 * g, 128 * g + 128)
        p, q = cross(conv[0:64, tile], conv[64:128, tile])
        pack_ref[2 * g, 0:64, :] = low(p)
        pack_ref[2 * g + 1, 0:64, :] = low(q)
        source = qv_ref[0:2, 128 * (g // 2) : 128 * (g // 2) + 128]
        even = jnp.where(lane < 64, source, 0.0) if g % 2 == 0 else jnp.where(lane < 64, turn(source), 0.0)
        heads = jnp.where(c == 0, even, turn(even))
        up_rows = []
        for k in range(4):
            piece = up_ref[0:1, 128 * (g // 2) : 128 * (g // 2) + 128]
            piece = pltpu.roll(piece, (128 - 32 * k) % 128, 1) if k else piece
            piece = jnp.where(lane < 32, piece, 0.0)
            piece = jnp.where(x == 0, piece, pltpu.roll(piece, 32, 1))
            piece = jnp.where(c == 0, piece, turn(piece))
            up_rows.append(jnp.where(meta_ref[1] == g % 2, piece, 0.0))
        all_rows = [sums[0][:, tile], sums[1][:, tile], sums[2][:, tile], heads[0:1], heads[1:2], two_ref[0:1, tile],
                    two_ref[1:2, tile], two_ref[2:3, tile], two_ref[3:4, tile], *up_rows, jnp.zeros((3, 128), jnp.float32)]
        block = jnp.concatenate(all_rows, axis=0)
        pack_ref[2 * g, 64:80, :] = low(block)
        pack_ref[2 * g + 1, 64:80, :] = low(turn(block))


def final_kernel(c_ref, grad_ref, o_ref):
    for g in range(8):
        tile = slice(128 * g, 128 * g + 128)
        a, b = cross(f32(c_ref[2 * g]), f32(c_ref[2 * g + 1]))
        o_ref[0:64, tile] = grad_ref[0:64, tile] + a
        o_ref[64:128, tile] = grad_ref[64:128, tile] + b


def related(lens_ref, block):
    row = lax.broadcasted_iota(jnp.int32, (128, 128), 0)
    col = lax.broadcasted_iota(jnp.int32, (128, 128), 1)
    first = jnp.zeros((128, 128), jnp.int32)
    last = jnp.full((128, 128), 128, jnp.int32)
    e = 0
    for i in range(4):
        e = e + lens_ref[block * 4 + i]
        first = jnp.maximum(first, jnp.where(row >= e, e, 0))
        last = jnp.minimum(last, jnp.where(row < e, e, 128))
    return (col >= first) & (col < last)


def head_probs(query, key, rel, mine):
    masked_query = jnp.where(mine, query, jnp.zeros_like(query))
    scores = dot_nt(masked_query, key) * score_scale
    scores = jnp.where(rel, scores, -1000000000.0)
    top = jnp.max(scores, axis=-1, keepdims=True)
    expd = jnp.exp(scores - top)
    return expd / jnp.sum(expd, axis=-1, keepdims=True)


def attn_places(meta_ref, pieces, wqkv, wo):
    own, along_x, along_y, diag_a, diag_b = pieces
    y, x, c = meta_ref[1], meta_ref[2], meta_ref[3]
    groups = [[], [], [], []]
    for dy, dx, src in ((0, 0, own), (0, 1, along_x), (1, 0, along_y), (1, 1, None)):
        yy, xx = y ^ dy, x ^ dx
        for i in range(8):
            if src is not None:
                part = src.at[:, i]
            else:
                part = diag_a.at[:, i] if i < 4 else diag_b.at[:, i - 4]
            place = wqkv.at[i % 3, :, yy, c ^ (i // 3), xx] if i < 6 else wo.at[i - 6, :, yy, xx]
            groups[i % 3 if i < 6 else 3].append((part, place))
    return groups


def attn_scratch():
    return [pltpu.VMEM((3, 4, 2, 2, 2, 32, 512), BF), pltpu.VMEM((2, 4, 2, 2, 32, 512), BF)]


def attn_fwd_kernel(
    meta_ref, lens_ref, n_ref, n_other_ref, own, along_x, along_y, diag_a, diag_b, bias_ref,
    q_ref, k_ref, v_ref, m_ref, keep_ref, send_ref, wqkv, wo, ready,
):
    n = jnp.concatenate([n_ref[...], n_other_ref[...]], axis=0)
    ready(0)
    q_ref[...] = low(dot(n, wqkv[0].reshape(1024, 512)) + bias_ref[0:1, :])
    ready(1)
    k_ref[...] = low(dot(n, wqkv[1].reshape(1024, 512)))
    ready(2)
    v_ref[...] = low(dot(n, wqkv[2].reshape(1024, 512)) + bias_ref[1:2, :])
    half = lax.broadcasted_iota(jnp.int32, (128, 128), 1) // 64
    for b in range(2):
        rel = related(lens_ref, meta_ref[0] ^ b)
        for p in range(4):
            at = (slice(128 * b, 128 * b + 128), slice(128 * p, 128 * p + 128))
            query, key, value = q_ref[at], k_ref[at], v_ref[at]
            outs = [dot(low(head_probs(query, key, rel, half == h)), value) for h in range(2)]
            m_ref[at] = low(jnp.where(half == 0, outs[0], outs[1]))
    mixed = m_ref[...]
    ready(3)
    for h in range(2):
        out = dot(mixed, wo[h].reshape(512, 512))
        keep_ref[:, 512 * h : 512 * h + 512] = out[0:128]
        send_ref[:, 512 * h : 512 * h + 512] = low(out[128:256])


def attn_bwd_kernel(
    meta_ref, lens_ref, g_ref, g_other_ref, q_ref, k_ref, v_ref, own, along_x, along_y, diag_a, diag_b,
    dq_ref, dk_ref, dv_ref, sum_ref, keep_ref, send_ref, wqkv, wo, ready,
):
    grad_in = jnp.concatenate([g_ref[...], g_other_ref[...]], axis=0)
    ready(3)
    mixed_grad = low(dot_nt(grad_in[:, 0:512], wo[0].reshape(512, 512)) + dot_nt(grad_in[:, 512:1024], wo[1].reshape(512, 512)))
    half = lax.broadcasted_iota(jnp.int32, (128, 128), 1) // 64
    for p in range(4):
        sums = []
        for b in range(2):
            rel = related(lens_ref, meta_ref[0] ^ b)
            at = (slice(128 * b, 128 * b + 128), slice(128 * p, 128 * p + 128))
            query, key, value = q_ref[at], k_ref[at], v_ref[at]
            grad = mixed_grad[128 * b : 128 * b + 128, 128 * p : 128 * p + 128]
            dqs, dks, dvs = [], [], []
            for h in range(2):
                probs = head_probs(query, key, rel, half == h)
                grad_h = jnp.where(half == h, grad, jnp.zeros_like(grad))
                prob_grad = dot_nt(grad_h, value)
                dvs.append(dot_tn(low(probs), grad))
                score_grad = probs * (prob_grad - jnp.sum(probs * prob_grad, axis=-1, keepdims=True))
                score_low = low(score_grad)
                dqs.append(dot(score_low, key) * score_scale)
                dks.append(dot_tn(score_low, query) * score_scale)
            dq = jnp.where(half == 0, dqs[0], dqs[1])
            dk = jnp.where(half == 0, dks[0], dks[1])
            dv = jnp.where(half == 0, dvs[0], dvs[1])
            dq_ref[at], dk_ref[at], dv_ref[at] = low(dq), low(dk), low(dv)
            sums.append((column_sum(dq), column_sum(dv)))
        sum_ref[0:1, 128 * p : 128 * p + 128] = sums[0][0] + sums[1][0]
        sum_ref[1:2, 128 * p : 128 * p + 128] = sums[0][1] + sums[1][1]
    for j in range(3):
        ready(j)
    out = dot_nt(dq_ref[...], wqkv[0].reshape(1024, 512))
    out += dot_nt(dk_ref[...], wqkv[1].reshape(1024, 512))
    out += dot_nt(dv_ref[...], wqkv[2].reshape(1024, 512))
    keep_ref[...] = out[0:128]
    send_ref[...] = low(out[128:256])


def term_plan(meta_ref, own, send_x, send_y, keep_a, keep_b, gqkv, go):
    y, x, c = meta_ref[1], meta_ref[2], meta_ref[3]
    plan = []
    for dy, dx in ((0, 0), (0, 1), (1, 0), (1, 1)):
        yy, xx = y ^ dy, x ^ dx
        for i in range(8):
            if dy == 0 and dx == 0:
                part = own.at[:, i]
            elif i < 4:
                part = send_x.at[dy, :, i] if dx == 1 else keep_a.at[:, i]
            else:
                part = send_y.at[dx, :, i - 4] if dy == 1 else keep_b.at[:, i - 4]
            plan.append((gqkv.at[i % 3, :, yy, c ^ (i // 3), xx] if i < 6 else go.at[i - 6, :, yy, xx], part))
    return plan


def attn_term_kernel(meta_ref, n_ref, n_other_ref, dq_ref, dk_ref, dv_ref, m_ref, g_ref, g_other_ref, own, send_x, send_y, keep_a, keep_b, gqkv, go, sems):
    for z in range(4):
        cols = slice(256 * z, 256 * z + 256)
        n = jnp.concatenate([n_ref[:, cols], n_other_ref[:, cols]], axis=0)
        for j, ref in enumerate((dq_ref, dk_ref, dv_ref)):
            gqkv[j, z] = low(dot_tn(n, ref[...])).reshape(2, 2, 2, 32, 512)
    grad = jnp.concatenate([g_ref[...], g_other_ref[...]], axis=0)
    for z in range(4):
        term = low(dot_tn(m_ref[:, 128 * z : 128 * z + 128], grad))
        for h in range(2):
            go[h, z] = term[:, 512 * h : 512 * h + 512].reshape(2, 2, 32, 512)
    run_copies(term_plan(meta_ref, own, send_x, send_y, keep_a, keep_b, gqkv, go), sems)


def ffn_plan(both, wu, wd):
    return [[(both.at[:, 0:256], wu)], [(both.at[:, 256:384], wd.at[0]), (both.at[:, 384:512], wd.at[1])]]


def ffn_scratch():
    return [pltpu.VMEM((4, 256, 512), BF), pltpu.VMEM((2, 4, 128, 512), BF)]


def ffn_kernel(*refs):
    n_refs, g_refs, bias_ref = refs[0:8], refs[8:16], refs[17]
    act_ref, ug_ref, keep_ref, send_ref, sum_ref, wu, wd, ready = refs[18:26]
    ready(0)
    total = jnp.zeros((1, 512), jnp.float32)
    for i in (4, 5, 6, 7, 0, 1, 2, 3):
        rows = slice(128 * i, 128 * i + 128)
        up_pre = dot(n_refs[i][...], wu[...].reshape(1024, 512)) + bias_ref[...]
        cdf = gelu_cdf(up_pre)
        act_ref[rows, :] = low(up_pre * cdf)
        if i == 4:
            ready(1)
        act_grad = dot_nt(g_refs[i][:, 0:512], wd[0].reshape(512, 512)) + dot_nt(g_refs[i][:, 512:1024], wd[1].reshape(512, 512))
        up_grad = act_grad * gelu_slope(up_pre, cdf)
        total = total + column_sum(up_grad)
        ug_ref[rows, :] = low(up_grad)
        back = dot_nt(low(up_grad), wu[...].reshape(1024, 512))
        if i >= 4:
            send_ref[128 * i - 512 : 128 * i - 384, :] = low(back)
        else:
            keep_ref[rows, :] = back
    sum_ref[...] = total


def ffn_out_kernel(act_ref, both_ref, keep_ref, send_ref, wd, ready):
    ready(0)
    for h in range(2):
        cols = slice(512 * h, 512 * h + 512)
        keep_ref[:, cols] = dot(act_ref[0:512, :], wd[h].reshape(512, 512))
        send_ref[:, cols] = low(dot(act_ref[512:1024, :], wd[h].reshape(512, 512)))


def half_sum_kernel(keep_ref, got_ref, own_ref, x_ref, y_ref, across_ref):
    own_ref[...] = keep_ref[0:128, :] + f32(got_ref[0:128, :])
    for i, ref in enumerate((x_ref, y_ref, across_ref), 1):
        rows = slice(128 * i, 128 * i + 128)
        ref[...] = low(keep_ref[rows, :] + f32(got_ref[rows, :]))


def ffn_terms(act, grads, normeds, up_grad, after, cost=20):
    def body(*refs):
        act_ref, g_refs, n_refs, u_ref, out_ref = refs[0], refs[1:9], refs[9:17], refs[17], refs[-1]
        n = jnp.concatenate([ref[...] for ref in n_refs], axis=0)
        out_ref[0, 0:256] = low(dot_tn(n, u_ref[...]))
        g = jnp.concatenate([ref[...] for ref in g_refs], axis=0)
        down = low(dot_tn(act_ref[...], g))
        out_ref[0, 256:384] = down[:, 0:512]
        out_ref[0, 384:512] = down[:, 512:1024]

    rows = pl.BlockSpec((128, 1024), lambda i: (0, 0))
    part = pl.BlockSpec((128, 256), lambda i: (0, i))
    return pl.pallas_call(
        body,
        grid=(4,),
        in_specs=[pl.BlockSpec((1024, 128), lambda i: (0, i))] + [rows] * 8 + [part] * 8
        + [pl.BlockSpec((1024, 512), lambda i: (0, 0))] + [ANY] * len(after),
        out_specs=pl.BlockSpec((1, 512, 512), lambda i: (i, 0, 0)),
        out_shape=out_hbm(shape((4, 512, 512))),
        compiler_params=pltpu.CompilerParams(vmem_limit_bytes=20 << 20),
        cost_estimate=estimate(20),
    )(act, grads[0], *[in_hbm(v) for v in grads[1:]], normeds[0], *[in_hbm(v) for v in normeds[1:]], up_grad, *after)


def fold_call(keep_a, keep_b, got_x, got_y, after, cost=3):
    def body(a_ref, b_ref, x_ref, y_ref, *refs):
        refs[-2][...] = low(f32(a_ref[...]) + f32(x_ref[0]))
        refs[-1][...] = low(f32(b_ref[...]) + f32(y_ref[0]))

    part = pl.BlockSpec((2, 4, 32, 512), lambda i: (i, 0, 0, 0))
    second = pl.BlockSpec((1, 2, 4, 32, 512), lambda i: (1, i, 0, 0, 0))
    return pl.pallas_call(
        body,
        grid=(2,),
        in_specs=[part, part, second, second] + [ANY] * len(after),
        out_specs=[part, part],
        out_shape=[out_hbm(shape((4, 4, 32, 512)))] * 2,
        compiler_params=pltpu.CompilerParams(vmem_limit_bytes=16 << 20),
        cost_estimate=estimate(cost),
    )(in_hbm(keep_a), in_hbm(keep_b), in_hbm(got_x), in_hbm(got_y), *after)


def join_call(own, got_x, got_y, last_a, last_b, after, cost=3):
    def body(own_ref, x_ref, y_ref, a_ref, b_ref, *refs):
        refs[-1][:, 0:4] = low(f32(own_ref[:, 0:4]) + f32(x_ref[0]) + f32(a_ref[...]))
        refs[-1][:, 4:8] = low(f32(own_ref[:, 4:8]) + f32(y_ref[0]) + f32(b_ref[...]))

    full = pl.BlockSpec((2, 8, 32, 512), lambda i: (i, 0, 0, 0))
    part = pl.BlockSpec((2, 4, 32, 512), lambda i: (i, 0, 0, 0))
    first = pl.BlockSpec((1, 2, 4, 32, 512), lambda i: (0, i, 0, 0, 0))
    return pl.pallas_call(
        body,
        grid=(2,),
        in_specs=[full, first, first, part, part] + [ANY] * len(after),
        out_specs=full,
        out_shape=out_hbm(shape((4, 8, 32, 512))),
        compiler_params=pltpu.CompilerParams(vmem_limit_bytes=16 << 20),
        cost_estimate=estimate(cost),
    )(in_hbm(own), in_hbm(got_x), in_hbm(got_y), in_hbm(last_a), in_hbm(last_b), *after)


def output_kernel(one_ref, keep_ref, got_ref, got_y_ref, got_d_ref, vec_ref, o_ref):
    got = f32(got_ref[...]) + f32(got_y_ref[...]) + f32(got_d_ref[...])
    o_ref[...] = low(one_ref[...] + keep_ref[...] + got + vec_ref[8:9, :])


def up_grad_kernel(got_ref, sum_ref, up_ref, down_ref):
    for z in range(4):
        for k in range(8):
            at = 128 * (8 * z + k)
            up_ref[:, at : at + 128] = f32(got_ref[k, :, 128 * z : 128 * z + 128])
    down_ref[:, 0:512] = f32(sum_ref[256:384])
    down_ref[:, 512:1024] = f32(sum_ref[384:512])


def qkv_grad_kernel(meta_ref, sum_ref, got_ref, q_ref, k_ref, v_ref, o_ref):
    c = meta_ref[3]
    for j, ref in enumerate((q_ref, k_ref, v_ref)):
        for t in range(4):
            tile = slice(128 * t, 128 * t + 128)
            mine, theirs = f32(sum_ref[j, :, tile]), f32(got_ref[3 + j, :, tile])
            a, b = cross(jnp.where(c == 0, mine, theirs), jnp.where(c == 0, theirs, mine))
            ref[:, 256 * t : 256 * t + 128] = a
            ref[:, 256 * t + 128 : 256 * t + 256] = b
    for h in range(2):
        o_ref[:, 512 * h : 512 * h + 512] = f32(sum_ref[6 + h])


def swap(v, axis):
    return lax.ppermute(v, axis, [(0, 1), (1, 0)])


def swap_across(v):
    return lax.ppermute(v, ("y", "x"), [(i, 3 - i) for i in range(4)])


def gather_z(v):
    return lax.all_gather(v, "z", axis=0, tiled=False)


def scatter_z(v):
    return lax.psum_scatter(v, "z", scatter_dimension=0, tiled=False)


def pick(v, index, axis):
    return lax.dynamic_index_in_dim(v, index, axis, keepdims=False)


def local(
    frames, lengths, cotangent, conv_kernel, conv_bias, norm_one_gain, norm_one_bias,
    query_weight, query_bias, key_weight, value_weight, value_bias, out_weight, out_bias,
    norm_two_gain, norm_two_bias, up_weight, up_bias, down_weight, down_bias,
):
    zi, yi, ci, xi = (lax.axis_index(a) for a in ("z", "y", "c", "x"))
    meta = jnp.stack([(zi * 2 + yi) * 2 + ci, yi, xi, ci]).astype(jnp.int32)
    row, row_f, half = shape((128, 1024)), shape((128, 1024), F32), shape((256, 512))
    groups, plane = ("z", "y", "c"), ("y", "c", "x")

    def spread_plane(own, along_x, along_y, across):
        four = (own, along_x, along_y, across)
        return (*four, *(swap(v, "c") for v in four))

    def half_sum(keep, send, saved, cost, after):
        return whole_call(
            half_sum_kernel, (keep, swap(send, "c")), [saved, VMEM], [row_f, row, row, row], [saved] + [VMEM] * 3, cost=cost, after=after
        )

    vectors = (conv_bias, norm_one_gain, norm_one_bias, query_bias, value_bias, out_bias, norm_two_gain, norm_two_bias, down_bias, up_bias)
    qkv_mine, qkv_theirs, out_part, small = whole_call(
        first_kernel, (lengths, *vectors, query_weight, key_weight, value_weight, out_weight), [None] * 15,
        [shape((3, 32, 512)), shape((3, 32, 512)), shape((2, 32, 512)), shape((16, 128), F32)], [VMEM] * 4, cost=0.05, after=(),
    )
    attn_part = jnp.concatenate([qkv_mine, swap(qkv_theirs, "c"), out_part], axis=0)
    attn_own = gather_z(attn_part)

    up_split, grad_out, grad_send = whole_call(
        ffn_prep_kernel, (lengths, up_weight, cotangent), [None] * 3, [shape((8, 32, 512)), row, row], [VMEM] * 3, cost=0.05, after=(qkv_mine,)
    )
    grad_y = swap(grad_send, "y")
    up_part = lax.all_to_all(up_split, plane, 0, 0, tiled=True)

    payload = whole_call(pack_kernel, (frames, small), [None, VMEM], shape((16, 80, 128)), VMEM, cost=0.05, after=(in_hbm(attn_part), in_hbm(grad_y)))
    got = lax.all_to_all(payload, groups, 0, 0, tiled=True)
    kernel_other = swap(conv_kernel, "x")
    grad_x = swap(tie(grad_send, kernel_other), "x")
    lens = got[:, 77, 0:4].astype(jnp.int32).reshape(64)
    ffn_part = jnp.concatenate([up_part.reshape(256, 512), down_weight[:, :512], down_weight[:, 512:]], axis=0)
    ffn_both = gather_z(ffn_part)
    conv_out = conv_pass(conv_fwd_kernel, lens, meta, got, conv_kernel, kernel_other, cost=30, after=(in_hbm(attn_own), in_hbm(grad_x)))
    conv_got = lax.all_to_all(conv_out, groups, 0, 0, tiled=True)

    grad_d = swap_across(tie(grad_send, kernel_other))
    grads_out = spread_plane(grad_out, grad_x, grad_y, grad_d)
    attn_own = attn_own
    attn_x, attn_y = swap(attn_own, "x"), swap(attn_own, "y")
    diag_a, diag_b = swap(attn_x[:, 0:4], "y"), swap(attn_y[:, 4:8], "x")
    attn_pieces = (attn_own, attn_x, attn_y, diag_a, diag_b)

    got_small = got[:, 64:80]
    got_small_other = swap(got_small, "x")
    vec, up_bias_own, qv_bias = whole_call(
        vector_kernel, (meta, got_small, got_small_other), [SMEM, VMEM, VMEM],
        [shape((16, 1024), F32), shape((1, 512), F32), shape((2, 512), F32)], [VMEM] * 3, cost=3, after=(conv_out,),
    )
    conv_act, hidden_zero, zero_saved, n_one = whole_call(
        norm_one_kernel, (conv_got, frames, vec), [VMEM, None, VMEM], [row_f, row_f, row_f, row], [None, VMEM, None, VMEM],
        cost=1, after=(*(in_hbm(v) for v in grads_out[3:]), in_hbm(attn_x), in_hbm(attn_y)),
    )
    n_one_other = swap(n_one, "c")

    def attn_copies(first):
        return lambda *refs: attn_places(refs[0], refs[first : first + 5], refs[-2], refs[-1])

    query, key, value, mixed, attn_keep, attn_send = whole_call(
        attn_fwd_kernel, (meta, lens, n_one, n_one_other, *attn_pieces, qv_bias), [SMEM, SMEM, VMEM, VMEM] + [ANY] * 5 + [VMEM],
        [half] * 4 + [row_f, row], [None] * 4 + [VMEM] * 2, attn_scratch(), plan=attn_copies(4), vmem=16, cost=8, after=(),
    )
    hidden_one, n_two = whole_call(
        norm_two_kernel, (hidden_zero, attn_keep, swap(attn_send, "c"), vec), [VMEM] * 4, [row_f, row], [VMEM] * 2,
        cost=0.1, after=(in_hbm(ffn_both),),
    )

    n_twos = spread_plane(n_two, swap(n_two, "x"), swap(n_two, "y"), swap_across(n_two))
    many, many_f, many_half = shape((1024, 512)), shape((512, 1024), F32), shape((512, 1024))
    activated, up_grad, back_keep, back_send, up_bias_term = whole_call(
        ffn_kernel, (*n_twos, *grads_out, ffn_both, up_bias_own), ([VMEM] + [None] * 7) * 2 + [ANY, VMEM],
        [many, many, many_f, many_half, shape((1, 512), F32)], [VMEM] * 5, ffn_scratch(),
        plan=lambda *refs: ffn_plan(refs[16], refs[-2], refs[-1]), vmem=20, cost=30,
    )
    two_own, two_x, two_y, two_across = half_sum(back_keep, back_send, VMEM, 0.05, ())
    ffn_keep, ffn_send = whole_call(
        ffn_out_kernel, (activated, ffn_both), [VMEM, ANY], [many_f, many_half], [None, None], ffn_scratch()[1:],
        plan=lambda *refs: ffn_plan(refs[1], None, refs[-1])[1:], cost=1, after=(two_x,),
    )
    two_got = (swap(two_x, "x"), swap(two_y, "y"), swap_across(two_across))
    ffn_term = ffn_terms(activated, grads_out, n_twos, up_grad, (two_x,), 6)
    one_grad, attn_grad, two_sums = whole_call(
        norm_two_back_kernel, (two_own, *two_got, hidden_one, grad_out, vec), [VMEM] * 7, [row_f, row, shape((4, 1024), F32)],
        [None, VMEM, None], cost=5, after=(in_hbm(ffn_term), in_hbm(ffn_send)),
    )
    attn_grad_other = swap(attn_grad, "c")
    ffn_sum = scatter_z(ffn_term)
    dq, dk, dv, qv_sum, one_keep, one_send = whole_call(
        attn_bwd_kernel, (meta, lens, attn_grad, attn_grad_other, query, key, value, *attn_pieces),
        [SMEM, SMEM, VMEM, VMEM] + [None] * 3 + [ANY] * 5, [half] * 3 + [shape((2, 512), F32), row_f, row], [VMEM] * 6, attn_scratch(),
        plan=attn_copies(7), vmem=16, cost=70, after=(),
    )
    zero_grad, payload_back = whole_call(
        norm_one_back_kernel, (meta, one_keep, swap(one_send, "c"), zero_saved, conv_act, one_grad, vec, two_sums, qv_sum, up_bias_term),
        [SMEM, VMEM, VMEM, None, None, None, VMEM, None, VMEM, VMEM], [row_f, shape((16, 80, 128))], [None, VMEM],
        [pltpu.VMEM((128, 1024), F32)], cost=10, after=(),
    )
    grad_got = lax.all_to_all(payload_back, groups, 0, 0, tiled=True)
    out_own, out_x, out_y, out_across = half_sum(ffn_keep, ffn_send, None, 0.05, (payload_back,))

    piece, part = out_hbm(shape((4, 8, 32, 512))), out_hbm(shape((4, 4, 32, 512)))
    pair = out_hbm(shape((2, 4, 4, 32, 512)))
    term_own, term_x, term_y, keep_a, keep_b = whole_call(
        attn_term_kernel, (meta, n_one, n_one_other, dq, dk, dv, mixed, attn_grad, attn_grad_other),
        [SMEM, VMEM, VMEM] + [None] * 4 + [VMEM] * 2, [piece, pair, pair, part, part], [HBM] * 5,
        attn_scratch() + [pltpu.SemaphoreType.DMA((32,))], vmem=16, cost=1, after=(payload_back,),
    )
    got_x, got_y = swap(term_x, "x"), swap(term_y, "y")
    conv_back_out = conv_pass(conv_back_kernel, lens, meta, grad_got, conv_kernel, kernel_other, cost=10, after=(out_x,))
    send_a, send_b = fold_call(keep_a, keep_b, got_x, got_y, (conv_back_out,), 3)
    back_got = lax.all_to_all(conv_back_out, groups, 0, 0, tiled=True)
    out_got = (swap(tie(out_x, send_b), "x"), swap(tie(out_y, send_b), "y"), swap_across(tie(out_across, send_b)))
    kernel_keep, kernel_send = conv_grads(lens, meta, got, grad_got, cost=30, after=(conv_back_out,))
    last_a, last_b = swap(send_a, "y"), swap(send_b, "x")
    attn_half = join_call(term_own, got_x, got_y, last_a, last_b, (kernel_send, back_got, in_hbm(ffn_sum)), 3)
    attn_sum = scatter_z(attn_half)

    frames_grad = whole_call(final_kernel, (back_got, zero_grad), [VMEM, None], row_f, None, cost=0.05, after=(in_hbm(attn_half),))
    output = whole_call(
        output_kernel, (hidden_one, out_own, *out_got, vec), [VMEM, None] + [VMEM] * 4, row, None, cost=0.05, after=(in_hbm(attn_half),)
    )
    kernel_grad = kernel_keep + f32(swap(kernel_send, "x"))
    ffn_sum = tie(ffn_sum, attn_half)
    up_got = lax.all_to_all(ffn_sum[0:256].reshape(8, 32, 512), plane, 0, 0, tiled=True)
    up_weight_grad, down_weight_grad = whole_call(
        up_grad_kernel, (up_got, ffn_sum), [VMEM, None], [shape((32, 4096), F32), shape((128, 1024), F32)], [None] * 2, cost=0.05
    )
    small_sum = jnp.sum(f32(grad_got[:, 64:80, 0:64]), axis=0).reshape(16, 2, 32)
    small_grad = pick(small_sum, xi, 1) + swap(tie(pick(small_sum, 1 - xi, 1), send_a), "x")
    small_grads = [small_grad[i] for i in range(9)]
    attn_sum = tie(attn_sum, output, up_weight_grad, kernel_grad, small_grad, frames_grad)
    query_weight_grad, key_weight_grad, value_weight_grad, out_weight_grad = whole_call(
        qkv_grad_kernel, (meta, attn_sum, swap(attn_sum, "c")), [SMEM, None, None], [shape((32, 1024), F32)] * 4, [None] * 4
    )

    return (
        output, frames_grad, kernel_grad, small_grads[0], small_grads[1], small_grads[2], query_weight_grad, small_grads[3],
        key_weight_grad, value_weight_grad, small_grads[4], out_weight_grad, small_grads[5], small_grads[6], small_grads[7],
        up_weight_grad, small_grad[9:13].reshape(128), down_weight_grad, small_grads[8],
    )


MATRICES_IN = (0, 1, 2, 3, 7, 9, 10, 12, 16, 18)
MATRICES_OUT = (0, 1, 2, 6, 8, 9, 11, 15, 17)


def solution(mesh):
    n_dp, n_fsdp = mesh.shape["dp"], mesh.shape["fsdp"]
    if n_fsdp == 2 and n_dp == GROUPS:
        axes = ("z", "y", "c", "x")
        mesh = Mesh(mesh.devices.reshape(n_dp // 4, 2, 2, n_fsdp), axes)
        body = local
    else:
        axes = ("dp", "fsdp")
        body = local_plain
    in_specs = tuple(P(axes, None) if i in MATRICES_IN else P(axes) for i in range(20))
    out_specs = tuple(P(axes, None) if i in MATRICES_OUT else P(axes) for i in range(19))
    return jax.shard_map(body, mesh=mesh, in_specs=in_specs, out_specs=out_specs, check_vma=False)
```

```python
import functools

import jax
import jax.numpy as jnp
import numpy as np
from jax import lax
from jax.experimental import pallas as pl
from jax.experimental.pallas import tpu as pltpu
from jax.sharding import Mesh
from jax.sharding import PartitionSpec as P

HEAD_DIM = 64
GROUPS = 16
KW = 128


norm_eps = 1e-05
score_scale = 0.125


def layer_norm(rows, scale_vec, shift_vec):
    row_mean = jnp.mean(rows, axis=-1, keepdims=True)
    centred = rows - row_mean
    spread = jnp.mean(centred * centred, axis=-1, keepdims=True)
    return centred * lax.rsqrt(spread + norm_eps) * scale_vec + shift_vec


def gelu_exact(values):
    return jax.nn.gelu(values, approximate=False)


def unfold(source, segment, first_tap, tap_count, flipped):
    rows_count, model_width = source.shape
    half_width = KW // 2
    channels = model_width // GROUPS
    padded = jnp.pad(source, ((half_width, half_width), (0, 0))).reshape(
        rows_count + KW, GROUPS, channels
    )
    seg_padded = jnp.pad(segment, (half_width, half_width), constant_values=-1)
    offsets = [
        KW - tap_index if flipped else tap_index
        for tap_index in range(first_tap, first_tap + tap_count)
    ]
    shifted = jnp.stack([padded[offset : offset + rows_count] for offset in offsets], axis=2)
    same_seg = jnp.stack(
        [seg_padded[offset : offset + rows_count] == segment for offset in offsets], axis=1
    )
    kept_taps = jnp.where(same_seg[:, None, :, None], shifted, jnp.zeros((), source.dtype))
    return kept_taps.reshape(rows_count, GROUPS, tap_count * channels)


def conv_forward(source, segment, conv_kernel):
    rows_count, model_width = source.shape
    channels = model_width // GROUPS
    tap_count = KW // 8
    summed = jnp.zeros((rows_count, GROUPS, channels), jnp.float32)
    for block_index in range(8):
        first_tap = block_index * tap_count
        unfolded = unfold(source, segment, first_tap, tap_count, False)
        kernel_block = conv_kernel[:, first_tap * channels : (first_tap + tap_count) * channels]
        kernel_block = kernel_block.reshape(GROUPS, channels, tap_count * channels)
        summed = summed + jnp.einsum(
            "tgi,goi->tgo", unfolded, kernel_block, preferred_element_type=jnp.float32
        )
    return summed.reshape(rows_count, model_width)


def conv_backward(source, segment, conv_kernel, grad_low):
    rows_count, model_width = source.shape
    channels = model_width // GROUPS
    tap_count = KW // 8
    grad_groups = grad_low.reshape(rows_count, GROUPS, channels)
    kernel_pieces = []
    input_grad = jnp.zeros((rows_count, GROUPS, channels), jnp.float32)
    for block_index in range(8):
        first_tap = block_index * tap_count
        unfolded = unfold(source, segment, first_tap, tap_count, False)
        kernel_term = jnp.einsum(
            "tgo,tgi->goi", grad_groups, unfolded, preferred_element_type=jnp.float32
        )
        kernel_pieces.append(kernel_term.reshape(model_width, tap_count * channels))
        turned = unfold(grad_low, segment, first_tap, tap_count, True).reshape(
            rows_count, GROUPS, tap_count, channels
        )
        kernel_block = conv_kernel[:, first_tap * channels : (first_tap + tap_count) * channels]
        kernel_block = kernel_block.reshape(GROUPS, channels, tap_count, channels)
        input_grad = input_grad + jnp.einsum(
            "tgko,gokc->tgc", turned, kernel_block, preferred_element_type=jnp.float32
        )
    return (kernel_pieces, input_grad.reshape(rows_count, model_width))


def sum_kernel_half(piece):
    return lax.psum_scatter(piece, ("dp", "fsdp"), scatter_dimension=0, tiled=True)


def attention_scores(query_h, key_h, related):
    scores = (
        jnp.einsum("qhd,khd->hqk", query_h, key_h, preferred_element_type=jnp.float32) * score_scale
    )
    return jnp.where(related[None], scores, -1000000000.0)


def local_plain(
    frames,
    lengths,
    cotangent,
    conv_kernel,
    conv_bias,
    norm_one_gain,
    norm_one_bias,
    query_weight,
    query_bias,
    key_weight,
    value_weight,
    value_bias,
    out_weight,
    out_bias,
    norm_two_gain,
    norm_two_bias,
    up_weight,
    up_bias,
    down_weight,
    down_bias,
):
    rows_count, model_width = frames.shape
    head_count = model_width // HEAD_DIM
    ends = jnp.cumsum(lengths[0])
    positions = lax.broadcasted_iota(jnp.int32, (rows_count, ends.shape[0]), 0)
    segment = jnp.sum((positions >= ends[None, :]).astype(jnp.int32), axis=1)
    valid = (segment < ends.shape[0]).astype(jnp.float32)
    related = segment[:, None] == segment[None, :]
    conv_set = (conv_kernel, conv_bias, norm_one_gain, norm_one_bias)
    attn_set = (
        query_weight,
        key_weight,
        value_weight,
        out_weight,
        query_bias,
        value_bias,
        out_bias,
    )
    ffn_set = (up_weight, down_weight, up_bias, down_bias, norm_two_gain, norm_two_bias)
    source_f = frames.astype(jnp.float32)
    conv_full = (
        lax.all_gather(conv_set[0], ("dp", "fsdp"), axis=0, tiled=True),
        lax.all_gather(conv_set[1], ("dp", "fsdp"), axis=0, tiled=True),
        lax.all_gather(conv_set[2], ("dp", "fsdp"), axis=0, tiled=True),
        lax.all_gather(conv_set[3], ("dp", "fsdp"), axis=0, tiled=True),
    )
    kernel_full, conv_bias_full, gain_one, shift_one = conv_full
    conv_act = conv_forward(frames, segment, kernel_full) + conv_bias_full.astype(jnp.float32)
    conv_gelu, conv_pull = jax.vjp(gelu_exact, conv_act)
    hidden_zero = source_f + conv_gelu
    normed_one, norm_one_pull = jax.vjp(
        layer_norm, hidden_zero, gain_one.astype(jnp.float32), shift_one.astype(jnp.float32)
    )
    normed_one_low = normed_one.astype(jnp.bfloat16)
    attn_full = (
        lax.all_gather(attn_set[0], ("dp", "fsdp"), axis=0, tiled=True),
        lax.all_gather(attn_set[1], ("dp", "fsdp"), axis=0, tiled=True),
        lax.all_gather(attn_set[2], ("dp", "fsdp"), axis=0, tiled=True),
        lax.all_gather(attn_set[3], ("dp", "fsdp"), axis=0, tiled=True),
        lax.all_gather(attn_set[4], ("dp", "fsdp"), axis=0, tiled=True),
        lax.all_gather(attn_set[5], ("dp", "fsdp"), axis=0, tiled=True),
        lax.all_gather(attn_set[6], ("dp", "fsdp"), axis=0, tiled=True),
    )
    query_full, key_full, value_full, out_full, query_bias_full, value_bias_full, out_bias_full = (
        attn_full
    )
    query_low = (
        jnp.dot(normed_one_low, query_full, preferred_element_type=jnp.float32)
        + query_bias_full.astype(jnp.float32)
    ).astype(jnp.bfloat16)
    key_low = jnp.dot(normed_one_low, key_full, preferred_element_type=jnp.float32).astype(
        jnp.bfloat16
    )
    value_low = (
        jnp.dot(normed_one_low, value_full, preferred_element_type=jnp.float32)
        + value_bias_full.astype(jnp.float32)
    ).astype(jnp.bfloat16)
    query_h = query_low.reshape(rows_count, head_count, HEAD_DIM)
    key_h = key_low.reshape(rows_count, head_count, HEAD_DIM)
    value_h = value_low.reshape(rows_count, head_count, HEAD_DIM)
    scores = attention_scores(query_h, key_h, related)
    row_top = jnp.max(scores, axis=-1, keepdims=True)
    expd = jnp.exp(scores - row_top)
    row_total = jnp.sum(expd, axis=-1, keepdims=True)
    probs = expd / row_total
    logsum = row_top + jnp.log(row_total)
    mixed = jnp.einsum(
        "hqk,khd->qhd", probs.astype(jnp.bfloat16), value_h, preferred_element_type=jnp.float32
    )
    mixed_low = mixed.reshape(rows_count, model_width).astype(jnp.bfloat16)
    hidden_one = (
        hidden_zero
        + jnp.dot(mixed_low, out_full, preferred_element_type=jnp.float32)
        + out_bias_full.astype(jnp.float32)
    )
    ffn_full = (
        lax.all_gather(ffn_set[0], ("dp", "fsdp"), axis=0, tiled=True),
        lax.all_gather(ffn_set[1], ("dp", "fsdp"), axis=0, tiled=True),
        lax.all_gather(ffn_set[2], ("dp", "fsdp"), axis=0, tiled=True),
        lax.all_gather(ffn_set[3], ("dp", "fsdp"), axis=0, tiled=True),
        lax.all_gather(ffn_set[4], ("dp", "fsdp"), axis=0, tiled=True),
        lax.all_gather(ffn_set[5], ("dp", "fsdp"), axis=0, tiled=True),
    )
    up_full, down_full, up_bias_full, down_bias_full, gain_two, shift_two = ffn_full
    normed_two, norm_two_pull = jax.vjp(
        layer_norm, hidden_one, gain_two.astype(jnp.float32), shift_two.astype(jnp.float32)
    )
    normed_two_low = normed_two.astype(jnp.bfloat16)
    up_pre = jnp.dot(
        normed_two_low, up_full, preferred_element_type=jnp.float32
    ) + up_bias_full.astype(jnp.float32)
    activated, gelu_pull = jax.vjp(gelu_exact, up_pre)
    activated_low = activated.astype(jnp.bfloat16)
    hidden_two = (
        hidden_one
        + jnp.dot(activated_low, down_full, preferred_element_type=jnp.float32)
        + down_bias_full.astype(jnp.float32)
    )
    output = hidden_two.astype(jnp.bfloat16)
    ffn_back = (
        lax.all_gather(ffn_set[0], ("dp", "fsdp"), axis=0, tiled=True),
        lax.all_gather(ffn_set[1], ("dp", "fsdp"), axis=0, tiled=True),
        lax.all_gather(ffn_set[2], ("dp", "fsdp"), axis=0, tiled=True),
        lax.all_gather(ffn_set[3], ("dp", "fsdp"), axis=0, tiled=True),
        lax.all_gather(ffn_set[4], ("dp", "fsdp"), axis=0, tiled=True),
        lax.all_gather(ffn_set[5], ("dp", "fsdp"), axis=0, tiled=True),
    )
    up_back, down_back = (ffn_back[0], ffn_back[1])
    grad_out = cotangent.astype(jnp.float32) * valid[:, None]
    grad_out_low = grad_out.astype(jnp.bfloat16)
    down_weight_term = jnp.einsum(
        "tf,td->fd", activated_low, grad_out_low, preferred_element_type=jnp.float32
    )
    down_bias_term = jnp.sum(grad_out, axis=0)
    down_sums = (
        lax.psum_scatter(down_weight_term, ("dp", "fsdp"), scatter_dimension=0, tiled=True),
        lax.psum_scatter(down_bias_term, ("dp", "fsdp"), scatter_dimension=0, tiled=True),
    )
    act_grad = jnp.einsum("td,fd->tf", grad_out_low, down_back, preferred_element_type=jnp.float32)
    up_grad = gelu_pull(act_grad)[0]
    up_grad_low = up_grad.astype(jnp.bfloat16)
    up_bias_term = jnp.sum(up_grad, axis=0)
    up_weight_term = jnp.einsum(
        "td,tf->df", normed_two_low, up_grad_low, preferred_element_type=jnp.float32
    )
    normed_two_grad = jnp.einsum(
        "tf,df->td", up_grad_low, up_back, preferred_element_type=jnp.float32
    )
    norm_two_input, gain_two_term, shift_two_term = norm_two_pull(normed_two_grad)
    hidden_one_grad = grad_out + norm_two_input
    up_sums = (
        lax.psum_scatter(up_weight_term, ("dp", "fsdp"), scatter_dimension=0, tiled=True),
        lax.psum_scatter(up_bias_term, ("dp", "fsdp"), scatter_dimension=0, tiled=True),
        lax.psum_scatter(gain_two_term, ("dp", "fsdp"), scatter_dimension=0, tiled=True),
        lax.psum_scatter(shift_two_term, ("dp", "fsdp"), scatter_dimension=0, tiled=True),
    )
    attn_back = (
        lax.all_gather(attn_set[0], ("dp", "fsdp"), axis=0, tiled=True),
        lax.all_gather(attn_set[1], ("dp", "fsdp"), axis=0, tiled=True),
        lax.all_gather(attn_set[2], ("dp", "fsdp"), axis=0, tiled=True),
        lax.all_gather(attn_set[3], ("dp", "fsdp"), axis=0, tiled=True),
        lax.all_gather(attn_set[4], ("dp", "fsdp"), axis=0, tiled=True),
        lax.all_gather(attn_set[5], ("dp", "fsdp"), axis=0, tiled=True),
        lax.all_gather(attn_set[6], ("dp", "fsdp"), axis=0, tiled=True),
    )
    query_back, key_back, value_back, out_back = (
        attn_back[0],
        attn_back[1],
        attn_back[2],
        attn_back[3],
    )
    attn_grad_low = hidden_one_grad.astype(jnp.bfloat16)
    out_bias_term = jnp.sum(hidden_one_grad, axis=0)
    out_weight_term = jnp.einsum(
        "tc,td->cd", mixed_low, attn_grad_low, preferred_element_type=jnp.float32
    )
    mixed_grad = jnp.einsum(
        "td,cd->tc", attn_grad_low, out_back, preferred_element_type=jnp.float32
    ).astype(jnp.bfloat16)
    mixed_grad_h = mixed_grad.reshape(rows_count, head_count, HEAD_DIM)
    probs_again = jnp.exp(attention_scores(query_h, key_h, related) - logsum)
    prob_grad = jnp.einsum(
        "qhd,khd->hqk", mixed_grad_h, value_h, preferred_element_type=jnp.float32
    )
    value_grad = jnp.einsum(
        "hqk,qhd->khd",
        probs_again.astype(jnp.bfloat16),
        mixed_grad_h,
        preferred_element_type=jnp.float32,
    )
    score_grad = probs_again * (
        prob_grad - jnp.sum(probs_again * prob_grad, axis=-1, keepdims=True)
    )
    score_low = score_grad.astype(jnp.bfloat16)
    query_grad = (
        jnp.einsum("hqk,khd->qhd", score_low, key_h, preferred_element_type=jnp.float32)
        * score_scale
    ).reshape(rows_count, model_width)
    key_grad = (
        jnp.einsum("hqk,qhd->khd", score_low, query_h, preferred_element_type=jnp.float32)
        * score_scale
    ).reshape(rows_count, model_width)
    value_grad = value_grad.reshape(rows_count, model_width)
    query_bias_term = jnp.sum(query_grad, axis=0)
    value_bias_term = jnp.sum(value_grad, axis=0)
    query_grad_low = query_grad.astype(jnp.bfloat16)
    key_grad_low = key_grad.astype(jnp.bfloat16)
    value_grad_low = value_grad.astype(jnp.bfloat16)
    query_weight_term = jnp.einsum(
        "tc,td->cd", normed_one_low, query_grad_low, preferred_element_type=jnp.float32
    )
    key_weight_term = jnp.einsum(
        "tc,td->cd", normed_one_low, key_grad_low, preferred_element_type=jnp.float32
    )
    value_weight_term = jnp.einsum(
        "tc,td->cd", normed_one_low, value_grad_low, preferred_element_type=jnp.float32
    )
    normed_one_grad = jnp.einsum(
        "td,cd->tc", query_grad_low, query_back, preferred_element_type=jnp.float32
    )
    normed_one_grad = normed_one_grad + jnp.einsum(
        "td,cd->tc", key_grad_low, key_back, preferred_element_type=jnp.float32
    )
    normed_one_grad = normed_one_grad + jnp.einsum(
        "td,cd->tc", value_grad_low, value_back, preferred_element_type=jnp.float32
    )
    norm_one_input, gain_one_term, shift_one_term = norm_one_pull(normed_one_grad)
    hidden_zero_grad = hidden_one_grad + norm_one_input
    conv_grad = conv_pull(hidden_zero_grad)[0]
    conv_bias_term = jnp.sum(conv_grad, axis=0)
    conv_grad_low = conv_grad.astype(jnp.bfloat16)
    attn_sums = (
        lax.psum_scatter(query_weight_term, ("dp", "fsdp"), scatter_dimension=0, tiled=True),
        lax.psum_scatter(key_weight_term, ("dp", "fsdp"), scatter_dimension=0, tiled=True),
        lax.psum_scatter(value_weight_term, ("dp", "fsdp"), scatter_dimension=0, tiled=True),
        lax.psum_scatter(out_weight_term, ("dp", "fsdp"), scatter_dimension=0, tiled=True),
        lax.psum_scatter(query_bias_term, ("dp", "fsdp"), scatter_dimension=0, tiled=True),
        lax.psum_scatter(value_bias_term, ("dp", "fsdp"), scatter_dimension=0, tiled=True),
        lax.psum_scatter(out_bias_term, ("dp", "fsdp"), scatter_dimension=0, tiled=True),
        lax.psum_scatter(conv_bias_term, ("dp", "fsdp"), scatter_dimension=0, tiled=True),
        lax.psum_scatter(gain_one_term, ("dp", "fsdp"), scatter_dimension=0, tiled=True),
        lax.psum_scatter(shift_one_term, ("dp", "fsdp"), scatter_dimension=0, tiled=True),
    )
    conv_back = (
        lax.all_gather(conv_set[0], ("dp", "fsdp"), axis=0, tiled=True),
        lax.all_gather(conv_set[1], ("dp", "fsdp"), axis=0, tiled=True),
        lax.all_gather(conv_set[2], ("dp", "fsdp"), axis=0, tiled=True),
        lax.all_gather(conv_set[3], ("dp", "fsdp"), axis=0, tiled=True),
    )
    kernel_pieces, frames_conv_grad = conv_backward(frames, segment, conv_back[0], conv_grad_low)
    kernel_halves = []
    for half_index in range(2):
        half_term = jnp.concatenate(kernel_pieces[half_index * 4 : (half_index + 1) * 4], axis=1)
        kernel_halves.append(sum_kernel_half(half_term))
    kernel_grad_out = jnp.concatenate(kernel_halves, axis=1)
    frames_grad = hidden_zero_grad + frames_conv_grad
    return (
        output,
        frames_grad,
        kernel_grad_out,
        attn_sums[7],
        attn_sums[8],
        attn_sums[9],
        attn_sums[0],
        attn_sums[4],
        attn_sums[1],
        attn_sums[2],
        attn_sums[5],
        attn_sums[3],
        attn_sums[6],
        up_sums[2],
        up_sums[3],
        up_sums[0],
        up_sums[1],
        down_sums[0],
        down_sums[1],
    )


NT = (((1,), (1,)), ((), ()))
TN = (((0,), (0,)), ((), ()))
BF, F32 = jnp.bfloat16, jnp.float32


def f32(v):
    return v.astype(jnp.float32)


def low(v):
    return v.astype(jnp.bfloat16)


def dot(a, b):
    return jnp.dot(a, b, preferred_element_type=jnp.float32)


def dot_nt(a, b):
    return lax.dot_general(a, b, NT, preferred_element_type=jnp.float32)


def dot_tn(a, b):
    return lax.dot_general(a, b, TN, preferred_element_type=jnp.float32)


SMEM = pl.BlockSpec(memory_space=pltpu.SMEM)
VMEM = pl.BlockSpec(memory_space=pltpu.VMEM)
ANY = pl.BlockSpec(memory_space=pl.ANY)
HBM = pl.BlockSpec(memory_space=pltpu.HBM)


def shape(dims, dtype=BF):
    return jax.ShapeDtypeStruct(dims, dtype)


def in_hbm(v):
    return pltpu.with_memory_space_constraint(v, pltpu.HBM)


def out_hbm(v):
    return pltpu.HBM(v.shape, v.dtype)


def estimate(cost):
    return pl.CostEstimate(flops=int(cost * 1e9), bytes_accessed=1 << 10, transcendentals=0)


def tie(v, *after):
    def body(*refs):
        pass

    return pl.pallas_call(
        body,
        in_specs=[ANY] * (1 + len(after)),
        out_specs=ANY,
        out_shape=shape(v.shape, v.dtype),
        input_output_aliases={0: 0},
        cost_estimate=estimate(0.1),
    )(v, *after)


def run_copies(plan, sems):
    copies = [pltpu.make_async_copy(a, b, sems.at[i]) for i, (a, b) in enumerate(plan)]
    for copy in copies:
        copy.start()
    for copy in copies:
        copy.wait()


def whole_call(kernel, ins, in_specs, outs, out_specs, scratch=(), cost=0.05, after=(), plan=None, vmem=12):
    many = isinstance(outs, (list, tuple))
    out_list, out_specs = (list(outs), list(out_specs)) if many else ([outs], [out_specs])
    staged_in = [i for i, sp in enumerate(in_specs) if sp is None]
    staged_out = [i for i, sp in enumerate(out_specs) if sp is None]
    stages = [pltpu.VMEM(ins[i].shape, ins[i].dtype) for i in staged_in]
    stages += [pltpu.VMEM(out_list[i].shape, out_list[i].dtype) for i in staged_out]
    n_in, n_out, n_stage = len(ins), len(out_list), len(stages)

    def body(*refs):
        given, made = list(refs[:n_in]), list(refs[n_in + len(after) : n_in + len(after) + n_out])
        rest = refs[n_in + len(after) + n_out :]
        stage, own, sems = rest[:n_stage], rest[n_stage:-1], rest[-1]
        first, last = [], []
        for ref, i in zip(stage, staged_in):
            first.append((given[i], ref))
            given[i] = ref
        for ref, i in zip(stage[len(staged_in) :], staged_out):
            last.append((ref, made[i]))
            made[i] = ref
        groups = plan(*given, *made, *own) if plan is not None else []
        copies = [pltpu.make_async_copy(a, b, sems.at[i]) for i, (a, b) in enumerate(first + sum(groups, []))]
        for copy in copies:
            copy.start()
        for copy in copies[: len(first)]:
            copy.wait()
        ends = [len(first) + sum(len(g) for g in groups[:i]) for i in range(len(groups) + 1)]

        def ready(group):
            for copy in copies[ends[group] : ends[group + 1]]:
                copy.wait()

        kernel(*given, *made, *own, *([ready] if groups else []))
        run_copies(last, sems)

    result = pl.pallas_call(
        body,
        in_specs=[HBM if sp is None else sp for sp in in_specs] + [ANY] * len(after),
        out_specs=[HBM if sp is None else sp for sp in out_specs],
        out_shape=[out_hbm(v) if sp is None else pltpu.VMEM(v.shape, v.dtype) if sp is VMEM else v for v, sp in zip(out_list, out_specs)],
        scratch_shapes=stages + list(scratch) + [pltpu.SemaphoreType.DMA((64,))],
        compiler_params=pltpu.CompilerParams(vmem_limit_bytes=vmem << 20),
        cost_estimate=estimate(cost),
    )(*[in_hbm(v) if sp is None or sp is ANY else v for v, sp in zip(ins, in_specs)], *after)
    return result if many else result[0]


def left(dims):
    return lax.broadcasted_iota(jnp.int32, dims, 1) < 64


def turn(v):
    return pltpu.roll(v, 64, 1)


def cross(a, b):
    lo = left(a.shape)
    return jnp.where(lo, a, turn(b)), jnp.where(lo, turn(a), b)


def pack_kernel(f_ref, s_ref, o_ref):
    small = low(s_ref[...])
    for g in range(8):
        tile = slice(128 * g, 128 * g + 128)
        p, q = cross(f32(f_ref[0:64, tile]), f32(f_ref[64:128, tile]))
        o_ref[2 * g, 0:64, :] = low(p)
        o_ref[2 * g + 1, 0:64, :] = low(q)
    for g in range(16):
        o_ref[g, 64:80, :] = small


def first_kernel(lens_ref, *refs):
    vectors, bias_ref = refs[0:9], refs[9]
    q_ref, k_ref, v_ref, o_ref, mine_ref, theirs_ref, out_ref, small_ref = refs[10:18]
    c = lax.axis_index("c")
    for j, ref in enumerate((q_ref, k_ref, v_ref)):
        for t in range(4):
            even, odd = cross(f32(ref[:, 256 * t : 256 * t + 128]), f32(ref[:, 256 * t + 128 : 256 * t + 256]))
            tile = slice(128 * t, 128 * t + 128)
            mine_ref[j, :, tile] = low(jnp.where(c == 0, even, odd))
            theirs_ref[j, :, tile] = low(jnp.where(c == 0, odd, even))
    for h in range(2):
        out_ref[h] = o_ref[:, 512 * h : 512 * h + 512]
    small_ref[...] = jnp.zeros_like(small_ref)
    for i, ref in enumerate(vectors):
        small_ref[i : i + 1, 0:32] = f32(ref[...]).reshape(1, 32)
    bias = f32(bias_ref[...]).reshape(1, 128)
    lane = lax.broadcasted_iota(jnp.int32, (1, 128), 1)
    for k in range(4):
        row = pltpu.roll(bias, 128 - 32 * k, 1) if k else bias
        small_ref[9 + k : 10 + k, :] = jnp.where(lane < 32, row, 0.0)
    small_ref[13:14, 0:4] = lens_ref[...].astype(jnp.float32)


def ffn_prep_kernel(lens_ref, u_ref, cot_ref, up_ref, g_ref, g_send_ref):
    valid = jnp.sum(lens_ref[...], axis=1, keepdims=True)
    for z in range(4):
        for k in range(8):
            at = 128 * (8 * z + k)
            up_ref[k, :, 128 * z : 128 * z + 128] = u_ref[:, at : at + 128]
    slot = lax.broadcasted_iota(jnp.int32, (128, 1024), 0)
    g_ref[...] = jnp.where(slot < valid, cot_ref[...], jnp.zeros_like(cot_ref))
    g_send_ref[...] = g_ref[...]


def vector_kernel(meta_ref, mine_ref, theirs_ref, vec_ref, up_ref, qv_ref):
    c, x = meta_ref[3], meta_ref[2]
    lane = lax.broadcasted_iota(jnp.int32, (16, 128), 1)
    tiles = []
    for t in range(8):
        tile = jnp.zeros((16, 128), jnp.float32)
        for k in range(4):
            part = jnp.where(x == k % 2, f32(mine_ref[2 * t + k // 2]), f32(theirs_ref[2 * t + k // 2]))
            tile = jnp.where(lane // 32 == k, pltpu.roll(part, 32 * k, 1) if k else part, tile)
        tiles.append(tile)
        vec_ref[:, 128 * t : 128 * t + 128] = tile
    for z in range(4):
        own = jnp.where(meta_ref[1] == 0, tiles[2 * z], tiles[2 * z + 1])
        own = jnp.where(c == 0, own, turn(own))
        own = jnp.where(x == 0, own, pltpu.roll(own, 96, 1))
        up = own[9:10, :]
        for k in range(1, 4):
            up = jnp.where(lane[0:1] // 32 == k, pltpu.roll(own[9 + k : 10 + k, :], 32 * k, 1), up)
        up_ref[0:1, 128 * z : 128 * z + 128] = up
    for t in range(4):
        even, odd = cross(tiles[2 * t], tiles[2 * t + 1])
        qv_ref[:, 128 * t : 128 * t + 128] = jnp.where(c == 0, even, odd)[3:5]


NB = 4
GROUP = 2
ROWS = 208


def starts_of(lens_ref, block):
    starts = [jnp.int32(0)]
    for i in range(4):
        starts.append(starts[-1] + lens_ref[block * 4 + i])
    return starts + [jnp.int32(128)]


def spread(block, starts, buf, out):
    v = f32(block)
    turned, lo = turn(v), left((64, 128))
    buf[80:144, :] = jnp.where(lo, v, turned)
    buf[144:208, :] = jnp.where(lo, turned, v)
    row = lax.broadcasted_iota(jnp.int32, (224, 128), 0)
    acc = jnp.zeros((224, 128), jnp.float32)
    for i in range(5):
        gap = 16 * (i + 1)
        keep = (row >= starts[i] + gap) & (row < starts[i + 1] + gap)
        acc = jnp.where(keep, buf[80 - gap : 304 - gap, :], acc)
    out[0:224, :] = acc


def fill_taps(spread_rows, wide, taps, b, shift):
    wide[0:224, :] = jnp.where(left((224, 128)), spread_rows[0:224, :], spread_rows[1:225, :])
    for p in range(8):
        off = 2 * p + shift
        taps[ROWS * b : ROWS * b + ROWS, 128 * p : 128 * p + 128] = low(wide[off : off + ROWS, :])


def fill_regions(starts, reg):
    row = lax.broadcasted_iota(jnp.int32, (336, 128), 0) - 64
    region = jnp.zeros((336, 128), jnp.int32)
    for i in range(1, 5):
        region = region + (row >= starts[i] + 16 * i).astype(jnp.int32)
    reg[...] = jnp.where((row >= 0) & (row < ROWS), region, -1)


def merge(y, b, reg, total, outs, starts):
    lo = left((224, 128))
    mine = jnp.where(lo, reg[64:288, :], reg[48:272, :])
    acc = jnp.zeros((224, 128), jnp.float32)
    for m in range(4):
        first = ROWS * b + 32 * m
        acc = acc + jnp.where(reg[32 * m : 32 * m + 224, :] == mine, y[first : first + 224, 128 * m : 128 * m + 128], 0.0)
    total[...] = acc
    part = total[0:ROWS, :] + turn(total[16 : ROWS + 16, :])
    outs[0:ROWS, :] = jnp.where(left((ROWS, 128)), part, turn(part))
    lo = left((64, 128))
    slot = lax.broadcasted_iota(jnp.int32, (64, 128), 0) + jnp.where(lo, 0, 64)
    packed = jnp.zeros((64, 128), jnp.float32)
    for i in range(5):
        gap = 16 * (i + 1)
        keep = (slot >= starts[i]) & (slot < starts[i + 1])
        packed = jnp.where(keep, jnp.where(lo, outs[gap : gap + 64, :], outs[gap + 64 : gap + 128, :]), packed)
    return low(packed)


def conv_body(lens_ref, src_ref, w, out_ref, scratch, shift):
    bufs, rows, wides, taps, regs, y, totals, outs = scratch
    blocks = [starts_of(lens_ref, pl.program_id(0) * NB + b) for b in range(NB)]
    for g in range(NB // GROUP):
        for b in range(GROUP * g, GROUP * g + GROUP):
            k = b % 2
            spread(src_ref[b, 0:64, :], blocks[b], bufs.at[k], rows.at[k])
            fill_taps(rows.at[k], wides.at[k], taps, b, shift)
        part = slice(ROWS * GROUP * g, ROWS * GROUP * (g + 1))
        y[64 + part.start : 64 + part.stop, :] = dot_nt(taps[part, :], w[...])
        if g > 0:
            merge_group(g - 1, blocks, y, regs, totals, outs, out_ref)
    merge_group(NB // GROUP - 1, blocks, y, regs, totals, outs, out_ref)


def merge_group(g, blocks, y, regs, totals, outs, out_ref):
    for b in range(GROUP * g, GROUP * g + GROUP):
        k = b % 2
        fill_regions(blocks[b], regs.at[k])
        out_ref[b] = merge(y, b, regs.at[k], totals.at[k], outs.at[k], blocks[b])


def conv_fwd_kernel(lens_ref, meta_ref, src_ref, own_ref, other_ref, out_ref, w, *scratch):
    @pl.when(pl.program_id(0) == 0)
    def _():
        x = meta_ref[2]
        for m in range(8):
            cols = slice(1024 * m, 1024 * m + 1024)
            w[pl.ds(pl.multiple_of(64 * m + 32 * x, 32), 32), :] = own_ref[:, cols]
            w[pl.ds(pl.multiple_of(64 * m + 32 * (1 - x), 32), 32), :] = other_ref[:, cols]

    conv_body(lens_ref, src_ref, w, out_ref, scratch, 0)


def conv_back_kernel(lens_ref, meta_ref, src_ref, own_ref, other_ref, out_ref, w, *scratch):
    @pl.when(pl.program_id(0) == 0)
    def _():
        x = meta_ref[2]
        for t in range(64):
            cols = slice(128 * t, 128 * t + 128)
            a, b = f32(own_ref[:, cols]), f32(other_ref[:, cols])
            pair = jnp.concatenate([jnp.where(x == 0, a, b), jnp.where(x == 0, b, a)], axis=0).T
            place = 127 - (2 * t + 1)
            m, j = place // 16, place % 16
            w[64 * m : 64 * m + 64, 64 * j : 64 * j + 64] = low(pair[64:128])
            w[64 * m : 64 * m + 64, 64 * j + 64 : 64 * j + 128] = low(pair[0:64])

    conv_body(lens_ref, src_ref, w, out_ref, scratch, 1)


def conv_grad_kernel(lens_ref, meta_ref, src_ref, g_ref, keep_ref, send_ref, acc, gt, buf, rows, wide, taps, reg, pair, regs):
    step = pl.program_id(0)
    for b in range(NB):
        starts = starts_of(lens_ref, step * NB + b)
        spread(src_ref[b, 0:64, :], starts, buf, rows)
        fill_taps(rows, wide, taps, b, 0)
        fill_regions(starts, reg)
        spread(g_ref[b, 0:64, :], starts, buf, rows.at[64:288])
        lo = left((320, 128))
        pair[16:336, :] = jnp.where(lo, rows[16:336, :], rows[0:320, :])
        regs[16:336, :] = jnp.where(lo, reg[16:336, :], reg[0:320, :])
        mine = reg[64 : 64 + ROWS, :]
        for m in range(4):
            first = 128 - 32 * m
            keep = regs[first : first + ROWS, :] == mine
            gt[ROWS * b : ROWS * b + ROWS, 128 * m : 128 * m + 128] = low(jnp.where(keep, pair[first : first + ROWS, :], 0.0))
    term = dot_tn(gt[...], taps[...])

    @pl.when(step == 0)
    def _():
        acc[...] = term

    @pl.when(step > 0)
    def _():
        acc[...] += term

    @pl.when(step == pl.num_programs(0) - 1)
    def _():
        x = meta_ref[2]
        for m in range(8):
            cols = slice(1024 * m, 1024 * m + 1024)
            keep_ref[:, cols] = acc[pl.ds(pl.multiple_of(64 * m + 32 * x, 32), 32), :]
            send_ref[:, cols] = low(acc[pl.ds(pl.multiple_of(64 * m + 32 * (1 - x), 32), 32), :])


def conv_call(kernel, lens, meta, arrays, outs, out_specs, scratch, after=(), cost=30):
    blocks = arrays[0].shape[0]
    in_specs = [
        pl.BlockSpec((NB, *a.shape[1:]), lambda i, l, m: (i, 0, 0)) if a.ndim == 3 else pl.BlockSpec(a.shape, lambda i, l, m: (0, 0))
        for a in arrays
    ]
    count = 2 + len(arrays)

    def body(*refs):
        kernel(*refs[:count], *refs[count + len(after) :])

    return pl.pallas_call(
        body,
        grid_spec=pltpu.PrefetchScalarGridSpec(
            num_scalar_prefetch=2, grid=(blocks // NB,), in_specs=in_specs + [ANY] * len(after), out_specs=out_specs, scratch_shapes=scratch
        ),
        out_shape=outs,
        compiler_params=pltpu.CompilerParams(vmem_limit_bytes=20 << 20),
        cost_estimate=estimate(cost),
    )(lens, meta, *[a if a.ndim == 3 else in_hbm(a) for a in arrays], *after)


def conv_pass(kernel, lens, meta, src, own, other, after=(), cost=30):
    scratch = [
        pltpu.VMEM((512, 1024), BF), pltpu.VMEM((2, 304, 128), F32), pltpu.VMEM((2, 232, 128), F32), pltpu.VMEM((2, 224, 128), F32),
        pltpu.VMEM((ROWS * NB, 1024), BF), pltpu.VMEM((2, 336, 128), jnp.int32), pltpu.VMEM((128 + ROWS * NB, 512), F32),
        pltpu.VMEM((2, 224, 128), F32), pltpu.VMEM((2, ROWS, 128), F32),
    ]
    spec = pl.BlockSpec((NB, 64, 128), lambda i, l, m: (i, 0, 0))
    return conv_call(kernel, lens, meta, (src, own, other), shape((src.shape[0], 64, 128)), spec, scratch, after, cost)


def conv_grads(lens, meta, src, grad, after=(), cost=30):
    scratch = [
        pltpu.VMEM((512, 1024), F32), pltpu.VMEM((ROWS * NB, 512), BF), pltpu.VMEM((304, 128), F32), pltpu.VMEM((336, 128), F32),
        pltpu.VMEM((224, 128), F32), pltpu.VMEM((ROWS * NB, 1024), BF), pltpu.VMEM((336, 128), jnp.int32), pltpu.VMEM((336, 128), F32),
        pltpu.VMEM((336, 128), jnp.int32),
    ]
    spec = pl.BlockSpec((32, 8192), lambda i, l, m: (0, 0))
    return conv_call(conv_grad_kernel, lens, meta, (src, grad), [out_hbm(shape((32, 8192), F32)), out_hbm(shape((32, 8192)))], [spec, spec], scratch, after, cost)


INV_SQRT2 = 0.7071067811865476
INV_SQRT_2PI = 0.3989422804014327


def gelu_cdf(v):
    return 0.5 + 0.5 * lax.erf(v * INV_SQRT2)


def gelu_slope(v, cdf):
    return cdf + v * (jnp.exp(-0.5 * v * v) * INV_SQRT_2PI)


def normed(v):
    centred = v - jnp.mean(v, axis=-1, keepdims=True)
    scale = lax.rsqrt(jnp.mean(centred * centred, axis=-1, keepdims=True) + norm_eps)
    return centred * scale, scale


def norm_pull(unit, scale, gain, grad):
    grad_unit = grad * gain
    mean_grad = jnp.mean(grad_unit, axis=-1, keepdims=True)
    mean_both = jnp.mean(grad_unit * unit, axis=-1, keepdims=True)
    return scale * (grad_unit - mean_grad - unit * mean_both)


def column_sum(v):
    return jnp.sum(v, axis=0, keepdims=True)


def norm_one_kernel(c_ref, f_ref, vec_ref, act_ref, zero_ref, zero_out_ref, n_ref):
    for g in range(8):
        tile = slice(128 * g, 128 * g + 128)
        a, b = cross(f32(c_ref[2 * g]), f32(c_ref[2 * g + 1]))
        act_ref[0:64, tile] = a + vec_ref[0:1, tile]
        act_ref[64:128, tile] = b + vec_ref[0:1, tile]
    for i in range(4):
        rows = slice(32 * i, 32 * i + 32)
        act = act_ref[rows, :]
        zero = f32(f_ref[rows, :]) + act * gelu_cdf(act)
        zero_ref[rows, :] = zero
        zero_out_ref[rows, :] = zero
        n_ref[rows, :] = low(normed(zero)[0] * vec_ref[1:2, :] + vec_ref[2:3, :])


def norm_two_kernel(zero_ref, keep_ref, got_ref, vec_ref, one_ref, n_ref):
    for i in range(4):
        rows = slice(32 * i, 32 * i + 32)
        one = zero_ref[rows, :] + vec_ref[5:6, :] + keep_ref[rows, :] + f32(got_ref[rows, :])
        one_ref[rows, :] = one
        n_ref[rows, :] = low(normed(one)[0] * vec_ref[6:7, :] + vec_ref[7:8, :])


def norm_two_back_kernel(keep_ref, got_ref, got_y_ref, got_d_ref, one_ref, g_ref, vec_ref, grad_ref, low_ref, sum_ref):
    sums = [jnp.zeros((1, 1024), jnp.float32) for _ in range(4)]
    for i in range(4):
        rows = slice(32 * i, 32 * i + 32)
        grad = keep_ref[rows, :] + f32(got_ref[rows, :]) + f32(got_y_ref[rows, :]) + f32(got_d_ref[rows, :])
        unit, scale = normed(one_ref[rows, :])
        out = f32(g_ref[rows, :])
        total = out + norm_pull(unit, scale, vec_ref[6:7, :], grad)
        grad_ref[rows, :] = total
        low_ref[rows, :] = low(total)
        for k, v in enumerate((total, grad * unit, grad, out)):
            sums[k] = sums[k] + column_sum(v)
    for k in range(4):
        sum_ref[k : k + 1, :] = sums[k]


def norm_one_back_kernel(meta_ref, keep_ref, got_ref, zero_ref, act_ref, one_grad_ref, vec_ref, two_ref, qv_ref, up_ref, grad_ref, pack_ref, conv):
    c, x = meta_ref[3], meta_ref[2]
    sums = [jnp.zeros((1, 1024), jnp.float32) for _ in range(3)]
    for i in range(4):
        rows = slice(32 * i, 32 * i + 32)
        grad = keep_ref[rows, :] + f32(got_ref[rows, :])
        unit, scale = normed(zero_ref[rows, :])
        total = one_grad_ref[rows, :] + norm_pull(unit, scale, vec_ref[1:2, :], grad)
        grad_ref[rows, :] = total
        act = act_ref[rows, :]
        conv_grad = total * gelu_slope(act, gelu_cdf(act))
        conv[rows, :] = conv_grad
        for k, v in enumerate((conv_grad, grad * unit, grad)):
            sums[k] = sums[k] + column_sum(v)
    lane = lax.broadcasted_iota(jnp.int32, (1, 128), 1)
    for g in range(8):
        tile = slice(128 * g, 128 * g + 128)
        p, q = cross(conv[0:64, tile], conv[64:128, tile])
        pack_ref[2 * g, 0:64, :] = low(p)
        pack_ref[2 * g + 1, 0:64, :] = low(q)
        source = qv_ref[0:2, 128 * (g // 2) : 128 * (g // 2) + 128]
        even = jnp.where(lane < 64, source, 0.0) if g % 2 == 0 else jnp.where(lane < 64, turn(source), 0.0)
        heads = jnp.where(c == 0, even, turn(even))
        up_rows = []
        for k in range(4):
            piece = up_ref[0:1, 128 * (g // 2) : 128 * (g // 2) + 128]
            piece = pltpu.roll(piece, (128 - 32 * k) % 128, 1) if k else piece
            piece = jnp.where(lane < 32, piece, 0.0)
            piece = jnp.where(x == 0, piece, pltpu.roll(piece, 32, 1))
            piece = jnp.where(c == 0, piece, turn(piece))
            up_rows.append(jnp.where(meta_ref[1] == g % 2, piece, 0.0))
        all_rows = [sums[0][:, tile], sums[1][:, tile], sums[2][:, tile], heads[0:1], heads[1:2], two_ref[0:1, tile],
                    two_ref[1:2, tile], two_ref[2:3, tile], two_ref[3:4, tile], *up_rows, jnp.zeros((3, 128), jnp.float32)]
        block = jnp.concatenate(all_rows, axis=0)
        pack_ref[2 * g, 64:80, :] = low(block)
        pack_ref[2 * g + 1, 64:80, :] = low(turn(block))


def final_kernel(c_ref, grad_ref, o_ref):
    for g in range(8):
        tile = slice(128 * g, 128 * g + 128)
        a, b = cross(f32(c_ref[2 * g]), f32(c_ref[2 * g + 1]))
        o_ref[0:64, tile] = grad_ref[0:64, tile] + a
        o_ref[64:128, tile] = grad_ref[64:128, tile] + b


def related(lens_ref, block):
    row = lax.broadcasted_iota(jnp.int32, (128, 128), 0)
    col = lax.broadcasted_iota(jnp.int32, (128, 128), 1)
    first = jnp.zeros((128, 128), jnp.int32)
    last = jnp.full((128, 128), 128, jnp.int32)
    e = 0
    for i in range(4):
        e = e + lens_ref[block * 4 + i]
        first = jnp.maximum(first, jnp.where(row >= e, e, 0))
        last = jnp.minimum(last, jnp.where(row < e, e, 128))
    return (col >= first) & (col < last)


def head_probs(query, key, rel, mine):
    masked_query = jnp.where(mine, query, jnp.zeros_like(query))
    scores = dot_nt(masked_query, key) * score_scale
    scores = jnp.where(rel, scores, -1000000000.0)
    top = jnp.max(scores, axis=-1, keepdims=True)
    expd = jnp.exp(scores - top)
    return expd / jnp.sum(expd, axis=-1, keepdims=True)


def attn_places(meta_ref, pieces, wqkv, wo):
    own, along_x, along_y, diag_a, diag_b = pieces
    y, x, c = meta_ref[1], meta_ref[2], meta_ref[3]
    groups = [[], [], [], []]
    every, low_z, high_z = slice(0, 4), slice(0, 2), slice(2, 4)
    for dy, dx, zs, src in (
        (0, 0, every, own), (0, 1, every, along_x), (1, 0, every, along_y), (1, 1, low_z, diag_a), (1, 1, high_z, diag_b)
    ):
        yy, xx = y ^ dy, x ^ dx
        for i in range(8):
            place = wqkv.at[i % 3, zs, yy, c ^ (i // 3), xx] if i < 6 else wo.at[i - 6, zs, yy, xx]
            groups[i % 3 if i < 6 else 3].append((src.at[:, i], place))
    return groups


def attn_scratch():
    return [pltpu.VMEM((3, 4, 2, 2, 2, 32, 512), BF), pltpu.VMEM((2, 4, 2, 2, 32, 512), BF)]


def attn_fwd_kernel(
    meta_ref, lens_ref, n_ref, n_other_ref, own, along_x, along_y, diag_a, diag_b, bias_ref,
    q_ref, k_ref, v_ref, m_ref, keep_ref, send_ref, wqkv, wo, ready,
):
    n = jnp.concatenate([n_ref[...], n_other_ref[...]], axis=0)
    ready(0)
    q_ref[...] = low(dot(n, wqkv[0].reshape(1024, 512)) + bias_ref[0:1, :])
    ready(1)
    k_ref[...] = low(dot(n, wqkv[1].reshape(1024, 512)))
    ready(2)
    v_ref[...] = low(dot(n, wqkv[2].reshape(1024, 512)) + bias_ref[1:2, :])
    half = lax.broadcasted_iota(jnp.int32, (128, 128), 1) // 64
    for b in range(2):
        rel = related(lens_ref, meta_ref[0] ^ b)
        for p in range(4):
            at = (slice(128 * b, 128 * b + 128), slice(128 * p, 128 * p + 128))
            query, key, value = q_ref[at], k_ref[at], v_ref[at]
            outs = [dot(low(head_probs(query, key, rel, half == h)), value) for h in range(2)]
            m_ref[at] = low(jnp.where(half == 0, outs[0], outs[1]))
    mixed = m_ref[...]
    ready(3)
    for h in range(2):
        out = dot(mixed, wo[h].reshape(512, 512))
        keep_ref[:, 512 * h : 512 * h + 512] = out[0:128]
        send_ref[:, 512 * h : 512 * h + 512] = low(out[128:256])


def attn_bwd_kernel(
    meta_ref, lens_ref, g_ref, g_other_ref, q_ref, k_ref, v_ref, own, along_x, along_y, diag_a, diag_b,
    dq_ref, dk_ref, dv_ref, sum_ref, keep_ref, send_ref, wqkv, wo, ready,
):
    grad_in = jnp.concatenate([g_ref[...], g_other_ref[...]], axis=0)
    ready(3)
    mixed_grad = low(dot_nt(grad_in[:, 0:512], wo[0].reshape(512, 512)) + dot_nt(grad_in[:, 512:1024], wo[1].reshape(512, 512)))
    half = lax.broadcasted_iota(jnp.int32, (128, 128), 1) // 64
    for p in range(4):
        sums = []
        for b in range(2):
            rel = related(lens_ref, meta_ref[0] ^ b)
            at = (slice(128 * b, 128 * b + 128), slice(128 * p, 128 * p + 128))
            query, key, value = q_ref[at], k_ref[at], v_ref[at]
            grad = mixed_grad[128 * b : 128 * b + 128, 128 * p : 128 * p + 128]
            dqs, dks, dvs = [], [], []
            for h in range(2):
                probs = head_probs(query, key, rel, half == h)
                grad_h = jnp.where(half == h, grad, jnp.zeros_like(grad))
                prob_grad = dot_nt(grad_h, value)
                dvs.append(dot_tn(low(probs), grad))
                score_grad = probs * (prob_grad - jnp.sum(probs * prob_grad, axis=-1, keepdims=True))
                score_low = low(score_grad)
                dqs.append(dot(score_low, key) * score_scale)
                dks.append(dot_tn(score_low, query) * score_scale)
            dq = jnp.where(half == 0, dqs[0], dqs[1])
            dk = jnp.where(half == 0, dks[0], dks[1])
            dv = jnp.where(half == 0, dvs[0], dvs[1])
            dq_ref[at], dk_ref[at], dv_ref[at] = low(dq), low(dk), low(dv)
            sums.append((column_sum(dq), column_sum(dv)))
        sum_ref[0:1, 128 * p : 128 * p + 128] = sums[0][0] + sums[1][0]
        sum_ref[1:2, 128 * p : 128 * p + 128] = sums[0][1] + sums[1][1]
    for j in range(3):
        ready(j)
    out = dot_nt(dq_ref[...], wqkv[0].reshape(1024, 512))
    out += dot_nt(dk_ref[...], wqkv[1].reshape(1024, 512))
    out += dot_nt(dv_ref[...], wqkv[2].reshape(1024, 512))
    keep_ref[...] = out[0:128]
    send_ref[...] = low(out[128:256])


def term_plan(meta_ref, own, send_x, send_y, keep_a, keep_b, gqkv, go):
    y, x, c = meta_ref[1], meta_ref[2], meta_ref[3]
    plan = []
    for dy, dx in ((0, 0), (0, 1), (1, 0), (1, 1)):
        yy, xx = y ^ dy, x ^ dx
        for i in range(8):
            if dy == 0 and dx == 0:
                part = own.at[:, i]
            elif i < 4:
                part = send_x.at[dy, :, i] if dx == 1 else keep_a.at[:, i]
            else:
                part = send_y.at[dx, :, i - 4] if dy == 1 else keep_b.at[:, i - 4]
            plan.append((gqkv.at[i % 3, :, yy, c ^ (i // 3), xx] if i < 6 else go.at[i - 6, :, yy, xx], part))
    return plan


def attn_term_kernel(meta_ref, n_ref, n_other_ref, dq_ref, dk_ref, dv_ref, m_ref, g_ref, g_other_ref, own, send_x, send_y, keep_a, keep_b, gqkv, go, sems):
    for z in range(4):
        cols = slice(256 * z, 256 * z + 256)
        n = jnp.concatenate([n_ref[:, cols], n_other_ref[:, cols]], axis=0)
        for j, ref in enumerate((dq_ref, dk_ref, dv_ref)):
            gqkv[j, z] = low(dot_tn(n, ref[...])).reshape(2, 2, 2, 32, 512)
    grad = jnp.concatenate([g_ref[...], g_other_ref[...]], axis=0)
    for z in range(4):
        term = low(dot_tn(m_ref[:, 128 * z : 128 * z + 128], grad))
        for h in range(2):
            go[h, z] = term[:, 512 * h : 512 * h + 512].reshape(2, 2, 32, 512)
    run_copies(term_plan(meta_ref, own, send_x, send_y, keep_a, keep_b, gqkv, go), sems)


def ffn_plan(both, wu, wd):
    return [[(both.at[:, 0:256], wu)], [(both.at[:, 256:384], wd.at[0]), (both.at[:, 384:512], wd.at[1])]]


def ffn_scratch():
    return [pltpu.VMEM((4, 256, 512), BF), pltpu.VMEM((2, 4, 128, 512), BF)]


def ffn_kernel(*refs):
    n_refs, g_refs, bias_ref = refs[0:8], refs[8:16], refs[17]
    act_ref, ug_ref, keep_ref, send_ref, sum_ref, wu, wd, ready = refs[18:26]
    ready(0)
    total = jnp.zeros((1, 512), jnp.float32)
    for i in (4, 5, 6, 7, 0, 1, 2, 3):
        rows = slice(128 * i, 128 * i + 128)
        up_pre = dot(n_refs[i][...], wu[...].reshape(1024, 512)) + bias_ref[...]
        cdf = gelu_cdf(up_pre)
        act_ref[rows, :] = low(up_pre * cdf)
        if i == 4:
            ready(1)
        act_grad = dot_nt(g_refs[i][:, 0:512], wd[0].reshape(512, 512)) + dot_nt(g_refs[i][:, 512:1024], wd[1].reshape(512, 512))
        up_grad = act_grad * gelu_slope(up_pre, cdf)
        total = total + column_sum(up_grad)
        ug_ref[rows, :] = low(up_grad)
        back = dot_nt(low(up_grad), wu[...].reshape(1024, 512))
        if i >= 4:
            send_ref[128 * i - 512 : 128 * i - 384, :] = low(back)
        else:
            keep_ref[rows, :] = back
    sum_ref[...] = total


def ffn_out_kernel(act_ref, both_ref, keep_ref, send_ref, wd, ready):
    ready(0)
    for h in range(2):
        cols = slice(512 * h, 512 * h + 512)
        keep_ref[:, cols] = dot(act_ref[0:512, :], wd[h].reshape(512, 512))
        send_ref[:, cols] = low(dot(act_ref[512:1024, :], wd[h].reshape(512, 512)))


def half_sum_kernel(keep_ref, got_ref, own_ref, x_ref, y_ref, across_ref):
    own_ref[...] = keep_ref[0:128, :] + f32(got_ref[0:128, :])
    for i, ref in enumerate((x_ref, y_ref, across_ref), 1):
        rows = slice(128 * i, 128 * i + 128)
        ref[...] = low(keep_ref[rows, :] + f32(got_ref[rows, :]))


def ffn_terms(act, grads, normeds, up_grad, after, cost=20):
    def body(*refs):
        act_ref, g_refs, n_refs, u_ref, out_ref = refs[0], refs[1:9], refs[9:17], refs[17], refs[-1]
        n = jnp.concatenate([ref[...] for ref in n_refs], axis=0)
        out_ref[0, 0:256] = low(dot_tn(n, u_ref[...]))
        g = jnp.concatenate([ref[...] for ref in g_refs], axis=0)
        down = low(dot_tn(act_ref[...], g))
        out_ref[0, 256:384] = down[:, 0:512]
        out_ref[0, 384:512] = down[:, 512:1024]

    rows = pl.BlockSpec((128, 1024), lambda i: (0, 0))
    part = pl.BlockSpec((128, 256), lambda i: (0, i))
    return pl.pallas_call(
        body,
        grid=(4,),
        in_specs=[pl.BlockSpec((1024, 128), lambda i: (0, i))] + [rows] * 8 + [part] * 8
        + [pl.BlockSpec((1024, 512), lambda i: (0, 0))] + [ANY] * len(after),
        out_specs=pl.BlockSpec((1, 512, 512), lambda i: (i, 0, 0)),
        out_shape=out_hbm(shape((4, 512, 512))),
        compiler_params=pltpu.CompilerParams(vmem_limit_bytes=20 << 20),
        cost_estimate=estimate(20),
    )(act, grads[0], *[in_hbm(v) for v in grads[1:]], normeds[0], *[in_hbm(v) for v in normeds[1:]], up_grad, *after)


def fold_call(keep_a, keep_b, got_x, got_y, after, cost=3):
    def body(a_ref, b_ref, x_ref, y_ref, *refs):
        refs[-2][...] = low(f32(a_ref[...]) + f32(x_ref[0]))
        refs[-1][...] = low(f32(b_ref[...]) + f32(y_ref[0]))

    part = pl.BlockSpec((2, 4, 32, 512), lambda i: (i, 0, 0, 0))
    second = pl.BlockSpec((1, 2, 4, 32, 512), lambda i: (1, i, 0, 0, 0))
    return pl.pallas_call(
        body,
        grid=(2,),
        in_specs=[part, part, second, second] + [ANY] * len(after),
        out_specs=[part, part],
        out_shape=[out_hbm(shape((4, 4, 32, 512)))] * 2,
        compiler_params=pltpu.CompilerParams(vmem_limit_bytes=16 << 20),
        cost_estimate=estimate(cost),
    )(in_hbm(keep_a), in_hbm(keep_b), in_hbm(got_x), in_hbm(got_y), *after)


def join_call(own, got_x, got_y, last_a, last_b, after, cost=3):
    def body(own_ref, x_ref, y_ref, a_ref, b_ref, *refs):
        refs[-1][:, 0:4] = low(f32(own_ref[:, 0:4]) + f32(x_ref[0]) + f32(a_ref[...]))
        refs[-1][:, 4:8] = low(f32(own_ref[:, 4:8]) + f32(y_ref[0]) + f32(b_ref[...]))

    full = pl.BlockSpec((2, 8, 32, 512), lambda i: (i, 0, 0, 0))
    part = pl.BlockSpec((2, 4, 32, 512), lambda i: (i, 0, 0, 0))
    first = pl.BlockSpec((1, 2, 4, 32, 512), lambda i: (0, i, 0, 0, 0))
    return pl.pallas_call(
        body,
        grid=(2,),
        in_specs=[full, first, first, part, part] + [ANY] * len(after),
        out_specs=full,
        out_shape=out_hbm(shape((4, 8, 32, 512))),
        compiler_params=pltpu.CompilerParams(vmem_limit_bytes=16 << 20),
        cost_estimate=estimate(cost),
    )(in_hbm(own), in_hbm(got_x), in_hbm(got_y), in_hbm(last_a), in_hbm(last_b), *after)


def output_kernel(one_ref, keep_ref, got_ref, got_y_ref, got_d_ref, vec_ref, o_ref):
    got = f32(got_ref[...]) + f32(got_y_ref[...]) + f32(got_d_ref[...])
    o_ref[...] = low(one_ref[...] + keep_ref[...] + got + vec_ref[8:9, :])


def up_grad_kernel(got_ref, sum_ref, up_ref, down_ref):
    for z in range(4):
        for k in range(8):
            at = 128 * (8 * z + k)
            up_ref[:, at : at + 128] = f32(got_ref[k, :, 128 * z : 128 * z + 128])
    down_ref[:, 0:512] = f32(sum_ref[256:384])
    down_ref[:, 512:1024] = f32(sum_ref[384:512])


def qkv_grad_kernel(meta_ref, sum_ref, got_ref, q_ref, k_ref, v_ref, o_ref):
    c = meta_ref[3]
    for j, ref in enumerate((q_ref, k_ref, v_ref)):
        for t in range(4):
            tile = slice(128 * t, 128 * t + 128)
            mine, theirs = f32(sum_ref[j, :, tile]), f32(got_ref[3 + j, :, tile])
            a, b = cross(jnp.where(c == 0, mine, theirs), jnp.where(c == 0, theirs, mine))
            ref[:, 256 * t : 256 * t + 128] = a
            ref[:, 256 * t + 128 : 256 * t + 256] = b
    for h in range(2):
        o_ref[:, 512 * h : 512 * h + 512] = f32(sum_ref[6 + h])


def swap(v, axis):
    return lax.ppermute(v, axis, [(0, 1), (1, 0)])


def swap_across(v):
    return lax.ppermute(v, ("y", "x"), [(i, 3 - i) for i in range(4)])


def gather_z(v):
    return lax.all_gather(v, "z", axis=0, tiled=False)


def scatter_z(v):
    return lax.psum_scatter(v, "z", scatter_dimension=0, tiled=False)


def pick(v, index, axis):
    return lax.dynamic_index_in_dim(v, index, axis, keepdims=False)


def local(
    frames, lengths, cotangent, conv_kernel, conv_bias, norm_one_gain, norm_one_bias,
    query_weight, query_bias, key_weight, value_weight, value_bias, out_weight, out_bias,
    norm_two_gain, norm_two_bias, up_weight, up_bias, down_weight, down_bias,
):
    zi, yi, ci, xi = (lax.axis_index(a) for a in ("z", "y", "c", "x"))
    meta = jnp.stack([(zi * 2 + yi) * 2 + ci, yi, xi, ci]).astype(jnp.int32)
    row, row_f, half = shape((128, 1024)), shape((128, 1024), F32), shape((256, 512))
    groups, plane = ("z", "y", "c"), ("y", "c", "x")

    def spread_plane(own, along_x, along_y, across):
        four = (own, along_x, along_y, across)
        return (*four, *(swap(v, "c") for v in four))

    def half_sum(keep, send, saved, cost, after):
        return whole_call(
            half_sum_kernel, (keep, swap(send, "c")), [saved, VMEM], [row_f, row, row, row], [saved] + [VMEM] * 3, cost=cost, after=after
        )

    vectors = (conv_bias, norm_one_gain, norm_one_bias, query_bias, value_bias, out_bias, norm_two_gain, norm_two_bias, down_bias, up_bias)
    qkv_mine, qkv_theirs, out_part, small = whole_call(
        first_kernel, (lengths, *vectors, query_weight, key_weight, value_weight, out_weight), [None] * 15,
        [shape((3, 32, 512)), shape((3, 32, 512)), shape((2, 32, 512)), shape((16, 128), F32)], [VMEM] * 4, cost=0.05, after=(),
    )
    attn_part = jnp.concatenate([qkv_mine, swap(qkv_theirs, "c"), out_part], axis=0)
    attn_own = gather_z(attn_part)

    up_split, grad_out, grad_send = whole_call(
        ffn_prep_kernel, (lengths, up_weight, cotangent), [None] * 3, [shape((8, 32, 512)), row, row], [VMEM] * 3, cost=0.05, after=(qkv_mine,)
    )
    grad_y = swap(grad_send, "y")
    up_part = lax.all_to_all(up_split, plane, 0, 0, tiled=True)

    payload = whole_call(pack_kernel, (frames, small), [None, VMEM], shape((16, 80, 128)), VMEM, cost=0.05, after=(in_hbm(attn_part), in_hbm(grad_y)))
    got = lax.all_to_all(payload, groups, 0, 0, tiled=True)
    kernel_other = swap(conv_kernel, "x")
    grad_x = swap(tie(grad_send, kernel_other), "x")
    lens = got[:, 77, 0:4].astype(jnp.int32).reshape(64)
    ffn_part = jnp.concatenate([up_part.reshape(256, 512), down_weight[:, :512], down_weight[:, 512:]], axis=0)
    ffn_both = gather_z(ffn_part)
    conv_out = conv_pass(conv_fwd_kernel, lens, meta, got, conv_kernel, kernel_other, cost=30, after=(in_hbm(attn_own), in_hbm(grad_x)))
    conv_got = lax.all_to_all(conv_out, groups, 0, 0, tiled=True)

    grad_d = swap_across(tie(grad_send, kernel_other))
    grads_out = spread_plane(grad_out, grad_x, grad_y, grad_d)
    attn_own = attn_own
    attn_x, attn_y = swap(attn_own, "x"), swap(attn_own, "y")
    diag_a, diag_b = swap(attn_x[0:2], "y"), swap(attn_y[2:4], "x")
    attn_pieces = (attn_own, attn_x, attn_y, diag_a, diag_b)

    got_small = got[:, 64:80]
    got_small_other = swap(got_small, "x")
    vec, up_bias_own, qv_bias = whole_call(
        vector_kernel, (meta, got_small, got_small_other), [SMEM, VMEM, VMEM],
        [shape((16, 1024), F32), shape((1, 512), F32), shape((2, 512), F32)], [VMEM] * 3, cost=3, after=(conv_out,),
    )
    conv_act, hidden_zero, zero_saved, n_one = whole_call(
        norm_one_kernel, (conv_got, frames, vec), [VMEM, None, VMEM], [row_f, row_f, row_f, row], [None, VMEM, None, VMEM],
        cost=1, after=(*(in_hbm(v) for v in grads_out[3:]), in_hbm(attn_x), in_hbm(attn_y)),
    )
    n_one_other = swap(n_one, "c")

    def attn_copies(first):
        return lambda *refs: attn_places(refs[0], refs[first : first + 5], refs[-2], refs[-1])

    query, key, value, mixed, attn_keep, attn_send = whole_call(
        attn_fwd_kernel, (meta, lens, n_one, n_one_other, *attn_pieces, qv_bias), [SMEM, SMEM, VMEM, VMEM] + [ANY] * 5 + [VMEM],
        [half] * 4 + [row_f, row], [None] * 4 + [VMEM] * 2, attn_scratch(), plan=attn_copies(4), vmem=16, cost=8, after=(),
    )
    hidden_one, n_two = whole_call(
        norm_two_kernel, (hidden_zero, attn_keep, swap(attn_send, "c"), vec), [VMEM] * 4, [row_f, row], [VMEM] * 2,
        cost=0.1, after=(in_hbm(ffn_both),),
    )

    n_twos = spread_plane(n_two, swap(n_two, "x"), swap(n_two, "y"), swap_across(n_two))
    many, many_f, many_half = shape((1024, 512)), shape((512, 1024), F32), shape((512, 1024))
    activated, up_grad, back_keep, back_send, up_bias_term = whole_call(
        ffn_kernel, (*n_twos, *grads_out, ffn_both, up_bias_own), ([VMEM] + [None] * 7) * 2 + [ANY, VMEM],
        [many, many, many_f, many_half, shape((1, 512), F32)], [VMEM] * 5, ffn_scratch(),
        plan=lambda *refs: ffn_plan(refs[16], refs[-2], refs[-1]), vmem=20, cost=30,
    )
    two_own, two_x, two_y, two_across = half_sum(back_keep, back_send, VMEM, 0.05, ())
    ffn_keep, ffn_send = whole_call(
        ffn_out_kernel, (activated, ffn_both), [VMEM, ANY], [many_f, many_half], [None, None], ffn_scratch()[1:],
        plan=lambda *refs: ffn_plan(refs[1], None, refs[-1])[1:], cost=1, after=(two_x,),
    )
    two_got = (swap(two_x, "x"), swap(two_y, "y"), swap_across(two_across))
    ffn_term = ffn_terms(activated, grads_out, n_twos, up_grad, (two_x,), 20)
    one_grad, attn_grad, two_sums = whole_call(
        norm_two_back_kernel, (two_own, *two_got, hidden_one, grad_out, vec), [VMEM] * 7, [row_f, row, shape((4, 1024), F32)],
        [None, VMEM, None], cost=5, after=(in_hbm(ffn_term), in_hbm(ffn_send)),
    )
    attn_grad_other = swap(attn_grad, "c")
    ffn_sum = scatter_z(ffn_term)
    dq, dk, dv, qv_sum, one_keep, one_send = whole_call(
        attn_bwd_kernel, (meta, lens, attn_grad, attn_grad_other, query, key, value, *attn_pieces),
        [SMEM, SMEM, VMEM, VMEM] + [None] * 3 + [ANY] * 5, [half] * 3 + [shape((2, 512), F32), row_f, row], [VMEM] * 6, attn_scratch(),
        plan=attn_copies(7), vmem=16, cost=70, after=(),
    )
    zero_grad, payload_back = whole_call(
        norm_one_back_kernel, (meta, one_keep, swap(one_send, "c"), zero_saved, conv_act, one_grad, vec, two_sums, qv_sum, up_bias_term),
        [SMEM, VMEM, VMEM, None, None, None, VMEM, None, VMEM, VMEM], [row_f, shape((16, 80, 128))], [None, VMEM],
        [pltpu.VMEM((128, 1024), F32)], cost=10, after=(),
    )
    grad_got = lax.all_to_all(payload_back, groups, 0, 0, tiled=True)
    out_own, out_x, out_y, out_across = half_sum(ffn_keep, ffn_send, None, 0.05, (payload_back,))

    piece, part = out_hbm(shape((4, 8, 32, 512))), out_hbm(shape((4, 4, 32, 512)))
    pair = out_hbm(shape((2, 4, 4, 32, 512)))
    term_own, term_x, term_y, keep_a, keep_b = whole_call(
        attn_term_kernel, (meta, n_one, n_one_other, dq, dk, dv, mixed, attn_grad, attn_grad_other),
        [SMEM, VMEM, VMEM] + [None] * 4 + [VMEM] * 2, [piece, pair, pair, part, part], [HBM] * 5,
        attn_scratch() + [pltpu.SemaphoreType.DMA((32,))], vmem=16, cost=1, after=(payload_back,),
    )
    got_x, got_y = swap(term_x, "x"), swap(term_y, "y")
    conv_back_out = conv_pass(conv_back_kernel, lens, meta, grad_got, conv_kernel, kernel_other, cost=10, after=(out_x,))
    send_a, send_b = fold_call(keep_a, keep_b, got_x, got_y, (conv_back_out,), 3)
    back_got = lax.all_to_all(conv_back_out, groups, 0, 0, tiled=True)
    out_got = (swap(tie(out_x, send_b), "x"), swap(tie(out_y, send_b), "y"), swap_across(tie(out_across, send_b)))
    kernel_keep, kernel_send = conv_grads(lens, meta, got, grad_got, cost=30, after=(conv_back_out,))
    last_a, last_b = swap(send_a, "y"), swap(send_b, "x")
    attn_half = join_call(term_own, got_x, got_y, last_a, last_b, (kernel_send, back_got, in_hbm(ffn_sum)), 3)
    attn_sum = scatter_z(attn_half)

    frames_grad = whole_call(final_kernel, (back_got, zero_grad), [VMEM, None], row_f, None, cost=0.05, after=(in_hbm(attn_half),))
    output = whole_call(
        output_kernel, (hidden_one, out_own, *out_got, vec), [VMEM, None] + [VMEM] * 4, row, None, cost=0.05, after=(in_hbm(attn_half),)
    )
    kernel_grad = kernel_keep + f32(swap(kernel_send, "x"))
    ffn_sum = tie(ffn_sum, attn_half)
    up_got = lax.all_to_all(ffn_sum[0:256].reshape(8, 32, 512), plane, 0, 0, tiled=True)
    up_weight_grad, down_weight_grad = whole_call(
        up_grad_kernel, (up_got, ffn_sum), [VMEM, None], [shape((32, 4096), F32), shape((128, 1024), F32)], [None] * 2, cost=0.05
    )
    small_sum = jnp.sum(f32(grad_got[:, 64:80, 0:64]), axis=0).reshape(16, 2, 32)
    small_grad = pick(small_sum, xi, 1) + swap(tie(pick(small_sum, 1 - xi, 1), send_a), "x")
    small_grads = [small_grad[i] for i in range(9)]
    attn_sum = tie(attn_sum, output, up_weight_grad, kernel_grad, small_grad, frames_grad)
    query_weight_grad, key_weight_grad, value_weight_grad, out_weight_grad = whole_call(
        qkv_grad_kernel, (meta, attn_sum, swap(attn_sum, "c")), [SMEM, None, None], [shape((32, 1024), F32)] * 4, [None] * 4
    )

    return (
        output, frames_grad, kernel_grad, small_grads[0], small_grads[1], small_grads[2], query_weight_grad, small_grads[3],
        key_weight_grad, value_weight_grad, small_grads[4], out_weight_grad, small_grads[5], small_grads[6], small_grads[7],
        up_weight_grad, small_grad[9:13].reshape(128), down_weight_grad, small_grads[8],
    )


MATRICES_IN = (0, 1, 2, 3, 7, 9, 10, 12, 16, 18)
MATRICES_OUT = (0, 1, 2, 6, 8, 9, 11, 15, 17)


def solution(mesh):
    n_dp, n_fsdp = mesh.shape["dp"], mesh.shape["fsdp"]
    if n_fsdp == 2 and n_dp == GROUPS:
        axes = ("z", "y", "c", "x")
        mesh = Mesh(mesh.devices.reshape(n_dp // 4, 2, 2, n_fsdp), axes)
        body = local
    else:
        axes = ("dp", "fsdp")
        body = local_plain
    in_specs = tuple(P(axes, None) if i in MATRICES_IN else P(axes) for i in range(20))
    out_specs = tuple(P(axes, None) if i in MATRICES_OUT else P(axes) for i in range(19))
    return jax.shard_map(body, mesh=mesh, in_specs=in_specs, out_specs=out_specs, check_vma=False)
```

```python
import functools

import jax
import jax.numpy as jnp
import numpy as np
from jax import lax
from jax.experimental import pallas as pl
from jax.experimental.pallas import tpu as pltpu
from jax.sharding import Mesh
from jax.sharding import PartitionSpec as P

HEAD_DIM = 64
GROUPS = 16
KW = 128


norm_eps = 1e-05
score_scale = 0.125


def layer_norm(rows, scale_vec, shift_vec):
    row_mean = jnp.mean(rows, axis=-1, keepdims=True)
    centred = rows - row_mean
    spread = jnp.mean(centred * centred, axis=-1, keepdims=True)
    return centred * lax.rsqrt(spread + norm_eps) * scale_vec + shift_vec


def gelu_exact(values):
    return jax.nn.gelu(values, approximate=False)


def unfold(source, segment, first_tap, tap_count, flipped):
    rows_count, model_width = source.shape
    half_width = KW // 2
    channels = model_width // GROUPS
    padded = jnp.pad(source, ((half_width, half_width), (0, 0))).reshape(
        rows_count + KW, GROUPS, channels
    )
    seg_padded = jnp.pad(segment, (half_width, half_width), constant_values=-1)
    offsets = [
        KW - tap_index if flipped else tap_index
        for tap_index in range(first_tap, first_tap + tap_count)
    ]
    shifted = jnp.stack([padded[offset : offset + rows_count] for offset in offsets], axis=2)
    same_seg = jnp.stack(
        [seg_padded[offset : offset + rows_count] == segment for offset in offsets], axis=1
    )
    kept_taps = jnp.where(same_seg[:, None, :, None], shifted, jnp.zeros((), source.dtype))
    return kept_taps.reshape(rows_count, GROUPS, tap_count * channels)


def conv_forward(source, segment, conv_kernel):
    rows_count, model_width = source.shape
    channels = model_width // GROUPS
    tap_count = KW // 8
    summed = jnp.zeros((rows_count, GROUPS, channels), jnp.float32)
    for block_index in range(8):
        first_tap = block_index * tap_count
        unfolded = unfold(source, segment, first_tap, tap_count, False)
        kernel_block = conv_kernel[:, first_tap * channels : (first_tap + tap_count) * channels]
        kernel_block = kernel_block.reshape(GROUPS, channels, tap_count * channels)
        summed = summed + jnp.einsum(
            "tgi,goi->tgo", unfolded, kernel_block, preferred_element_type=jnp.float32
        )
    return summed.reshape(rows_count, model_width)


def conv_backward(source, segment, conv_kernel, grad_low):
    rows_count, model_width = source.shape
    channels = model_width // GROUPS
    tap_count = KW // 8
    grad_groups = grad_low.reshape(rows_count, GROUPS, channels)
    kernel_pieces = []
    input_grad = jnp.zeros((rows_count, GROUPS, channels), jnp.float32)
    for block_index in range(8):
        first_tap = block_index * tap_count
        unfolded = unfold(source, segment, first_tap, tap_count, False)
        kernel_term = jnp.einsum(
            "tgo,tgi->goi", grad_groups, unfolded, preferred_element_type=jnp.float32
        )
        kernel_pieces.append(kernel_term.reshape(model_width, tap_count * channels))
        turned = unfold(grad_low, segment, first_tap, tap_count, True).reshape(
            rows_count, GROUPS, tap_count, channels
        )
        kernel_block = conv_kernel[:, first_tap * channels : (first_tap + tap_count) * channels]
        kernel_block = kernel_block.reshape(GROUPS, channels, tap_count, channels)
        input_grad = input_grad + jnp.einsum(
            "tgko,gokc->tgc", turned, kernel_block, preferred_element_type=jnp.float32
        )
    return (kernel_pieces, input_grad.reshape(rows_count, model_width))


def sum_kernel_half(piece):
    return lax.psum_scatter(piece, ("dp", "fsdp"), scatter_dimension=0, tiled=True)


def attention_scores(query_h, key_h, related):
    scores = (
        jnp.einsum("qhd,khd->hqk", query_h, key_h, preferred_element_type=jnp.float32) * score_scale
    )
    return jnp.where(related[None], scores, -1000000000.0)


def local_plain(
    frames,
    lengths,
    cotangent,
    conv_kernel,
    conv_bias,
    norm_one_gain,
    norm_one_bias,
    query_weight,
    query_bias,
    key_weight,
    value_weight,
    value_bias,
    out_weight,
    out_bias,
    norm_two_gain,
    norm_two_bias,
    up_weight,
    up_bias,
    down_weight,
    down_bias,
):
    rows_count, model_width = frames.shape
    head_count = model_width // HEAD_DIM
    ends = jnp.cumsum(lengths[0])
    positions = lax.broadcasted_iota(jnp.int32, (rows_count, ends.shape[0]), 0)
    segment = jnp.sum((positions >= ends[None, :]).astype(jnp.int32), axis=1)
    valid = (segment < ends.shape[0]).astype(jnp.float32)
    related = segment[:, None] == segment[None, :]
    conv_set = (conv_kernel, conv_bias, norm_one_gain, norm_one_bias)
    attn_set = (
        query_weight,
        key_weight,
        value_weight,
        out_weight,
        query_bias,
        value_bias,
        out_bias,
    )
    ffn_set = (up_weight, down_weight, up_bias, down_bias, norm_two_gain, norm_two_bias)
    source_f = frames.astype(jnp.float32)
    conv_full = (
        lax.all_gather(conv_set[0], ("dp", "fsdp"), axis=0, tiled=True),
        lax.all_gather(conv_set[1], ("dp", "fsdp"), axis=0, tiled=True),
        lax.all_gather(conv_set[2], ("dp", "fsdp"), axis=0, tiled=True),
        lax.all_gather(conv_set[3], ("dp", "fsdp"), axis=0, tiled=True),
    )
    kernel_full, conv_bias_full, gain_one, shift_one = conv_full
    conv_act = conv_forward(frames, segment, kernel_full) + conv_bias_full.astype(jnp.float32)
    conv_gelu, conv_pull = jax.vjp(gelu_exact, conv_act)
    hidden_zero = source_f + conv_gelu
    normed_one, norm_one_pull = jax.vjp(
        layer_norm, hidden_zero, gain_one.astype(jnp.float32), shift_one.astype(jnp.float32)
    )
    normed_one_low = normed_one.astype(jnp.bfloat16)
    attn_full = (
        lax.all_gather(attn_set[0], ("dp", "fsdp"), axis=0, tiled=True),
        lax.all_gather(attn_set[1], ("dp", "fsdp"), axis=0, tiled=True),
        lax.all_gather(attn_set[2], ("dp", "fsdp"), axis=0, tiled=True),
        lax.all_gather(attn_set[3], ("dp", "fsdp"), axis=0, tiled=True),
        lax.all_gather(attn_set[4], ("dp", "fsdp"), axis=0, tiled=True),
        lax.all_gather(attn_set[5], ("dp", "fsdp"), axis=0, tiled=True),
        lax.all_gather(attn_set[6], ("dp", "fsdp"), axis=0, tiled=True),
    )
    query_full, key_full, value_full, out_full, query_bias_full, value_bias_full, out_bias_full = (
        attn_full
    )
    query_low = (
        jnp.dot(normed_one_low, query_full, preferred_element_type=jnp.float32)
        + query_bias_full.astype(jnp.float32)
    ).astype(jnp.bfloat16)
    key_low = jnp.dot(normed_one_low, key_full, preferred_element_type=jnp.float32).astype(
        jnp.bfloat16
    )
    value_low = (
        jnp.dot(normed_one_low, value_full, preferred_element_type=jnp.float32)
        + value_bias_full.astype(jnp.float32)
    ).astype(jnp.bfloat16)
    query_h = query_low.reshape(rows_count, head_count, HEAD_DIM)
    key_h = key_low.reshape(rows_count, head_count, HEAD_DIM)
    value_h = value_low.reshape(rows_count, head_count, HEAD_DIM)
    scores = attention_scores(query_h, key_h, related)
    row_top = jnp.max(scores, axis=-1, keepdims=True)
    expd = jnp.exp(scores - row_top)
    row_total = jnp.sum(expd, axis=-1, keepdims=True)
    probs = expd / row_total
    logsum = row_top + jnp.log(row_total)
    mixed = jnp.einsum(
        "hqk,khd->qhd", probs.astype(jnp.bfloat16), value_h, preferred_element_type=jnp.float32
    )
    mixed_low = mixed.reshape(rows_count, model_width).astype(jnp.bfloat16)
    hidden_one = (
        hidden_zero
        + jnp.dot(mixed_low, out_full, preferred_element_type=jnp.float32)
        + out_bias_full.astype(jnp.float32)
    )
    ffn_full = (
        lax.all_gather(ffn_set[0], ("dp", "fsdp"), axis=0, tiled=True),
        lax.all_gather(ffn_set[1], ("dp", "fsdp"), axis=0, tiled=True),
        lax.all_gather(ffn_set[2], ("dp", "fsdp"), axis=0, tiled=True),
        lax.all_gather(ffn_set[3], ("dp", "fsdp"), axis=0, tiled=True),
        lax.all_gather(ffn_set[4], ("dp", "fsdp"), axis=0, tiled=True),
        lax.all_gather(ffn_set[5], ("dp", "fsdp"), axis=0, tiled=True),
    )
    up_full, down_full, up_bias_full, down_bias_full, gain_two, shift_two = ffn_full
    normed_two, norm_two_pull = jax.vjp(
        layer_norm, hidden_one, gain_two.astype(jnp.float32), shift_two.astype(jnp.float32)
    )
    normed_two_low = normed_two.astype(jnp.bfloat16)
    up_pre = jnp.dot(
        normed_two_low, up_full, preferred_element_type=jnp.float32
    ) + up_bias_full.astype(jnp.float32)
    activated, gelu_pull = jax.vjp(gelu_exact, up_pre)
    activated_low = activated.astype(jnp.bfloat16)
    hidden_two = (
        hidden_one
        + jnp.dot(activated_low, down_full, preferred_element_type=jnp.float32)
        + down_bias_full.astype(jnp.float32)
    )
    output = hidden_two.astype(jnp.bfloat16)
    ffn_back = (
        lax.all_gather(ffn_set[0], ("dp", "fsdp"), axis=0, tiled=True),
        lax.all_gather(ffn_set[1], ("dp", "fsdp"), axis=0, tiled=True),
        lax.all_gather(ffn_set[2], ("dp", "fsdp"), axis=0, tiled=True),
        lax.all_gather(ffn_set[3], ("dp", "fsdp"), axis=0, tiled=True),
        lax.all_gather(ffn_set[4], ("dp", "fsdp"), axis=0, tiled=True),
        lax.all_gather(ffn_set[5], ("dp", "fsdp"), axis=0, tiled=True),
    )
    up_back, down_back = (ffn_back[0], ffn_back[1])
    grad_out = cotangent.astype(jnp.float32) * valid[:, None]
    grad_out_low = grad_out.astype(jnp.bfloat16)
    down_weight_term = jnp.einsum(
        "tf,td->fd", activated_low, grad_out_low, preferred_element_type=jnp.float32
    )
    down_bias_term = jnp.sum(grad_out, axis=0)
    down_sums = (
        lax.psum_scatter(down_weight_term, ("dp", "fsdp"), scatter_dimension=0, tiled=True),
        lax.psum_scatter(down_bias_term, ("dp", "fsdp"), scatter_dimension=0, tiled=True),
    )
    act_grad = jnp.einsum("td,fd->tf", grad_out_low, down_back, preferred_element_type=jnp.float32)
    up_grad = gelu_pull(act_grad)[0]
    up_grad_low = up_grad.astype(jnp.bfloat16)
    up_bias_term = jnp.sum(up_grad, axis=0)
    up_weight_term = jnp.einsum(
        "td,tf->df", normed_two_low, up_grad_low, preferred_element_type=jnp.float32
    )
    normed_two_grad = jnp.einsum(
        "tf,df->td", up_grad_low, up_back, preferred_element_type=jnp.float32
    )
    norm_two_input, gain_two_term, shift_two_term = norm_two_pull(normed_two_grad)
    hidden_one_grad = grad_out + norm_two_input
    up_sums = (
        lax.psum_scatter(up_weight_term, ("dp", "fsdp"), scatter_dimension=0, tiled=True),
        lax.psum_scatter(up_bias_term, ("dp", "fsdp"), scatter_dimension=0, tiled=True),
        lax.psum_scatter(gain_two_term, ("dp", "fsdp"), scatter_dimension=0, tiled=True),
        lax.psum_scatter(shift_two_term, ("dp", "fsdp"), scatter_dimension=0, tiled=True),
    )
    attn_back = (
        lax.all_gather(attn_set[0], ("dp", "fsdp"), axis=0, tiled=True),
        lax.all_gather(attn_set[1], ("dp", "fsdp"), axis=0, tiled=True),
        lax.all_gather(attn_set[2], ("dp", "fsdp"), axis=0, tiled=True),
        lax.all_gather(attn_set[3], ("dp", "fsdp"), axis=0, tiled=True),
        lax.all_gather(attn_set[4], ("dp", "fsdp"), axis=0, tiled=True),
        lax.all_gather(attn_set[5], ("dp", "fsdp"), axis=0, tiled=True),
        lax.all_gather(attn_set[6], ("dp", "fsdp"), axis=0, tiled=True),
    )
    query_back, key_back, value_back, out_back = (
        attn_back[0],
        attn_back[1],
        attn_back[2],
        attn_back[3],
    )
    attn_grad_low = hidden_one_grad.astype(jnp.bfloat16)
    out_bias_term = jnp.sum(hidden_one_grad, axis=0)
    out_weight_term = jnp.einsum(
        "tc,td->cd", mixed_low, attn_grad_low, preferred_element_type=jnp.float32
    )
    mixed_grad = jnp.einsum(
        "td,cd->tc", attn_grad_low, out_back, preferred_element_type=jnp.float32
    ).astype(jnp.bfloat16)
    mixed_grad_h = mixed_grad.reshape(rows_count, head_count, HEAD_DIM)
    probs_again = jnp.exp(attention_scores(query_h, key_h, related) - logsum)
    prob_grad = jnp.einsum(
        "qhd,khd->hqk", mixed_grad_h, value_h, preferred_element_type=jnp.float32
    )
    value_grad = jnp.einsum(
        "hqk,qhd->khd",
        probs_again.astype(jnp.bfloat16),
        mixed_grad_h,
        preferred_element_type=jnp.float32,
    )
    score_grad = probs_again * (
        prob_grad - jnp.sum(probs_again * prob_grad, axis=-1, keepdims=True)
    )
    score_low = score_grad.astype(jnp.bfloat16)
    query_grad = (
        jnp.einsum("hqk,khd->qhd", score_low, key_h, preferred_element_type=jnp.float32)
        * score_scale
    ).reshape(rows_count, model_width)
    key_grad = (
        jnp.einsum("hqk,qhd->khd", score_low, query_h, preferred_element_type=jnp.float32)
        * score_scale
    ).reshape(rows_count, model_width)
    value_grad = value_grad.reshape(rows_count, model_width)
    query_bias_term = jnp.sum(query_grad, axis=0)
    value_bias_term = jnp.sum(value_grad, axis=0)
    query_grad_low = query_grad.astype(jnp.bfloat16)
    key_grad_low = key_grad.astype(jnp.bfloat16)
    value_grad_low = value_grad.astype(jnp.bfloat16)
    query_weight_term = jnp.einsum(
        "tc,td->cd", normed_one_low, query_grad_low, preferred_element_type=jnp.float32
    )
    key_weight_term = jnp.einsum(
        "tc,td->cd", normed_one_low, key_grad_low, preferred_element_type=jnp.float32
    )
    value_weight_term = jnp.einsum(
        "tc,td->cd", normed_one_low, value_grad_low, preferred_element_type=jnp.float32
    )
    normed_one_grad = jnp.einsum(
        "td,cd->tc", query_grad_low, query_back, preferred_element_type=jnp.float32
    )
    normed_one_grad = normed_one_grad + jnp.einsum(
        "td,cd->tc", key_grad_low, key_back, preferred_element_type=jnp.float32
    )
    normed_one_grad = normed_one_grad + jnp.einsum(
        "td,cd->tc", value_grad_low, value_back, preferred_element_type=jnp.float32
    )
    norm_one_input, gain_one_term, shift_one_term = norm_one_pull(normed_one_grad)
    hidden_zero_grad = hidden_one_grad + norm_one_input
    conv_grad = conv_pull(hidden_zero_grad)[0]
    conv_bias_term = jnp.sum(conv_grad, axis=0)
    conv_grad_low = conv_grad.astype(jnp.bfloat16)
    attn_sums = (
        lax.psum_scatter(query_weight_term, ("dp", "fsdp"), scatter_dimension=0, tiled=True),
        lax.psum_scatter(key_weight_term, ("dp", "fsdp"), scatter_dimension=0, tiled=True),
        lax.psum_scatter(value_weight_term, ("dp", "fsdp"), scatter_dimension=0, tiled=True),
        lax.psum_scatter(out_weight_term, ("dp", "fsdp"), scatter_dimension=0, tiled=True),
        lax.psum_scatter(query_bias_term, ("dp", "fsdp"), scatter_dimension=0, tiled=True),
        lax.psum_scatter(value_bias_term, ("dp", "fsdp"), scatter_dimension=0, tiled=True),
        lax.psum_scatter(out_bias_term, ("dp", "fsdp"), scatter_dimension=0, tiled=True),
        lax.psum_scatter(conv_bias_term, ("dp", "fsdp"), scatter_dimension=0, tiled=True),
        lax.psum_scatter(gain_one_term, ("dp", "fsdp"), scatter_dimension=0, tiled=True),
        lax.psum_scatter(shift_one_term, ("dp", "fsdp"), scatter_dimension=0, tiled=True),
    )
    conv_back = (
        lax.all_gather(conv_set[0], ("dp", "fsdp"), axis=0, tiled=True),
        lax.all_gather(conv_set[1], ("dp", "fsdp"), axis=0, tiled=True),
        lax.all_gather(conv_set[2], ("dp", "fsdp"), axis=0, tiled=True),
        lax.all_gather(conv_set[3], ("dp", "fsdp"), axis=0, tiled=True),
    )
    kernel_pieces, frames_conv_grad = conv_backward(frames, segment, conv_back[0], conv_grad_low)
    kernel_halves = []
    for half_index in range(2):
        half_term = jnp.concatenate(kernel_pieces[half_index * 4 : (half_index + 1) * 4], axis=1)
        kernel_halves.append(sum_kernel_half(half_term))
    kernel_grad_out = jnp.concatenate(kernel_halves, axis=1)
    frames_grad = hidden_zero_grad + frames_conv_grad
    return (
        output,
        frames_grad,
        kernel_grad_out,
        attn_sums[7],
        attn_sums[8],
        attn_sums[9],
        attn_sums[0],
        attn_sums[4],
        attn_sums[1],
        attn_sums[2],
        attn_sums[5],
        attn_sums[3],
        attn_sums[6],
        up_sums[2],
        up_sums[3],
        up_sums[0],
        up_sums[1],
        down_sums[0],
        down_sums[1],
    )


NT = (((1,), (1,)), ((), ()))
TN = (((0,), (0,)), ((), ()))
BF, F32 = jnp.bfloat16, jnp.float32


def f32(v):
    return v.astype(jnp.float32)


def low(v):
    return v.astype(jnp.bfloat16)


def dot(a, b):
    return jnp.dot(a, b, preferred_element_type=jnp.float32)


def dot_nt(a, b):
    return lax.dot_general(a, b, NT, preferred_element_type=jnp.float32)


def dot_tn(a, b):
    return lax.dot_general(a, b, TN, preferred_element_type=jnp.float32)


SMEM = pl.BlockSpec(memory_space=pltpu.SMEM)
VMEM = pl.BlockSpec(memory_space=pltpu.VMEM)
ANY = pl.BlockSpec(memory_space=pl.ANY)
HBM = pl.BlockSpec(memory_space=pltpu.HBM)


def shape(dims, dtype=BF):
    return jax.ShapeDtypeStruct(dims, dtype)


def in_hbm(v):
    return pltpu.with_memory_space_constraint(v, pltpu.HBM)


def out_hbm(v):
    return pltpu.HBM(v.shape, v.dtype)


def estimate(cost):
    return pl.CostEstimate(flops=int(cost * 1e9), bytes_accessed=1 << 10, transcendentals=0)


def tie(v, *after):
    def body(*refs):
        pass

    return pl.pallas_call(
        body,
        in_specs=[ANY] * (1 + len(after)),
        out_specs=ANY,
        out_shape=shape(v.shape, v.dtype),
        input_output_aliases={0: 0},
        cost_estimate=estimate(0.1),
    )(v, *after)


def run_copies(plan, sems):
    copies = [pltpu.make_async_copy(a, b, sems.at[i]) for i, (a, b) in enumerate(plan)]
    for copy in copies:
        copy.start()
    for copy in copies:
        copy.wait()


def whole_call(kernel, ins, in_specs, outs, out_specs, scratch=(), cost=0.05, after=(), plan=None, vmem=12):
    many = isinstance(outs, (list, tuple))
    out_list, out_specs = (list(outs), list(out_specs)) if many else ([outs], [out_specs])
    staged_in = [i for i, sp in enumerate(in_specs) if sp is None]
    staged_out = [i for i, sp in enumerate(out_specs) if sp is None]
    stages = [pltpu.VMEM(ins[i].shape, ins[i].dtype) for i in staged_in]
    stages += [pltpu.VMEM(out_list[i].shape, out_list[i].dtype) for i in staged_out]
    n_in, n_out, n_stage = len(ins), len(out_list), len(stages)

    def body(*refs):
        given, made = list(refs[:n_in]), list(refs[n_in + len(after) : n_in + len(after) + n_out])
        rest = refs[n_in + len(after) + n_out :]
        stage, own, sems = rest[:n_stage], rest[n_stage:-1], rest[-1]
        first, last = [], []
        for ref, i in zip(stage, staged_in):
            first.append((given[i], ref))
            given[i] = ref
        for ref, i in zip(stage[len(staged_in) :], staged_out):
            last.append((ref, made[i]))
            made[i] = ref
        groups = plan(*given, *made, *own) if plan is not None else []
        copies = [pltpu.make_async_copy(a, b, sems.at[i]) for i, (a, b) in enumerate(first + sum(groups, []))]
        for copy in copies:
            copy.start()
        for copy in copies[: len(first)]:
            copy.wait()
        ends = [len(first) + sum(len(g) for g in groups[:i]) for i in range(len(groups) + 1)]

        def ready(group):
            for copy in copies[ends[group] : ends[group + 1]]:
                copy.wait()

        kernel(*given, *made, *own, *([ready] if groups else []))
        run_copies(last, sems)

    result = pl.pallas_call(
        body,
        in_specs=[HBM if sp is None else sp for sp in in_specs] + [ANY] * len(after),
        out_specs=[HBM if sp is None else sp for sp in out_specs],
        out_shape=[out_hbm(v) if sp is None else pltpu.VMEM(v.shape, v.dtype) if sp is VMEM else v for v, sp in zip(out_list, out_specs)],
        scratch_shapes=stages + list(scratch) + [pltpu.SemaphoreType.DMA((64,))],
        compiler_params=pltpu.CompilerParams(vmem_limit_bytes=vmem << 20),
        cost_estimate=estimate(cost),
    )(*[in_hbm(v) if sp is None or sp is ANY else v for v, sp in zip(ins, in_specs)], *after)
    return result if many else result[0]


def left(dims):
    return lax.broadcasted_iota(jnp.int32, dims, 1) < 64


def turn(v):
    return pltpu.roll(v, 64, 1)


def cross(a, b):
    lo = left(a.shape)
    return jnp.where(lo, a, turn(b)), jnp.where(lo, turn(a), b)


def pack_kernel(f_ref, s_ref, o_ref):
    small = low(s_ref[...])
    for g in range(8):
        tile = slice(128 * g, 128 * g + 128)
        p, q = cross(f32(f_ref[0:64, tile]), f32(f_ref[64:128, tile]))
        o_ref[2 * g, 0:64, :] = low(p)
        o_ref[2 * g + 1, 0:64, :] = low(q)
    for g in range(16):
        o_ref[g, 64:80, :] = small


def first_kernel(lens_ref, *refs):
    vectors, bias_ref = refs[0:9], refs[9]
    q_ref, k_ref, v_ref, o_ref, mine_ref, theirs_ref, out_ref, small_ref = refs[10:18]
    c = lax.axis_index("c")
    for j, ref in enumerate((q_ref, k_ref, v_ref)):
        for t in range(4):
            even, odd = cross(f32(ref[:, 256 * t : 256 * t + 128]), f32(ref[:, 256 * t + 128 : 256 * t + 256]))
            tile = slice(128 * t, 128 * t + 128)
            mine_ref[j, :, tile] = low(jnp.where(c == 0, even, odd))
            theirs_ref[j, :, tile] = low(jnp.where(c == 0, odd, even))
    for h in range(2):
        out_ref[h] = o_ref[:, 512 * h : 512 * h + 512]
    small_ref[...] = jnp.zeros_like(small_ref)
    for i, ref in enumerate(vectors):
        small_ref[i : i + 1, 0:32] = f32(ref[...]).reshape(1, 32)
    bias = f32(bias_ref[...]).reshape(1, 128)
    lane = lax.broadcasted_iota(jnp.int32, (1, 128), 1)
    for k in range(4):
        row = pltpu.roll(bias, 128 - 32 * k, 1) if k else bias
        small_ref[9 + k : 10 + k, :] = jnp.where(lane < 32, row, 0.0)
    small_ref[13:14, 0:4] = lens_ref[...].astype(jnp.float32)


def ffn_prep_kernel(lens_ref, u_ref, cot_ref, up_ref, g_ref, g_send_ref):
    valid = jnp.sum(lens_ref[...], axis=1, keepdims=True)
    for z in range(4):
        for k in range(8):
            at = 128 * (8 * z + k)
            up_ref[k, :, 128 * z : 128 * z + 128] = u_ref[:, at : at + 128]
    slot = lax.broadcasted_iota(jnp.int32, (128, 1024), 0)
    g_ref[...] = jnp.where(slot < valid, cot_ref[...], jnp.zeros_like(cot_ref))
    g_send_ref[...] = g_ref[...]


def vector_kernel(meta_ref, mine_ref, theirs_ref, vec_ref, up_ref, qv_ref):
    c, x = meta_ref[3], meta_ref[2]
    lane = lax.broadcasted_iota(jnp.int32, (16, 128), 1)
    tiles = []
    for t in range(8):
        tile = jnp.zeros((16, 128), jnp.float32)
        for k in range(4):
            part = jnp.where(x == k % 2, f32(mine_ref[2 * t + k // 2]), f32(theirs_ref[2 * t + k // 2]))
            tile = jnp.where(lane // 32 == k, pltpu.roll(part, 32 * k, 1) if k else part, tile)
        tiles.append(tile)
        vec_ref[:, 128 * t : 128 * t + 128] = tile
    for z in range(4):
        own = jnp.where(meta_ref[1] == 0, tiles[2 * z], tiles[2 * z + 1])
        own = jnp.where(c == 0, own, turn(own))
        own = jnp.where(x == 0, own, pltpu.roll(own, 96, 1))
        up = own[9:10, :]
        for k in range(1, 4):
            up = jnp.where(lane[0:1] // 32 == k, pltpu.roll(own[9 + k : 10 + k, :], 32 * k, 1), up)
        up_ref[0:1, 128 * z : 128 * z + 128] = up
    for t in range(4):
        even, odd = cross(tiles[2 * t], tiles[2 * t + 1])
        qv_ref[:, 128 * t : 128 * t + 128] = jnp.where(c == 0, even, odd)[3:5]


NB = 4
GROUP = 2
ROWS = 208


def starts_of(lens_ref, block):
    starts = [jnp.int32(0)]
    for i in range(4):
        starts.append(starts[-1] + lens_ref[block * 4 + i])
    return starts + [jnp.int32(128)]


def spread(block, starts, buf, out):
    v = f32(block)
    turned, lo = turn(v), left((64, 128))
    buf[80:144, :] = jnp.where(lo, v, turned)
    buf[144:208, :] = jnp.where(lo, turned, v)
    row = lax.broadcasted_iota(jnp.int32, (224, 128), 0)
    acc = jnp.zeros((224, 128), jnp.float32)
    for i in range(5):
        gap = 16 * (i + 1)
        keep = (row >= starts[i] + gap) & (row < starts[i + 1] + gap)
        acc = jnp.where(keep, buf[80 - gap : 304 - gap, :], acc)
    out[0:224, :] = acc


def fill_taps(spread_rows, wide, taps, b, shift):
    wide[0:224, :] = jnp.where(left((224, 128)), spread_rows[0:224, :], spread_rows[1:225, :])
    for p in range(8):
        off = 2 * p + shift
        taps[ROWS * b : ROWS * b + ROWS, 128 * p : 128 * p + 128] = low(wide[off : off + ROWS, :])


def fill_regions(starts, reg):
    row = lax.broadcasted_iota(jnp.int32, (336, 128), 0) - 64
    region = jnp.zeros((336, 128), jnp.int32)
    for i in range(1, 5):
        region = region + (row >= starts[i] + 16 * i).astype(jnp.int32)
    reg[...] = jnp.where((row >= 0) & (row < ROWS), region, -1)


def merge(y, b, reg, total, outs, starts):
    lo = left((224, 128))
    mine = jnp.where(lo, reg[64:288, :], reg[48:272, :])
    acc = jnp.zeros((224, 128), jnp.float32)
    for m in range(4):
        first = ROWS * b + 32 * m
        acc = acc + jnp.where(reg[32 * m : 32 * m + 224, :] == mine, y[first : first + 224, 128 * m : 128 * m + 128], 0.0)
    total[...] = acc
    part = total[0:ROWS, :] + turn(total[16 : ROWS + 16, :])
    outs[0:ROWS, :] = jnp.where(left((ROWS, 128)), part, turn(part))
    lo = left((64, 128))
    slot = lax.broadcasted_iota(jnp.int32, (64, 128), 0) + jnp.where(lo, 0, 64)
    packed = jnp.zeros((64, 128), jnp.float32)
    for i in range(5):
        gap = 16 * (i + 1)
        keep = (slot >= starts[i]) & (slot < starts[i + 1])
        packed = jnp.where(keep, jnp.where(lo, outs[gap : gap + 64, :], outs[gap + 64 : gap + 128, :]), packed)
    return low(packed)


def conv_body(lens_ref, src_ref, w, out_ref, scratch, shift):
    bufs, rows, wides, taps, regs, y, totals, outs = scratch
    blocks = [starts_of(lens_ref, pl.program_id(0) * NB + b) for b in range(NB)]
    for g in range(NB // GROUP):
        for b in range(GROUP * g, GROUP * g + GROUP):
            k = b % 2
            spread(src_ref[b, 0:64, :], blocks[b], bufs.at[k], rows.at[k])
            fill_taps(rows.at[k], wides.at[k], taps, b, shift)
        part = slice(ROWS * GROUP * g, ROWS * GROUP * (g + 1))
        y[64 + part.start : 64 + part.stop, :] = dot_nt(taps[part, :], w[...])
        if g > 0:
            merge_group(g - 1, blocks, y, regs, totals, outs, out_ref)
    merge_group(NB // GROUP - 1, blocks, y, regs, totals, outs, out_ref)


def merge_group(g, blocks, y, regs, totals, outs, out_ref):
    for b in range(GROUP * g, GROUP * g + GROUP):
        k = b % 2
        fill_regions(blocks[b], regs.at[k])
        out_ref[b] = merge(y, b, regs.at[k], totals.at[k], outs.at[k], blocks[b])


def conv_fwd_kernel(lens_ref, meta_ref, src_ref, own_ref, other_ref, out_ref, w, *scratch):
    @pl.when(pl.program_id(0) == 0)
    def _():
        x = meta_ref[2]
        for m in range(8):
            cols = slice(1024 * m, 1024 * m + 1024)
            w[pl.ds(pl.multiple_of(64 * m + 32 * x, 32), 32), :] = own_ref[:, cols]
            w[pl.ds(pl.multiple_of(64 * m + 32 * (1 - x), 32), 32), :] = other_ref[:, cols]

    conv_body(lens_ref, src_ref, w, out_ref, scratch, 0)


def conv_back_kernel(lens_ref, meta_ref, src_ref, own_ref, other_ref, out_ref, w, *scratch):
    @pl.when(pl.program_id(0) == 0)
    def _():
        x = meta_ref[2]
        for t in range(64):
            cols = slice(128 * t, 128 * t + 128)
            a, b = f32(own_ref[:, cols]), f32(other_ref[:, cols])
            pair = jnp.concatenate([jnp.where(x == 0, a, b), jnp.where(x == 0, b, a)], axis=0).T
            place = 127 - (2 * t + 1)
            m, j = place // 16, place % 16
            w[64 * m : 64 * m + 64, 64 * j : 64 * j + 64] = low(pair[64:128])
            w[64 * m : 64 * m + 64, 64 * j + 64 : 64 * j + 128] = low(pair[0:64])

    conv_body(lens_ref, src_ref, w, out_ref, scratch, 1)


def conv_grad_kernel(lens_ref, meta_ref, src_ref, g_ref, keep_ref, send_ref, acc, gt, buf, rows, wide, taps, reg, pair, regs):
    step = pl.program_id(0)
    for b in range(NB):
        starts = starts_of(lens_ref, step * NB + b)
        spread(src_ref[b, 0:64, :], starts, buf, rows)
        fill_taps(rows, wide, taps, b, 0)
        fill_regions(starts, reg)
        spread(g_ref[b, 0:64, :], starts, buf, rows.at[64:288])
        lo = left((320, 128))
        pair[16:336, :] = jnp.where(lo, rows[16:336, :], rows[0:320, :])
        regs[16:336, :] = jnp.where(lo, reg[16:336, :], reg[0:320, :])
        mine = reg[64 : 64 + ROWS, :]
        for m in range(4):
            first = 128 - 32 * m
            keep = regs[first : first + ROWS, :] == mine
            gt[ROWS * b : ROWS * b + ROWS, 128 * m : 128 * m + 128] = low(jnp.where(keep, pair[first : first + ROWS, :], 0.0))
    term = dot_tn(gt[...], taps[...])

    @pl.when(step == 0)
    def _():
        acc[...] = term

    @pl.when(step > 0)
    def _():
        acc[...] += term

    @pl.when(step == pl.num_programs(0) - 1)
    def _():
        x = meta_ref[2]
        for m in range(8):
            cols = slice(1024 * m, 1024 * m + 1024)
            keep_ref[:, cols] = acc[pl.ds(pl.multiple_of(64 * m + 32 * x, 32), 32), :]
            send_ref[:, cols] = low(acc[pl.ds(pl.multiple_of(64 * m + 32 * (1 - x), 32), 32), :])


def conv_call(kernel, lens, meta, arrays, outs, out_specs, scratch, after=(), cost=30):
    blocks = arrays[0].shape[0]
    in_specs = [
        pl.BlockSpec((NB, *a.shape[1:]), lambda i, l, m: (i, 0, 0)) if a.ndim == 3 else pl.BlockSpec(a.shape, lambda i, l, m: (0, 0))
        for a in arrays
    ]
    count = 2 + len(arrays)

    def body(*refs):
        kernel(*refs[:count], *refs[count + len(after) :])

    return pl.pallas_call(
        body,
        grid_spec=pltpu.PrefetchScalarGridSpec(
            num_scalar_prefetch=2, grid=(blocks // NB,), in_specs=in_specs + [ANY] * len(after), out_specs=out_specs, scratch_shapes=scratch
        ),
        out_shape=outs,
        compiler_params=pltpu.CompilerParams(vmem_limit_bytes=20 << 20),
        cost_estimate=estimate(cost),
    )(lens, meta, *[a if a.ndim == 3 else in_hbm(a) for a in arrays], *after)


def conv_pass(kernel, lens, meta, src, own, other, after=(), cost=30):
    scratch = [
        pltpu.VMEM((512, 1024), BF), pltpu.VMEM((2, 304, 128), F32), pltpu.VMEM((2, 232, 128), F32), pltpu.VMEM((2, 224, 128), F32),
        pltpu.VMEM((ROWS * NB, 1024), BF), pltpu.VMEM((2, 336, 128), jnp.int32), pltpu.VMEM((128 + ROWS * NB, 512), F32),
        pltpu.VMEM((2, 224, 128), F32), pltpu.VMEM((2, ROWS, 128), F32),
    ]
    spec = pl.BlockSpec((NB, 64, 128), lambda i, l, m: (i, 0, 0))
    return conv_call(kernel, lens, meta, (src, own, other), shape((src.shape[0], 64, 128)), spec, scratch, after, cost)


def conv_grads(lens, meta, src, grad, after=(), cost=30):
    scratch = [
        pltpu.VMEM((512, 1024), F32), pltpu.VMEM((ROWS * NB, 512), BF), pltpu.VMEM((304, 128), F32), pltpu.VMEM((336, 128), F32),
        pltpu.VMEM((224, 128), F32), pltpu.VMEM((ROWS * NB, 1024), BF), pltpu.VMEM((336, 128), jnp.int32), pltpu.VMEM((336, 128), F32),
        pltpu.VMEM((336, 128), jnp.int32),
    ]
    spec = pl.BlockSpec((32, 8192), lambda i, l, m: (0, 0))
    return conv_call(conv_grad_kernel, lens, meta, (src, grad), [out_hbm(shape((32, 8192), F32)), out_hbm(shape((32, 8192)))], [spec, spec], scratch, after, cost)


INV_SQRT2 = 0.7071067811865476
INV_SQRT_2PI = 0.3989422804014327


def gelu_cdf(v):
    return 0.5 + 0.5 * lax.erf(v * INV_SQRT2)


def gelu_slope(v, cdf):
    return cdf + v * (jnp.exp(-0.5 * v * v) * INV_SQRT_2PI)


def normed(v):
    centred = v - jnp.mean(v, axis=-1, keepdims=True)
    scale = lax.rsqrt(jnp.mean(centred * centred, axis=-1, keepdims=True) + norm_eps)
    return centred * scale, scale


def norm_pull(unit, scale, gain, grad):
    grad_unit = grad * gain
    mean_grad = jnp.mean(grad_unit, axis=-1, keepdims=True)
    mean_both = jnp.mean(grad_unit * unit, axis=-1, keepdims=True)
    return scale * (grad_unit - mean_grad - unit * mean_both)


def column_sum(v):
    return jnp.sum(v, axis=0, keepdims=True)


def norm_one_kernel(c_ref, f_ref, vec_ref, act_ref, zero_ref, zero_out_ref, n_ref):
    for g in range(8):
        tile = slice(128 * g, 128 * g + 128)
        a, b = cross(f32(c_ref[2 * g]), f32(c_ref[2 * g + 1]))
        act_ref[0:64, tile] = a + vec_ref[0:1, tile]
        act_ref[64:128, tile] = b + vec_ref[0:1, tile]
    for i in range(4):
        rows = slice(32 * i, 32 * i + 32)
        act = act_ref[rows, :]
        zero = f32(f_ref[rows, :]) + act * gelu_cdf(act)
        zero_ref[rows, :] = zero
        zero_out_ref[rows, :] = zero
        n_ref[rows, :] = low(normed(zero)[0] * vec_ref[1:2, :] + vec_ref[2:3, :])


def norm_two_kernel(zero_ref, keep_ref, got_ref, vec_ref, one_ref, n_ref):
    for i in range(4):
        rows = slice(32 * i, 32 * i + 32)
        one = zero_ref[rows, :] + vec_ref[5:6, :] + keep_ref[rows, :] + f32(got_ref[rows, :])
        one_ref[rows, :] = one
        n_ref[rows, :] = low(normed(one)[0] * vec_ref[6:7, :] + vec_ref[7:8, :])


def norm_two_back_kernel(keep_ref, got_ref, got_y_ref, got_d_ref, one_ref, g_ref, vec_ref, grad_ref, low_ref, sum_ref):
    sums = [jnp.zeros((1, 1024), jnp.float32) for _ in range(4)]
    for i in range(4):
        rows = slice(32 * i, 32 * i + 32)
        grad = keep_ref[rows, :] + f32(got_ref[rows, :]) + f32(got_y_ref[rows, :]) + f32(got_d_ref[rows, :])
        unit, scale = normed(one_ref[rows, :])
        out = f32(g_ref[rows, :])
        total = out + norm_pull(unit, scale, vec_ref[6:7, :], grad)
        grad_ref[rows, :] = total
        low_ref[rows, :] = low(total)
        for k, v in enumerate((total, grad * unit, grad, out)):
            sums[k] = sums[k] + column_sum(v)
    for k in range(4):
        sum_ref[k : k + 1, :] = sums[k]


def norm_one_back_kernel(meta_ref, keep_ref, got_ref, zero_ref, act_ref, one_grad_ref, vec_ref, two_ref, qv_ref, up_ref, grad_ref, pack_ref, conv):
    c, x = meta_ref[3], meta_ref[2]
    sums = [jnp.zeros((1, 1024), jnp.float32) for _ in range(3)]
    for i in range(4):
        rows = slice(32 * i, 32 * i + 32)
        grad = keep_ref[rows, :] + f32(got_ref[rows, :])
        unit, scale = normed(zero_ref[rows, :])
        total = one_grad_ref[rows, :] + norm_pull(unit, scale, vec_ref[1:2, :], grad)
        grad_ref[rows, :] = total
        act = act_ref[rows, :]
        conv_grad = total * gelu_slope(act, gelu_cdf(act))
        conv[rows, :] = conv_grad
        for k, v in enumerate((conv_grad, grad * unit, grad)):
            sums[k] = sums[k] + column_sum(v)
    lane = lax.broadcasted_iota(jnp.int32, (1, 128), 1)
    for g in range(8):
        tile = slice(128 * g, 128 * g + 128)
        p, q = cross(conv[0:64, tile], conv[64:128, tile])
        pack_ref[2 * g, 0:64, :] = low(p)
        pack_ref[2 * g + 1, 0:64, :] = low(q)
        source = qv_ref[0:2, 128 * (g // 2) : 128 * (g // 2) + 128]
        even = jnp.where(lane < 64, source, 0.0) if g % 2 == 0 else jnp.where(lane < 64, turn(source), 0.0)
        heads = jnp.where(c == 0, even, turn(even))
        up_rows = []
        for k in range(4):
            piece = up_ref[0:1, 128 * (g // 2) : 128 * (g // 2) + 128]
            piece = pltpu.roll(piece, (128 - 32 * k) % 128, 1) if k else piece
            piece = jnp.where(lane < 32, piece, 0.0)
            piece = jnp.where(x == 0, piece, pltpu.roll(piece, 32, 1))
            piece = jnp.where(c == 0, piece, turn(piece))
            up_rows.append(jnp.where(meta_ref[1] == g % 2, piece, 0.0))
        all_rows = [sums[0][:, tile], sums[1][:, tile], sums[2][:, tile], heads[0:1], heads[1:2], two_ref[0:1, tile],
                    two_ref[1:2, tile], two_ref[2:3, tile], two_ref[3:4, tile], *up_rows, jnp.zeros((3, 128), jnp.float32)]
        block = jnp.concatenate(all_rows, axis=0)
        pack_ref[2 * g, 64:80, :] = low(block)
        pack_ref[2 * g + 1, 64:80, :] = low(turn(block))


def final_kernel(c_ref, grad_ref, o_ref):
    for g in range(8):
        tile = slice(128 * g, 128 * g + 128)
        a, b = cross(f32(c_ref[2 * g]), f32(c_ref[2 * g + 1]))
        o_ref[0:64, tile] = grad_ref[0:64, tile] + a
        o_ref[64:128, tile] = grad_ref[64:128, tile] + b


def related(lens_ref, block):
    row = lax.broadcasted_iota(jnp.int32, (128, 128), 0)
    col = lax.broadcasted_iota(jnp.int32, (128, 128), 1)
    first = jnp.zeros((128, 128), jnp.int32)
    last = jnp.full((128, 128), 128, jnp.int32)
    e = 0
    for i in range(4):
        e = e + lens_ref[block * 4 + i]
        first = jnp.maximum(first, jnp.where(row >= e, e, 0))
        last = jnp.minimum(last, jnp.where(row < e, e, 128))
    return (col >= first) & (col < last)


def head_probs(query, key, rel, mine):
    masked_query = jnp.where(mine, query, jnp.zeros_like(query))
    scores = dot_nt(masked_query, key) * score_scale
    scores = jnp.where(rel, scores, -1000000000.0)
    top = jnp.max(scores, axis=-1, keepdims=True)
    expd = jnp.exp(scores - top)
    return expd / jnp.sum(expd, axis=-1, keepdims=True)


def attn_places(meta_ref, pieces, wqkv, wo):
    own, along_x, along_y, diag_a, diag_b = pieces
    y, x, c = meta_ref[1], meta_ref[2], meta_ref[3]
    groups = [[], [], [], []]
    every, low_z, high_z = slice(0, 4), slice(0, 2), slice(2, 4)
    for dy, dx, zs, src in (
        (0, 0, every, own), (0, 1, every, along_x), (1, 0, every, along_y), (1, 1, low_z, diag_a), (1, 1, high_z, diag_b)
    ):
        yy, xx = y ^ dy, x ^ dx
        for i in range(8):
            place = wqkv.at[i % 3, zs, yy, c ^ (i // 3), xx] if i < 6 else wo.at[i - 6, zs, yy, xx]
            groups[i % 3 if i < 6 else 3].append((src.at[:, i], place))
    return groups


def attn_scratch():
    return [pltpu.VMEM((3, 4, 2, 2, 2, 32, 512), BF), pltpu.VMEM((2, 4, 2, 2, 32, 512), BF)]


def attn_fwd_kernel(
    meta_ref, lens_ref, n_ref, n_other_ref, own, along_x, along_y, diag_a, diag_b, bias_ref,
    q_ref, k_ref, v_ref, m_ref, keep_ref, send_ref, wqkv, wo, ready,
):
    n = jnp.concatenate([n_ref[...], n_other_ref[...]], axis=0)
    ready(0)
    q_ref[...] = low(dot(n, wqkv[0].reshape(1024, 512)) + bias_ref[0:1, :])
    ready(1)
    k_ref[...] = low(dot(n, wqkv[1].reshape(1024, 512)))
    ready(2)
    v_ref[...] = low(dot(n, wqkv[2].reshape(1024, 512)) + bias_ref[1:2, :])
    half = lax.broadcasted_iota(jnp.int32, (128, 128), 1) // 64
    for b in range(2):
        rel = related(lens_ref, meta_ref[0] ^ b)
        for p in range(4):
            at = (slice(128 * b, 128 * b + 128), slice(128 * p, 128 * p + 128))
            query, key, value = q_ref[at], k_ref[at], v_ref[at]
            outs = [dot(low(head_probs(query, key, rel, half == h)), value) for h in range(2)]
            m_ref[at] = low(jnp.where(half == 0, outs[0], outs[1]))
    mixed = m_ref[...]
    ready(3)
    for h in range(2):
        out = dot(mixed, wo[h].reshape(512, 512))
        keep_ref[:, 512 * h : 512 * h + 512] = out[0:128]
        send_ref[:, 512 * h : 512 * h + 512] = low(out[128:256])


def attn_bwd_kernel(
    meta_ref, lens_ref, g_ref, g_other_ref, q_ref, k_ref, v_ref, own, along_x, along_y, diag_a, diag_b,
    dq_ref, dk_ref, dv_ref, sum_ref, keep_ref, send_ref, wqkv, wo, ready,
):
    grad_in = jnp.concatenate([g_ref[...], g_other_ref[...]], axis=0)
    ready(3)
    mixed_grad = low(dot_nt(grad_in[:, 0:512], wo[0].reshape(512, 512)) + dot_nt(grad_in[:, 512:1024], wo[1].reshape(512, 512)))
    half = lax.broadcasted_iota(jnp.int32, (128, 128), 1) // 64
    for p in range(4):
        sums = []
        for b in range(2):
            rel = related(lens_ref, meta_ref[0] ^ b)
            at = (slice(128 * b, 128 * b + 128), slice(128 * p, 128 * p + 128))
            query, key, value = q_ref[at], k_ref[at], v_ref[at]
            grad = mixed_grad[128 * b : 128 * b + 128, 128 * p : 128 * p + 128]
            dqs, dks, dvs = [], [], []
            for h in range(2):
                probs = head_probs(query, key, rel, half == h)
                grad_h = jnp.where(half == h, grad, jnp.zeros_like(grad))
                prob_grad = dot_nt(grad_h, value)
                dvs.append(dot_tn(low(probs), grad))
                score_grad = probs * (prob_grad - jnp.sum(probs * prob_grad, axis=-1, keepdims=True))
                score_low = low(score_grad)
                dqs.append(dot(score_low, key) * score_scale)
                dks.append(dot_tn(score_low, query) * score_scale)
            dq = jnp.where(half == 0, dqs[0], dqs[1])
            dk = jnp.where(half == 0, dks[0], dks[1])
            dv = jnp.where(half == 0, dvs[0], dvs[1])
            dq_ref[at], dk_ref[at], dv_ref[at] = low(dq), low(dk), low(dv)
            sums.append((column_sum(dq), column_sum(dv)))
        sum_ref[0:1, 128 * p : 128 * p + 128] = sums[0][0] + sums[1][0]
        sum_ref[1:2, 128 * p : 128 * p + 128] = sums[0][1] + sums[1][1]
    for j in range(3):
        ready(j)
    out = dot_nt(dq_ref[...], wqkv[0].reshape(1024, 512))
    out += dot_nt(dk_ref[...], wqkv[1].reshape(1024, 512))
    out += dot_nt(dv_ref[...], wqkv[2].reshape(1024, 512))
    keep_ref[...] = out[0:128]
    send_ref[...] = low(out[128:256])


def term_plan(meta_ref, own, send_x, send_y, keep_a, keep_b, gqkv, go):
    y, x, c = meta_ref[1], meta_ref[2], meta_ref[3]
    plan = []
    for dy, dx in ((0, 0), (0, 1), (1, 0), (1, 1)):
        yy, xx = y ^ dy, x ^ dx
        for i in range(8):
            if dy == 0 and dx == 0:
                part = own.at[:, i]
            elif i < 4:
                part = send_x.at[dy, :, i] if dx == 1 else keep_a.at[:, i]
            else:
                part = send_y.at[dx, :, i - 4] if dy == 1 else keep_b.at[:, i - 4]
            plan.append((gqkv.at[i % 3, :, yy, c ^ (i // 3), xx] if i < 6 else go.at[i - 6, :, yy, xx], part))
    return plan


def attn_term_kernel(meta_ref, n_ref, n_other_ref, dq_ref, dk_ref, dv_ref, m_ref, g_ref, g_other_ref, own, send_x, send_y, keep_a, keep_b, gqkv, go, sems):
    for z in range(4):
        cols = slice(256 * z, 256 * z + 256)
        n = jnp.concatenate([n_ref[:, cols], n_other_ref[:, cols]], axis=0)
        for j, ref in enumerate((dq_ref, dk_ref, dv_ref)):
            gqkv[j, z] = low(dot_tn(n, ref[...])).reshape(2, 2, 2, 32, 512)
    grad = jnp.concatenate([g_ref[...], g_other_ref[...]], axis=0)
    for z in range(4):
        term = low(dot_tn(m_ref[:, 128 * z : 128 * z + 128], grad))
        for h in range(2):
            go[h, z] = term[:, 512 * h : 512 * h + 512].reshape(2, 2, 32, 512)
    run_copies(term_plan(meta_ref, own, send_x, send_y, keep_a, keep_b, gqkv, go), sems)


def ffn_plan(both, wu, wd):
    return [[(both.at[:, 0:256], wu)], [(both.at[:, 256:384], wd.at[0]), (both.at[:, 384:512], wd.at[1])]]


def ffn_scratch():
    return [pltpu.VMEM((4, 256, 512), BF), pltpu.VMEM((2, 4, 128, 512), BF)]


def ffn_kernel(*refs):
    n_refs, g_refs, bias_ref = refs[0:8], refs[8:16], refs[17]
    act_ref, ug_ref, keep_ref, send_ref, sum_ref, wu, wd, ready = refs[18:26]
    ready(0)
    total = jnp.zeros((1, 512), jnp.float32)
    for i in (4, 5, 6, 7, 0, 1, 2, 3):
        rows = slice(128 * i, 128 * i + 128)
        up_pre = dot(n_refs[i][...], wu[...].reshape(1024, 512)) + bias_ref[...]
        cdf = gelu_cdf(up_pre)
        act_ref[rows, :] = low(up_pre * cdf)
        if i == 4:
            ready(1)
        act_grad = dot_nt(g_refs[i][:, 0:512], wd[0].reshape(512, 512)) + dot_nt(g_refs[i][:, 512:1024], wd[1].reshape(512, 512))
        up_grad = act_grad * gelu_slope(up_pre, cdf)
        total = total + column_sum(up_grad)
        ug_ref[rows, :] = low(up_grad)
        back = dot_nt(low(up_grad), wu[...].reshape(1024, 512))
        if i >= 4:
            send_ref[128 * i - 512 : 128 * i - 384, :] = low(back)
        else:
            keep_ref[rows, :] = back
    sum_ref[...] = total


def ffn_out_kernel(act_ref, both_ref, keep_ref, send_ref, wd, ready):
    ready(0)
    for h in range(2):
        cols = slice(512 * h, 512 * h + 512)
        keep_ref[:, cols] = dot(act_ref[0:512, :], wd[h].reshape(512, 512))
        send_ref[:, cols] = low(dot(act_ref[512:1024, :], wd[h].reshape(512, 512)))


def half_sum_kernel(keep_ref, got_ref, own_ref, x_ref, y_ref, across_ref):
    own_ref[...] = keep_ref[0:128, :] + f32(got_ref[0:128, :])
    for i, ref in enumerate((x_ref, y_ref, across_ref), 1):
        rows = slice(128 * i, 128 * i + 128)
        ref[...] = low(keep_ref[rows, :] + f32(got_ref[rows, :]))


def ffn_terms(act, grads, normeds, up_grad, after, cost=20):
    def body(*refs):
        act_ref, g_refs, n_refs, u_ref, out_ref = refs[0], refs[1:9], refs[9:17], refs[17], refs[-1]
        n = jnp.concatenate([ref[...] for ref in n_refs], axis=0)
        out_ref[0, 0:256] = low(dot_tn(n, u_ref[...]))
        g = jnp.concatenate([ref[...] for ref in g_refs], axis=0)
        down = low(dot_tn(act_ref[...], g))
        out_ref[0, 256:384] = down[:, 0:512]
        out_ref[0, 384:512] = down[:, 512:1024]

    rows = pl.BlockSpec((128, 1024), lambda i: (0, 0))
    part = pl.BlockSpec((128, 256), lambda i: (0, i))
    return pl.pallas_call(
        body,
        grid=(4,),
        in_specs=[pl.BlockSpec((1024, 128), lambda i: (0, i))] + [rows] * 8 + [part] * 8
        + [pl.BlockSpec((1024, 512), lambda i: (0, 0))] + [ANY] * len(after),
        out_specs=pl.BlockSpec((1, 512, 512), lambda i: (i, 0, 0)),
        out_shape=out_hbm(shape((4, 512, 512))),
        compiler_params=pltpu.CompilerParams(vmem_limit_bytes=20 << 20),
        cost_estimate=estimate(20),
    )(act, grads[0], *[in_hbm(v) for v in grads[1:]], normeds[0], *[in_hbm(v) for v in normeds[1:]], up_grad, *after)


def fold_call(keep_a, keep_b, got_x, got_y, after, cost=3):
    def body(a_ref, b_ref, x_ref, y_ref, *refs):
        refs[-2][...] = low(f32(a_ref[...]) + f32(x_ref[0]))
        refs[-1][...] = low(f32(b_ref[...]) + f32(y_ref[0]))

    part = pl.BlockSpec((2, 4, 32, 512), lambda i: (i, 0, 0, 0))
    second = pl.BlockSpec((1, 2, 4, 32, 512), lambda i: (1, i, 0, 0, 0))
    return pl.pallas_call(
        body,
        grid=(2,),
        in_specs=[part, part, second, second] + [ANY] * len(after),
        out_specs=[part, part],
        out_shape=[out_hbm(shape((4, 4, 32, 512)))] * 2,
        compiler_params=pltpu.CompilerParams(vmem_limit_bytes=16 << 20),
        cost_estimate=estimate(cost),
    )(in_hbm(keep_a), in_hbm(keep_b), in_hbm(got_x), in_hbm(got_y), *after)


def join_call(own, got_x, got_y, last_a, last_b, after, cost=3):
    def body(own_ref, x_ref, y_ref, a_ref, b_ref, *refs):
        refs[-1][:, 0:4] = low(f32(own_ref[:, 0:4]) + f32(x_ref[0]) + f32(a_ref[...]))
        refs[-1][:, 4:8] = low(f32(own_ref[:, 4:8]) + f32(y_ref[0]) + f32(b_ref[...]))

    full = pl.BlockSpec((2, 8, 32, 512), lambda i: (i, 0, 0, 0))
    part = pl.BlockSpec((2, 4, 32, 512), lambda i: (i, 0, 0, 0))
    first = pl.BlockSpec((1, 2, 4, 32, 512), lambda i: (0, i, 0, 0, 0))
    return pl.pallas_call(
        body,
        grid=(2,),
        in_specs=[full, first, first, part, part] + [ANY] * len(after),
        out_specs=full,
        out_shape=out_hbm(shape((4, 8, 32, 512))),
        compiler_params=pltpu.CompilerParams(vmem_limit_bytes=16 << 20),
        cost_estimate=estimate(cost),
    )(in_hbm(own), in_hbm(got_x), in_hbm(got_y), in_hbm(last_a), in_hbm(last_b), *after)


def output_kernel(one_ref, keep_ref, got_ref, got_y_ref, got_d_ref, vec_ref, o_ref):
    got = f32(got_ref[...]) + f32(got_y_ref[...]) + f32(got_d_ref[...])
    o_ref[...] = low(one_ref[...] + keep_ref[...] + got + vec_ref[8:9, :])


def up_grad_kernel(got_ref, sum_ref, up_ref, down_ref):
    for z in range(4):
        for k in range(8):
            at = 128 * (8 * z + k)
            up_ref[:, at : at + 128] = f32(got_ref[k, :, 128 * z : 128 * z + 128])
    down_ref[:, 0:512] = f32(sum_ref[256:384])
    down_ref[:, 512:1024] = f32(sum_ref[384:512])


def qkv_grad_kernel(meta_ref, sum_ref, got_ref, q_ref, k_ref, v_ref, o_ref):
    c = meta_ref[3]
    for j, ref in enumerate((q_ref, k_ref, v_ref)):
        for t in range(4):
            tile = slice(128 * t, 128 * t + 128)
            mine, theirs = f32(sum_ref[j, :, tile]), f32(got_ref[3 + j, :, tile])
            a, b = cross(jnp.where(c == 0, mine, theirs), jnp.where(c == 0, theirs, mine))
            ref[:, 256 * t : 256 * t + 128] = a
            ref[:, 256 * t + 128 : 256 * t + 256] = b
    for h in range(2):
        o_ref[:, 512 * h : 512 * h + 512] = f32(sum_ref[6 + h])


def swap(v, axis):
    return lax.ppermute(v, axis, [(0, 1), (1, 0)])


def swap_across(v):
    return lax.ppermute(v, ("y", "x"), [(i, 3 - i) for i in range(4)])


def gather_z(v):
    return lax.all_gather(v, "z", axis=0, tiled=False)


def scatter_z(v):
    return lax.psum_scatter(v, "z", scatter_dimension=0, tiled=False)


def pick(v, index, axis):
    return lax.dynamic_index_in_dim(v, index, axis, keepdims=False)


def local(
    frames, lengths, cotangent, conv_kernel, conv_bias, norm_one_gain, norm_one_bias,
    query_weight, query_bias, key_weight, value_weight, value_bias, out_weight, out_bias,
    norm_two_gain, norm_two_bias, up_weight, up_bias, down_weight, down_bias,
):
    zi, yi, ci, xi = (lax.axis_index(a) for a in ("z", "y", "c", "x"))
    meta = jnp.stack([(zi * 2 + yi) * 2 + ci, yi, xi, ci]).astype(jnp.int32)
    row, row_f, half = shape((128, 1024)), shape((128, 1024), F32), shape((256, 512))
    groups, plane = ("z", "y", "c"), ("y", "c", "x")

    def spread_plane(own, along_x, along_y, across):
        four = (own, along_x, along_y, across)
        return (*four, *(swap(v, "c") for v in four))

    def half_sum(keep, send, saved, cost, after):
        return whole_call(
            half_sum_kernel, (keep, swap(send, "c")), [saved, VMEM], [row_f, row, row, row], [saved] + [VMEM] * 3, cost=cost, after=after
        )

    vectors = (conv_bias, norm_one_gain, norm_one_bias, query_bias, value_bias, out_bias, norm_two_gain, norm_two_bias, down_bias, up_bias)
    qkv_mine, qkv_theirs, out_part, small = whole_call(
        first_kernel, (lengths, *vectors, query_weight, key_weight, value_weight, out_weight), [None] * 15,
        [shape((3, 32, 512)), shape((3, 32, 512)), shape((2, 32, 512)), shape((16, 128), F32)], [VMEM] * 4, cost=0.05, after=(),
    )
    attn_part = jnp.concatenate([qkv_mine, swap(qkv_theirs, "c"), out_part], axis=0)
    attn_own = gather_z(attn_part)

    up_split, grad_out, grad_send = whole_call(
        ffn_prep_kernel, (lengths, up_weight, cotangent), [None] * 3, [shape((8, 32, 512)), row, row], [VMEM] * 3, cost=0.05, after=(qkv_mine,)
    )
    grad_y = swap(grad_send, "y")
    up_part = lax.all_to_all(up_split, plane, 0, 0, tiled=True)

    payload = whole_call(pack_kernel, (frames, small), [None, VMEM], shape((16, 80, 128)), VMEM, cost=0.05, after=(in_hbm(attn_part), in_hbm(grad_y)))
    got = lax.all_to_all(payload, groups, 0, 0, tiled=True)
    kernel_other = swap(conv_kernel, "x")
    grad_x = swap(tie(grad_send, kernel_other), "x")
    lens = got[:, 77, 0:4].astype(jnp.int32).reshape(64)
    ffn_part = jnp.concatenate([up_part.reshape(256, 512), down_weight[:, :512], down_weight[:, 512:]], axis=0)
    ffn_both = gather_z(ffn_part)
    conv_out = conv_pass(conv_fwd_kernel, lens, meta, got, conv_kernel, kernel_other, cost=30, after=(in_hbm(attn_own), in_hbm(grad_x)))
    conv_got = lax.all_to_all(conv_out, groups, 0, 0, tiled=True)

    grad_d = swap_across(tie(grad_send, kernel_other))
    grads_out = spread_plane(grad_out, grad_x, grad_y, grad_d)
    attn_own = attn_own
    attn_x, attn_y = swap(attn_own, "x"), swap(attn_own, "y")
    diag_a, diag_b = swap(attn_x[0:2], "y"), swap(attn_y[2:4], "x")
    attn_pieces = (attn_own, attn_x, attn_y, diag_a, diag_b)

    got_small = got[:, 64:80]
    got_small_other = swap(got_small, "x")
    vec, up_bias_own, qv_bias = whole_call(
        vector_kernel, (meta, got_small, got_small_other), [SMEM, VMEM, VMEM],
        [shape((16, 1024), F32), shape((1, 512), F32), shape((2, 512), F32)], [VMEM] * 3, cost=3, after=(conv_out,),
    )
    conv_act, hidden_zero, zero_saved, n_one = whole_call(
        norm_one_kernel, (conv_got, frames, vec), [VMEM, None, VMEM], [row_f, row_f, row_f, row], [None, VMEM, None, VMEM],
        cost=1, after=(*(in_hbm(v) for v in grads_out[3:]), in_hbm(attn_x), in_hbm(attn_y)),
    )
    n_one_other = swap(n_one, "c")

    def attn_copies(first):
        return lambda *refs: attn_places(refs[0], refs[first : first + 5], refs[-2], refs[-1])

    query, key, value, mixed, attn_keep, attn_send = whole_call(
        attn_fwd_kernel, (meta, lens, n_one, n_one_other, *attn_pieces, qv_bias), [SMEM, SMEM, VMEM, VMEM] + [ANY] * 5 + [VMEM],
        [half] * 4 + [row_f, row], [None] * 4 + [VMEM] * 2, attn_scratch(), plan=attn_copies(4), vmem=16, cost=8, after=(),
    )
    hidden_one, n_two = whole_call(
        norm_two_kernel, (hidden_zero, attn_keep, swap(attn_send, "c"), vec), [VMEM] * 4, [row_f, row], [VMEM] * 2,
        cost=0.1, after=(in_hbm(ffn_both),),
    )

    n_twos = spread_plane(n_two, swap(n_two, "x"), swap(n_two, "y"), swap_across(n_two))
    many, many_f, many_half = shape((1024, 512)), shape((512, 1024), F32), shape((512, 1024))
    activated, up_grad, back_keep, back_send, up_bias_term = whole_call(
        ffn_kernel, (*n_twos, *grads_out, ffn_both, up_bias_own), ([VMEM] + [None] * 7) * 2 + [ANY, VMEM],
        [many, many, many_f, many_half, shape((1, 512), F32)], [VMEM] * 5, ffn_scratch(),
        plan=lambda *refs: ffn_plan(refs[16], refs[-2], refs[-1]), vmem=20, cost=30,
    )
    two_own, two_x, two_y, two_across = half_sum(back_keep, back_send, VMEM, 0.05, ())
    ffn_keep, ffn_send = whole_call(
        ffn_out_kernel, (activated, ffn_both), [None, ANY], [many_f, many_half], [None, None], ffn_scratch()[1:],
        plan=lambda *refs: ffn_plan(refs[1], None, refs[-1])[1:], cost=1, after=(two_x,),
    )
    two_got = (swap(two_x, "x"), swap(two_y, "y"), swap_across(two_across))
    ffn_term = ffn_terms(activated, grads_out, n_twos, up_grad, (two_x,), 20)
    one_grad, attn_grad, two_sums = whole_call(
        norm_two_back_kernel, (two_own, *two_got, hidden_one, grad_out, vec), [VMEM] * 7, [row_f, row, shape((4, 1024), F32)],
        [None, VMEM, None], cost=5, after=(in_hbm(ffn_term), in_hbm(ffn_send)),
    )
    attn_grad_other = swap(attn_grad, "c")
    ffn_sum = scatter_z(ffn_term)
    dq, dk, dv, qv_sum, one_keep, one_send = whole_call(
        attn_bwd_kernel, (meta, lens, attn_grad, attn_grad_other, query, key, value, *attn_pieces),
        [SMEM, SMEM, VMEM, VMEM] + [None] * 3 + [ANY] * 5, [half] * 3 + [shape((2, 512), F32), row_f, row], [VMEM] * 6, attn_scratch(),
        plan=attn_copies(7), vmem=16, cost=70, after=(),
    )
    zero_grad, payload_back = whole_call(
        norm_one_back_kernel, (meta, one_keep, swap(one_send, "c"), zero_saved, conv_act, one_grad, vec, two_sums, qv_sum, up_bias_term),
        [SMEM, VMEM, VMEM, None, None, None, VMEM, None, VMEM, VMEM], [row_f, shape((16, 80, 128))], [None, VMEM],
        [pltpu.VMEM((128, 1024), F32)], cost=10, after=(),
    )
    grad_got = lax.all_to_all(payload_back, groups, 0, 0, tiled=True)
    out_own, out_x, out_y, out_across = half_sum(ffn_keep, ffn_send, None, 0.05, (payload_back,))

    piece, part = out_hbm(shape((4, 8, 32, 512))), out_hbm(shape((4, 4, 32, 512)))
    pair = out_hbm(shape((2, 4, 4, 32, 512)))
    term_own, term_x, term_y, keep_a, keep_b = whole_call(
        attn_term_kernel, (meta, n_one, n_one_other, dq, dk, dv, mixed, attn_grad, attn_grad_other),
        [SMEM, VMEM, VMEM] + [None] * 4 + [VMEM] * 2, [piece, pair, pair, part, part], [HBM] * 5,
        attn_scratch() + [pltpu.SemaphoreType.DMA((32,))], vmem=16, cost=1, after=(payload_back,),
    )
    got_x, got_y = swap(term_x, "x"), swap(term_y, "y")
    conv_back_out = conv_pass(conv_back_kernel, lens, meta, grad_got, conv_kernel, kernel_other, cost=10, after=(out_x,))
    send_a, send_b = fold_call(keep_a, keep_b, got_x, got_y, (conv_back_out,), 3)
    back_got = lax.all_to_all(conv_back_out, groups, 0, 0, tiled=True)
    out_got = (swap(tie(out_x, send_b), "x"), swap(tie(out_y, send_b), "y"), swap_across(tie(out_across, send_b)))
    kernel_keep, kernel_send = conv_grads(lens, meta, got, grad_got, cost=30, after=(conv_back_out,))
    last_a, last_b = swap(send_a, "y"), swap(send_b, "x")
    attn_half = join_call(term_own, got_x, got_y, last_a, last_b, (in_hbm(kernel_send), back_got, in_hbm(ffn_sum)), 3)
    attn_sum = scatter_z(attn_half)

    frames_grad = whole_call(final_kernel, (back_got, zero_grad), [VMEM, None], row_f, None, cost=0.05, after=(in_hbm(attn_half),))
    output = whole_call(
        output_kernel, (hidden_one, out_own, *out_got, vec), [VMEM, None] + [VMEM] * 4, row, None, cost=0.05, after=(in_hbm(attn_half),)
    )
    kernel_grad = kernel_keep + f32(swap(kernel_send, "x"))
    ffn_sum = tie(ffn_sum, attn_half)
    up_got = lax.all_to_all(ffn_sum[0:256].reshape(8, 32, 512), plane, 0, 0, tiled=True)
    up_weight_grad, down_weight_grad = whole_call(
        up_grad_kernel, (up_got, ffn_sum), [VMEM, None], [shape((32, 4096), F32), shape((128, 1024), F32)], [None] * 2, cost=0.05
    )
    small_sum = jnp.sum(f32(grad_got[:, 64:80, 0:64]), axis=0).reshape(16, 2, 32)
    small_grad = pick(small_sum, xi, 1) + swap(tie(pick(small_sum, 1 - xi, 1), send_a), "x")
    small_grads = [small_grad[i] for i in range(9)]
    attn_sum = tie(attn_sum, output, up_weight_grad, kernel_grad, small_grad, frames_grad)
    query_weight_grad, key_weight_grad, value_weight_grad, out_weight_grad = whole_call(
        qkv_grad_kernel, (meta, attn_sum, swap(attn_sum, "c")), [SMEM, None, VMEM], [shape((32, 1024), F32)] * 4, [None] * 4
    )

    return (
        output, frames_grad, kernel_grad, small_grads[0], small_grads[1], small_grads[2], query_weight_grad, small_grads[3],
        key_weight_grad, value_weight_grad, small_grads[4], out_weight_grad, small_grads[5], small_grads[6], small_grads[7],
        up_weight_grad, small_grad[9:13].reshape(128), down_weight_grad, small_grads[8],
    )


MATRICES_IN = (0, 1, 2, 3, 7, 9, 10, 12, 16, 18)
MATRICES_OUT = (0, 1, 2, 6, 8, 9, 11, 15, 17)


def solution(mesh):
    n_dp, n_fsdp = mesh.shape["dp"], mesh.shape["fsdp"]
    if n_fsdp == 2 and n_dp == GROUPS:
        axes = ("z", "y", "c", "x")
        mesh = Mesh(mesh.devices.reshape(n_dp // 4, 2, 2, n_fsdp), axes)
        body = local
    else:
        axes = ("dp", "fsdp")
        body = local_plain
    in_specs = tuple(P(axes, None) if i in MATRICES_IN else P(axes) for i in range(20))
    out_specs = tuple(P(axes, None) if i in MATRICES_OUT else P(axes) for i in range(19))
    return jax.shard_map(body, mesh=mesh, in_specs=in_specs, out_specs=out_specs, check_vma=False)
```

```python
import functools

import jax
import jax.numpy as jnp
import numpy as np
from jax import lax
from jax.experimental import pallas as pl
from jax.experimental.pallas import tpu as pltpu
from jax.sharding import Mesh
from jax.sharding import PartitionSpec as P

HEAD_DIM = 64
GROUPS = 16
KW = 128


norm_eps = 1e-05
score_scale = 0.125


def layer_norm(rows, scale_vec, shift_vec):
    row_mean = jnp.mean(rows, axis=-1, keepdims=True)
    centred = rows - row_mean
    spread = jnp.mean(centred * centred, axis=-1, keepdims=True)
    return centred * lax.rsqrt(spread + norm_eps) * scale_vec + shift_vec


def gelu_exact(values):
    return jax.nn.gelu(values, approximate=False)


def unfold(source, segment, first_tap, tap_count, flipped):
    rows_count, model_width = source.shape
    half_width = KW // 2
    channels = model_width // GROUPS
    padded = jnp.pad(source, ((half_width, half_width), (0, 0))).reshape(
        rows_count + KW, GROUPS, channels
    )
    seg_padded = jnp.pad(segment, (half_width, half_width), constant_values=-1)
    offsets = [
        KW - tap_index if flipped else tap_index
        for tap_index in range(first_tap, first_tap + tap_count)
    ]
    shifted = jnp.stack([padded[offset : offset + rows_count] for offset in offsets], axis=2)
    same_seg = jnp.stack(
        [seg_padded[offset : offset + rows_count] == segment for offset in offsets], axis=1
    )
    kept_taps = jnp.where(same_seg[:, None, :, None], shifted, jnp.zeros((), source.dtype))
    return kept_taps.reshape(rows_count, GROUPS, tap_count * channels)


def conv_forward(source, segment, conv_kernel):
    rows_count, model_width = source.shape
    channels = model_width // GROUPS
    tap_count = KW // 8
    summed = jnp.zeros((rows_count, GROUPS, channels), jnp.float32)
    for block_index in range(8):
        first_tap = block_index * tap_count
        unfolded = unfold(source, segment, first_tap, tap_count, False)
        kernel_block = conv_kernel[:, first_tap * channels : (first_tap + tap_count) * channels]
        kernel_block = kernel_block.reshape(GROUPS, channels, tap_count * channels)
        summed = summed + jnp.einsum(
            "tgi,goi->tgo", unfolded, kernel_block, preferred_element_type=jnp.float32
        )
    return summed.reshape(rows_count, model_width)


def conv_backward(source, segment, conv_kernel, grad_low):
    rows_count, model_width = source.shape
    channels = model_width // GROUPS
    tap_count = KW // 8
    grad_groups = grad_low.reshape(rows_count, GROUPS, channels)
    kernel_pieces = []
    input_grad = jnp.zeros((rows_count, GROUPS, channels), jnp.float32)
    for block_index in range(8):
        first_tap = block_index * tap_count
        unfolded = unfold(source, segment, first_tap, tap_count, False)
        kernel_term = jnp.einsum(
            "tgo,tgi->goi", grad_groups, unfolded, preferred_element_type=jnp.float32
        )
        kernel_pieces.append(kernel_term.reshape(model_width, tap_count * channels))
        turned = unfold(grad_low, segment, first_tap, tap_count, True).reshape(
            rows_count, GROUPS, tap_count, channels
        )
        kernel_block = conv_kernel[:, first_tap * channels : (first_tap + tap_count) * channels]
        kernel_block = kernel_block.reshape(GROUPS, channels, tap_count, channels)
        input_grad = input_grad + jnp.einsum(
            "tgko,gokc->tgc", turned, kernel_block, preferred_element_type=jnp.float32
        )
    return (kernel_pieces, input_grad.reshape(rows_count, model_width))


def sum_kernel_half(piece):
    return lax.psum_scatter(piece, ("dp", "fsdp"), scatter_dimension=0, tiled=True)


def attention_scores(query_h, key_h, related):
    scores = (
        jnp.einsum("qhd,khd->hqk", query_h, key_h, preferred_element_type=jnp.float32) * score_scale
    )
    return jnp.where(related[None], scores, -1000000000.0)


def local_plain(
    frames,
    lengths,
    cotangent,
    conv_kernel,
    conv_bias,
    norm_one_gain,
    norm_one_bias,
    query_weight,
    query_bias,
    key_weight,
    value_weight,
    value_bias,
    out_weight,
    out_bias,
    norm_two_gain,
    norm_two_bias,
    up_weight,
    up_bias,
    down_weight,
    down_bias,
):
    rows_count, model_width = frames.shape
    head_count = model_width // HEAD_DIM
    ends = jnp.cumsum(lengths[0])
    positions = lax.broadcasted_iota(jnp.int32, (rows_count, ends.shape[0]), 0)
    segment = jnp.sum((positions >= ends[None, :]).astype(jnp.int32), axis=1)
    valid = (segment < ends.shape[0]).astype(jnp.float32)
    related = segment[:, None] == segment[None, :]
    conv_set = (conv_kernel, conv_bias, norm_one_gain, norm_one_bias)
    attn_set = (
        query_weight,
        key_weight,
        value_weight,
        out_weight,
        query_bias,
        value_bias,
        out_bias,
    )
    ffn_set = (up_weight, down_weight, up_bias, down_bias, norm_two_gain, norm_two_bias)
    source_f = frames.astype(jnp.float32)
    conv_full = (
        lax.all_gather(conv_set[0], ("dp", "fsdp"), axis=0, tiled=True),
        lax.all_gather(conv_set[1], ("dp", "fsdp"), axis=0, tiled=True),
        lax.all_gather(conv_set[2], ("dp", "fsdp"), axis=0, tiled=True),
        lax.all_gather(conv_set[3], ("dp", "fsdp"), axis=0, tiled=True),
    )
    kernel_full, conv_bias_full, gain_one, shift_one = conv_full
    conv_act = conv_forward(frames, segment, kernel_full) + conv_bias_full.astype(jnp.float32)
    conv_gelu, conv_pull = jax.vjp(gelu_exact, conv_act)
    hidden_zero = source_f + conv_gelu
    normed_one, norm_one_pull = jax.vjp(
        layer_norm, hidden_zero, gain_one.astype(jnp.float32), shift_one.astype(jnp.float32)
    )
    normed_one_low = normed_one.astype(jnp.bfloat16)
    attn_full = (
        lax.all_gather(attn_set[0], ("dp", "fsdp"), axis=0, tiled=True),
        lax.all_gather(attn_set[1], ("dp", "fsdp"), axis=0, tiled=True),
        lax.all_gather(attn_set[2], ("dp", "fsdp"), axis=0, tiled=True),
        lax.all_gather(attn_set[3], ("dp", "fsdp"), axis=0, tiled=True),
        lax.all_gather(attn_set[4], ("dp", "fsdp"), axis=0, tiled=True),
        lax.all_gather(attn_set[5], ("dp", "fsdp"), axis=0, tiled=True),
        lax.all_gather(attn_set[6], ("dp", "fsdp"), axis=0, tiled=True),
    )
    query_full, key_full, value_full, out_full, query_bias_full, value_bias_full, out_bias_full = (
        attn_full
    )
    query_low = (
        jnp.dot(normed_one_low, query_full, preferred_element_type=jnp.float32)
        + query_bias_full.astype(jnp.float32)
    ).astype(jnp.bfloat16)
    key_low = jnp.dot(normed_one_low, key_full, preferred_element_type=jnp.float32).astype(
        jnp.bfloat16
    )
    value_low = (
        jnp.dot(normed_one_low, value_full, preferred_element_type=jnp.float32)
        + value_bias_full.astype(jnp.float32)
    ).astype(jnp.bfloat16)
    query_h = query_low.reshape(rows_count, head_count, HEAD_DIM)
    key_h = key_low.reshape(rows_count, head_count, HEAD_DIM)
    value_h = value_low.reshape(rows_count, head_count, HEAD_DIM)
    scores = attention_scores(query_h, key_h, related)
    row_top = jnp.max(scores, axis=-1, keepdims=True)
    expd = jnp.exp(scores - row_top)
    row_total = jnp.sum(expd, axis=-1, keepdims=True)
    probs = expd / row_total
    logsum = row_top + jnp.log(row_total)
    mixed = jnp.einsum(
        "hqk,khd->qhd", probs.astype(jnp.bfloat16), value_h, preferred_element_type=jnp.float32
    )
    mixed_low = mixed.reshape(rows_count, model_width).astype(jnp.bfloat16)
    hidden_one = (
        hidden_zero
        + jnp.dot(mixed_low, out_full, preferred_element_type=jnp.float32)
        + out_bias_full.astype(jnp.float32)
    )
    ffn_full = (
        lax.all_gather(ffn_set[0], ("dp", "fsdp"), axis=0, tiled=True),
        lax.all_gather(ffn_set[1], ("dp", "fsdp"), axis=0, tiled=True),
        lax.all_gather(ffn_set[2], ("dp", "fsdp"), axis=0, tiled=True),
        lax.all_gather(ffn_set[3], ("dp", "fsdp"), axis=0, tiled=True),
        lax.all_gather(ffn_set[4], ("dp", "fsdp"), axis=0, tiled=True),
        lax.all_gather(ffn_set[5], ("dp", "fsdp"), axis=0, tiled=True),
    )
    up_full, down_full, up_bias_full, down_bias_full, gain_two, shift_two = ffn_full
    normed_two, norm_two_pull = jax.vjp(
        layer_norm, hidden_one, gain_two.astype(jnp.float32), shift_two.astype(jnp.float32)
    )
    normed_two_low = normed_two.astype(jnp.bfloat16)
    up_pre = jnp.dot(
        normed_two_low, up_full, preferred_element_type=jnp.float32
    ) + up_bias_full.astype(jnp.float32)
    activated, gelu_pull = jax.vjp(gelu_exact, up_pre)
    activated_low = activated.astype(jnp.bfloat16)
    hidden_two = (
        hidden_one
        + jnp.dot(activated_low, down_full, preferred_element_type=jnp.float32)
        + down_bias_full.astype(jnp.float32)
    )
    output = hidden_two.astype(jnp.bfloat16)
    ffn_back = (
        lax.all_gather(ffn_set[0], ("dp", "fsdp"), axis=0, tiled=True),
        lax.all_gather(ffn_set[1], ("dp", "fsdp"), axis=0, tiled=True),
        lax.all_gather(ffn_set[2], ("dp", "fsdp"), axis=0, tiled=True),
        lax.all_gather(ffn_set[3], ("dp", "fsdp"), axis=0, tiled=True),
        lax.all_gather(ffn_set[4], ("dp", "fsdp"), axis=0, tiled=True),
        lax.all_gather(ffn_set[5], ("dp", "fsdp"), axis=0, tiled=True),
    )
    up_back, down_back = (ffn_back[0], ffn_back[1])
    grad_out = cotangent.astype(jnp.float32) * valid[:, None]
    grad_out_low = grad_out.astype(jnp.bfloat16)
    down_weight_term = jnp.einsum(
        "tf,td->fd", activated_low, grad_out_low, preferred_element_type=jnp.float32
    )
    down_bias_term = jnp.sum(grad_out, axis=0)
    down_sums = (
        lax.psum_scatter(down_weight_term, ("dp", "fsdp"), scatter_dimension=0, tiled=True),
        lax.psum_scatter(down_bias_term, ("dp", "fsdp"), scatter_dimension=0, tiled=True),
    )
    act_grad = jnp.einsum("td,fd->tf", grad_out_low, down_back, preferred_element_type=jnp.float32)
    up_grad = gelu_pull(act_grad)[0]
    up_grad_low = up_grad.astype(jnp.bfloat16)
    up_bias_term = jnp.sum(up_grad, axis=0)
    up_weight_term = jnp.einsum(
        "td,tf->df", normed_two_low, up_grad_low, preferred_element_type=jnp.float32
    )
    normed_two_grad = jnp.einsum(
        "tf,df->td", up_grad_low, up_back, preferred_element_type=jnp.float32
    )
    norm_two_input, gain_two_term, shift_two_term = norm_two_pull(normed_two_grad)
    hidden_one_grad = grad_out + norm_two_input
    up_sums = (
        lax.psum_scatter(up_weight_term, ("dp", "fsdp"), scatter_dimension=0, tiled=True),
        lax.psum_scatter(up_bias_term, ("dp", "fsdp"), scatter_dimension=0, tiled=True),
        lax.psum_scatter(gain_two_term, ("dp", "fsdp"), scatter_dimension=0, tiled=True),
        lax.psum_scatter(shift_two_term, ("dp", "fsdp"), scatter_dimension=0, tiled=True),
    )
    attn_back = (
        lax.all_gather(attn_set[0], ("dp", "fsdp"), axis=0, tiled=True),
        lax.all_gather(attn_set[1], ("dp", "fsdp"), axis=0, tiled=True),
        lax.all_gather(attn_set[2], ("dp", "fsdp"), axis=0, tiled=True),
        lax.all_gather(attn_set[3], ("dp", "fsdp"), axis=0, tiled=True),
        lax.all_gather(attn_set[4], ("dp", "fsdp"), axis=0, tiled=True),
        lax.all_gather(attn_set[5], ("dp", "fsdp"), axis=0, tiled=True),
        lax.all_gather(attn_set[6], ("dp", "fsdp"), axis=0, tiled=True),
    )
    query_back, key_back, value_back, out_back = (
        attn_back[0],
        attn_back[1],
        attn_back[2],
        attn_back[3],
    )
    attn_grad_low = hidden_one_grad.astype(jnp.bfloat16)
    out_bias_term = jnp.sum(hidden_one_grad, axis=0)
    out_weight_term = jnp.einsum(
        "tc,td->cd", mixed_low, attn_grad_low, preferred_element_type=jnp.float32
    )
    mixed_grad = jnp.einsum(
        "td,cd->tc", attn_grad_low, out_back, preferred_element_type=jnp.float32
    ).astype(jnp.bfloat16)
    mixed_grad_h = mixed_grad.reshape(rows_count, head_count, HEAD_DIM)
    probs_again = jnp.exp(attention_scores(query_h, key_h, related) - logsum)
    prob_grad = jnp.einsum(
        "qhd,khd->hqk", mixed_grad_h, value_h, preferred_element_type=jnp.float32
    )
    value_grad = jnp.einsum(
        "hqk,qhd->khd",
        probs_again.astype(jnp.bfloat16),
        mixed_grad_h,
        preferred_element_type=jnp.float32,
    )
    score_grad = probs_again * (
        prob_grad - jnp.sum(probs_again * prob_grad, axis=-1, keepdims=True)
    )
    score_low = score_grad.astype(jnp.bfloat16)
    query_grad = (
        jnp.einsum("hqk,khd->qhd", score_low, key_h, preferred_element_type=jnp.float32)
        * score_scale
    ).reshape(rows_count, model_width)
    key_grad = (
        jnp.einsum("hqk,qhd->khd", score_low, query_h, preferred_element_type=jnp.float32)
        * score_scale
    ).reshape(rows_count, model_width)
    value_grad = value_grad.reshape(rows_count, model_width)
    query_bias_term = jnp.sum(query_grad, axis=0)
    value_bias_term = jnp.sum(value_grad, axis=0)
    query_grad_low = query_grad.astype(jnp.bfloat16)
    key_grad_low = key_grad.astype(jnp.bfloat16)
    value_grad_low = value_grad.astype(jnp.bfloat16)
    query_weight_term = jnp.einsum(
        "tc,td->cd", normed_one_low, query_grad_low, preferred_element_type=jnp.float32
    )
    key_weight_term = jnp.einsum(
        "tc,td->cd", normed_one_low, key_grad_low, preferred_element_type=jnp.float32
    )
    value_weight_term = jnp.einsum(
        "tc,td->cd", normed_one_low, value_grad_low, preferred_element_type=jnp.float32
    )
    normed_one_grad = jnp.einsum(
        "td,cd->tc", query_grad_low, query_back, preferred_element_type=jnp.float32
    )
    normed_one_grad = normed_one_grad + jnp.einsum(
        "td,cd->tc", key_grad_low, key_back, preferred_element_type=jnp.float32
    )
    normed_one_grad = normed_one_grad + jnp.einsum(
        "td,cd->tc", value_grad_low, value_back, preferred_element_type=jnp.float32
    )
    norm_one_input, gain_one_term, shift_one_term = norm_one_pull(normed_one_grad)
    hidden_zero_grad = hidden_one_grad + norm_one_input
    conv_grad = conv_pull(hidden_zero_grad)[0]
    conv_bias_term = jnp.sum(conv_grad, axis=0)
    conv_grad_low = conv_grad.astype(jnp.bfloat16)
    attn_sums = (
        lax.psum_scatter(query_weight_term, ("dp", "fsdp"), scatter_dimension=0, tiled=True),
        lax.psum_scatter(key_weight_term, ("dp", "fsdp"), scatter_dimension=0, tiled=True),
        lax.psum_scatter(value_weight_term, ("dp", "fsdp"), scatter_dimension=0, tiled=True),
        lax.psum_scatter(out_weight_term, ("dp", "fsdp"), scatter_dimension=0, tiled=True),
        lax.psum_scatter(query_bias_term, ("dp", "fsdp"), scatter_dimension=0, tiled=True),
        lax.psum_scatter(value_bias_term, ("dp", "fsdp"), scatter_dimension=0, tiled=True),
        lax.psum_scatter(out_bias_term, ("dp", "fsdp"), scatter_dimension=0, tiled=True),
        lax.psum_scatter(conv_bias_term, ("dp", "fsdp"), scatter_dimension=0, tiled=True),
        lax.psum_scatter(gain_one_term, ("dp", "fsdp"), scatter_dimension=0, tiled=True),
        lax.psum_scatter(shift_one_term, ("dp", "fsdp"), scatter_dimension=0, tiled=True),
    )
    conv_back = (
        lax.all_gather(conv_set[0], ("dp", "fsdp"), axis=0, tiled=True),
        lax.all_gather(conv_set[1], ("dp", "fsdp"), axis=0, tiled=True),
        lax.all_gather(conv_set[2], ("dp", "fsdp"), axis=0, tiled=True),
        lax.all_gather(conv_set[3], ("dp", "fsdp"), axis=0, tiled=True),
    )
    kernel_pieces, frames_conv_grad = conv_backward(frames, segment, conv_back[0], conv_grad_low)
    kernel_halves = []
    for half_index in range(2):
        half_term = jnp.concatenate(kernel_pieces[half_index * 4 : (half_index + 1) * 4], axis=1)
        kernel_halves.append(sum_kernel_half(half_term))
    kernel_grad_out = jnp.concatenate(kernel_halves, axis=1)
    frames_grad = hidden_zero_grad + frames_conv_grad
    return (
        output,
        frames_grad,
        kernel_grad_out,
        attn_sums[7],
        attn_sums[8],
        attn_sums[9],
        attn_sums[0],
        attn_sums[4],
        attn_sums[1],
        attn_sums[2],
        attn_sums[5],
        attn_sums[3],
        attn_sums[6],
        up_sums[2],
        up_sums[3],
        up_sums[0],
        up_sums[1],
        down_sums[0],
        down_sums[1],
    )


NT = (((1,), (1,)), ((), ()))
TN = (((0,), (0,)), ((), ()))
BF, F32 = jnp.bfloat16, jnp.float32


def f32(v):
    return v.astype(jnp.float32)


def low(v):
    return v.astype(jnp.bfloat16)


def dot(a, b):
    return jnp.dot(a, b, preferred_element_type=jnp.float32)


def dot_nt(a, b):
    return lax.dot_general(a, b, NT, preferred_element_type=jnp.float32)


def dot_tn(a, b):
    return lax.dot_general(a, b, TN, preferred_element_type=jnp.float32)


SMEM = pl.BlockSpec(memory_space=pltpu.SMEM)
VMEM = pl.BlockSpec(memory_space=pltpu.VMEM)
ANY = pl.BlockSpec(memory_space=pl.ANY)
HBM = pl.BlockSpec(memory_space=pltpu.HBM)


def shape(dims, dtype=BF):
    return jax.ShapeDtypeStruct(dims, dtype)


def in_hbm(v):
    return pltpu.with_memory_space_constraint(v, pltpu.HBM)


def out_hbm(v):
    return pltpu.HBM(v.shape, v.dtype)


def estimate(cost):
    return pl.CostEstimate(flops=int(cost * 1e9), bytes_accessed=1 << 10, transcendentals=0)


def tie(v, *after):
    def body(*refs):
        pass

    return pl.pallas_call(
        body,
        in_specs=[ANY] * (1 + len(after)),
        out_specs=ANY,
        out_shape=shape(v.shape, v.dtype),
        input_output_aliases={0: 0},
        cost_estimate=estimate(0.1),
    )(v, *after)


def run_copies(plan, sems):
    copies = [pltpu.make_async_copy(a, b, sems.at[i]) for i, (a, b) in enumerate(plan)]
    for copy in copies:
        copy.start()
    for copy in copies:
        copy.wait()


def whole_call(kernel, ins, in_specs, outs, out_specs, scratch=(), cost=0.05, after=(), plan=None, vmem=12):
    many = isinstance(outs, (list, tuple))
    out_list, out_specs = (list(outs), list(out_specs)) if many else ([outs], [out_specs])
    staged_in = [i for i, sp in enumerate(in_specs) if sp is None]
    staged_out = [i for i, sp in enumerate(out_specs) if sp is None]
    stages = [pltpu.VMEM(ins[i].shape, ins[i].dtype) for i in staged_in]
    stages += [pltpu.VMEM(out_list[i].shape, out_list[i].dtype) for i in staged_out]
    n_in, n_out, n_stage = len(ins), len(out_list), len(stages)

    def body(*refs):
        given, made = list(refs[:n_in]), list(refs[n_in + len(after) : n_in + len(after) + n_out])
        rest = refs[n_in + len(after) + n_out :]
        stage, own, sems = rest[:n_stage], rest[n_stage:-1], rest[-1]
        first, last = [], []
        for ref, i in zip(stage, staged_in):
            first.append((given[i], ref))
            given[i] = ref
        for ref, i in zip(stage[len(staged_in) :], staged_out):
            last.append((ref, made[i]))
            made[i] = ref
        groups = plan(*given, *made, *own) if plan is not None else []
        copies = [pltpu.make_async_copy(a, b, sems.at[i]) for i, (a, b) in enumerate(first + sum(groups, []))]
        for copy in copies:
            copy.start()
        for copy in copies[: len(first)]:
            copy.wait()
        ends = [len(first) + sum(len(g) for g in groups[:i]) for i in range(len(groups) + 1)]

        def ready(group):
            for copy in copies[ends[group] : ends[group + 1]]:
                copy.wait()

        kernel(*given, *made, *own, *([ready] if groups else []))
        run_copies(last, sems)

    result = pl.pallas_call(
        body,
        in_specs=[HBM if sp is None else sp for sp in in_specs] + [ANY] * len(after),
        out_specs=[HBM if sp is None else sp for sp in out_specs],
        out_shape=[out_hbm(v) if sp is None else pltpu.VMEM(v.shape, v.dtype) if sp is VMEM else v for v, sp in zip(out_list, out_specs)],
        scratch_shapes=stages + list(scratch) + [pltpu.SemaphoreType.DMA((64,))],
        compiler_params=pltpu.CompilerParams(vmem_limit_bytes=vmem << 20),
        cost_estimate=estimate(cost),
    )(*[in_hbm(v) if sp is None or sp is ANY else v for v, sp in zip(ins, in_specs)], *after)
    return result if many else result[0]


def left(dims):
    return lax.broadcasted_iota(jnp.int32, dims, 1) < 64


def turn(v):
    return pltpu.roll(v, 64, 1)


def cross(a, b):
    lo = left(a.shape)
    return jnp.where(lo, a, turn(b)), jnp.where(lo, turn(a), b)


def pack_kernel(f_ref, s_ref, o_ref):
    small = low(s_ref[...])
    for g in range(8):
        tile = slice(128 * g, 128 * g + 128)
        p, q = cross(f32(f_ref[0:64, tile]), f32(f_ref[64:128, tile]))
        o_ref[2 * g, 0:64, :] = low(p)
        o_ref[2 * g + 1, 0:64, :] = low(q)
    for g in range(16):
        o_ref[g, 64:80, :] = small


def first_kernel(lens_ref, *refs):
    vectors, bias_ref = refs[0:9], refs[9]
    q_ref, k_ref, v_ref, o_ref, mine_ref, theirs_ref, out_ref, small_ref = refs[10:18]
    c = lax.axis_index("c")
    for j, ref in enumerate((q_ref, k_ref, v_ref)):
        for t in range(4):
            even, odd = cross(f32(ref[:, 256 * t : 256 * t + 128]), f32(ref[:, 256 * t + 128 : 256 * t + 256]))
            tile = slice(128 * t, 128 * t + 128)
            mine_ref[j, :, tile] = low(jnp.where(c == 0, even, odd))
            theirs_ref[j, :, tile] = low(jnp.where(c == 0, odd, even))
    for h in range(2):
        out_ref[h] = o_ref[:, 512 * h : 512 * h + 512]
    small_ref[...] = jnp.zeros_like(small_ref)
    for i, ref in enumerate(vectors):
        small_ref[i : i + 1, 0:32] = f32(ref[...]).reshape(1, 32)
    bias = f32(bias_ref[...]).reshape(1, 128)
    lane = lax.broadcasted_iota(jnp.int32, (1, 128), 1)
    for k in range(4):
        row = pltpu.roll(bias, 128 - 32 * k, 1) if k else bias
        small_ref[9 + k : 10 + k, :] = jnp.where(lane < 32, row, 0.0)
    small_ref[13:14, 0:4] = lens_ref[...].astype(jnp.float32)


def ffn_prep_kernel(lens_ref, u_ref, cot_ref, up_ref, g_ref, g_send_ref):
    valid = jnp.sum(lens_ref[...], axis=1, keepdims=True)
    for z in range(4):
        for k in range(8):
            at = 128 * (8 * z + k)
            up_ref[k, :, 128 * z : 128 * z + 128] = u_ref[:, at : at + 128]
    slot = lax.broadcasted_iota(jnp.int32, (128, 1024), 0)
    g_ref[...] = jnp.where(slot < valid, cot_ref[...], jnp.zeros_like(cot_ref))
    g_send_ref[...] = g_ref[...]


def vector_kernel(meta_ref, mine_ref, theirs_ref, vec_ref, up_ref, qv_ref):
    c, x = meta_ref[3], meta_ref[2]
    lane = lax.broadcasted_iota(jnp.int32, (16, 128), 1)
    tiles = []
    for t in range(8):
        tile = jnp.zeros((16, 128), jnp.float32)
        for k in range(4):
            part = jnp.where(x == k % 2, f32(mine_ref[2 * t + k // 2]), f32(theirs_ref[2 * t + k // 2]))
            tile = jnp.where(lane // 32 == k, pltpu.roll(part, 32 * k, 1) if k else part, tile)
        tiles.append(tile)
        vec_ref[:, 128 * t : 128 * t + 128] = tile
    for z in range(4):
        own = jnp.where(meta_ref[1] == 0, tiles[2 * z], tiles[2 * z + 1])
        own = jnp.where(c == 0, own, turn(own))
        own = jnp.where(x == 0, own, pltpu.roll(own, 96, 1))
        up = own[9:10, :]
        for k in range(1, 4):
            up = jnp.where(lane[0:1] // 32 == k, pltpu.roll(own[9 + k : 10 + k, :], 32 * k, 1), up)
        up_ref[0:1, 128 * z : 128 * z + 128] = up
    for t in range(4):
        even, odd = cross(tiles[2 * t], tiles[2 * t + 1])
        qv_ref[:, 128 * t : 128 * t + 128] = jnp.where(c == 0, even, odd)[3:5]


NB = 4
GROUP = 2
ROWS = 208


def starts_of(lens_ref, block):
    starts = [jnp.int32(0)]
    for i in range(4):
        starts.append(starts[-1] + lens_ref[block * 4 + i])
    return starts + [jnp.int32(128)]


def spread(block, starts, buf, out):
    v = f32(block)
    turned, lo = turn(v), left((64, 128))
    buf[80:144, :] = jnp.where(lo, v, turned)
    buf[144:208, :] = jnp.where(lo, turned, v)
    row = lax.broadcasted_iota(jnp.int32, (224, 128), 0)
    acc = jnp.zeros((224, 128), jnp.float32)
    for i in range(5):
        gap = 16 * (i + 1)
        keep = (row >= starts[i] + gap) & (row < starts[i + 1] + gap)
        acc = jnp.where(keep, buf[80 - gap : 304 - gap, :], acc)
    out[0:224, :] = acc


def fill_taps(spread_rows, wide, taps, b, shift):
    wide[0:224, :] = jnp.where(left((224, 128)), spread_rows[0:224, :], spread_rows[1:225, :])
    for p in range(8):
        off = 2 * p + shift
        taps[ROWS * b : ROWS * b + ROWS, 128 * p : 128 * p + 128] = low(wide[off : off + ROWS, :])


def fill_regions(starts, reg):
    row = lax.broadcasted_iota(jnp.int32, (336, 128), 0) - 64
    region = jnp.zeros((336, 128), jnp.int32)
    for i in range(1, 5):
        region = region + (row >= starts[i] + 16 * i).astype(jnp.int32)
    reg[...] = jnp.where((row >= 0) & (row < ROWS), region, -1)


def merge(y, b, reg, total, outs, starts):
    lo = left((224, 128))
    mine = jnp.where(lo, reg[64:288, :], reg[48:272, :])
    acc = jnp.zeros((224, 128), jnp.float32)
    for m in range(4):
        first = ROWS * b + 32 * m
        acc = acc + jnp.where(reg[32 * m : 32 * m + 224, :] == mine, y[first : first + 224, 128 * m : 128 * m + 128], 0.0)
    total[...] = acc
    part = total[0:ROWS, :] + turn(total[16 : ROWS + 16, :])
    outs[0:ROWS, :] = jnp.where(left((ROWS, 128)), part, turn(part))
    lo = left((64, 128))
    slot = lax.broadcasted_iota(jnp.int32, (64, 128), 0) + jnp.where(lo, 0, 64)
    packed = jnp.zeros((64, 128), jnp.float32)
    for i in range(5):
        gap = 16 * (i + 1)
        keep = (slot >= starts[i]) & (slot < starts[i + 1])
        packed = jnp.where(keep, jnp.where(lo, outs[gap : gap + 64, :], outs[gap + 64 : gap + 128, :]), packed)
    return low(packed)


def conv_body(lens_ref, src_ref, w, out_ref, scratch, shift):
    bufs, rows, wides, taps, regs, y, totals, outs = scratch
    blocks = [starts_of(lens_ref, pl.program_id(0) * NB + b) for b in range(NB)]
    for g in range(NB // GROUP):
        for b in range(GROUP * g, GROUP * g + GROUP):
            k = b % 2
            spread(src_ref[b, 0:64, :], blocks[b], bufs.at[k], rows.at[k])
            fill_taps(rows.at[k], wides.at[k], taps, b, shift)
        part = slice(ROWS * GROUP * g, ROWS * GROUP * (g + 1))
        y[64 + part.start : 64 + part.stop, :] = dot_nt(taps[part, :], w[...])
        if g > 0:
            merge_group(g - 1, blocks, y, regs, totals, outs, out_ref)
    merge_group(NB // GROUP - 1, blocks, y, regs, totals, outs, out_ref)


def merge_group(g, blocks, y, regs, totals, outs, out_ref):
    for b in range(GROUP * g, GROUP * g + GROUP):
        k = b % 2
        fill_regions(blocks[b], regs.at[k])
        out_ref[b] = merge(y, b, regs.at[k], totals.at[k], outs.at[k], blocks[b])


def conv_fwd_kernel(lens_ref, meta_ref, src_ref, own_ref, other_ref, out_ref, w, *scratch):
    @pl.when(pl.program_id(0) == 0)
    def _():
        x = meta_ref[2]
        for m in range(8):
            cols = slice(1024 * m, 1024 * m + 1024)
            w[pl.ds(pl.multiple_of(64 * m + 32 * x, 32), 32), :] = own_ref[:, cols]
            w[pl.ds(pl.multiple_of(64 * m + 32 * (1 - x), 32), 32), :] = other_ref[:, cols]

    conv_body(lens_ref, src_ref, w, out_ref, scratch, 0)


def conv_back_kernel(lens_ref, meta_ref, src_ref, own_ref, other_ref, out_ref, w, *scratch):
    @pl.when(pl.program_id(0) == 0)
    def _():
        x = meta_ref[2]
        for t in range(64):
            cols = slice(128 * t, 128 * t + 128)
            a, b = f32(own_ref[:, cols]), f32(other_ref[:, cols])
            pair = jnp.concatenate([jnp.where(x == 0, a, b), jnp.where(x == 0, b, a)], axis=0).T
            place = 127 - (2 * t + 1)
            m, j = place // 16, place % 16
            w[64 * m : 64 * m + 64, 64 * j : 64 * j + 64] = low(pair[64:128])
            w[64 * m : 64 * m + 64, 64 * j + 64 : 64 * j + 128] = low(pair[0:64])

    conv_body(lens_ref, src_ref, w, out_ref, scratch, 1)


def conv_grad_kernel(lens_ref, meta_ref, src_ref, g_ref, keep_ref, send_ref, acc, gt, buf, rows, wide, taps, reg, pair, regs):
    step = pl.program_id(0)
    for b in range(NB):
        starts = starts_of(lens_ref, step * NB + b)
        spread(src_ref[b, 0:64, :], starts, buf, rows)
        fill_taps(rows, wide, taps, b, 0)
        fill_regions(starts, reg)
        spread(g_ref[b, 0:64, :], starts, buf, rows.at[64:288])
        lo = left((320, 128))
        pair[16:336, :] = jnp.where(lo, rows[16:336, :], rows[0:320, :])
        regs[16:336, :] = jnp.where(lo, reg[16:336, :], reg[0:320, :])
        mine = reg[64 : 64 + ROWS, :]
        for m in range(4):
            first = 128 - 32 * m
            keep = regs[first : first + ROWS, :] == mine
            gt[ROWS * b : ROWS * b + ROWS, 128 * m : 128 * m + 128] = low(jnp.where(keep, pair[first : first + ROWS, :], 0.0))
    term = dot_tn(gt[...], taps[...])

    @pl.when(step == 0)
    def _():
        acc[...] = term

    @pl.when(step > 0)
    def _():
        acc[...] += term

    @pl.when(step == pl.num_programs(0) - 1)
    def _():
        x = meta_ref[2]
        for m in range(8):
            cols = slice(1024 * m, 1024 * m + 1024)
            keep_ref[:, cols] = acc[pl.ds(pl.multiple_of(64 * m + 32 * x, 32), 32), :]
            send_ref[:, cols] = low(acc[pl.ds(pl.multiple_of(64 * m + 32 * (1 - x), 32), 32), :])


def conv_call(kernel, lens, meta, arrays, outs, out_specs, scratch, after=(), cost=30):
    blocks = arrays[0].shape[0]
    in_specs = [
        pl.BlockSpec((NB, *a.shape[1:]), lambda i, l, m: (i, 0, 0)) if a.ndim == 3 else pl.BlockSpec(a.shape, lambda i, l, m: (0, 0))
        for a in arrays
    ]
    count = 2 + len(arrays)

    def body(*refs):
        kernel(*refs[:count], *refs[count + len(after) :])

    return pl.pallas_call(
        body,
        grid_spec=pltpu.PrefetchScalarGridSpec(
            num_scalar_prefetch=2, grid=(blocks // NB,), in_specs=in_specs + [ANY] * len(after), out_specs=out_specs, scratch_shapes=scratch
        ),
        out_shape=outs,
        compiler_params=pltpu.CompilerParams(vmem_limit_bytes=20 << 20),
        cost_estimate=estimate(cost),
    )(lens, meta, *[a if a.ndim == 3 else in_hbm(a) for a in arrays], *after)


def conv_pass(kernel, lens, meta, src, own, other, after=(), cost=30):
    scratch = [
        pltpu.VMEM((512, 1024), BF), pltpu.VMEM((2, 304, 128), F32), pltpu.VMEM((2, 232, 128), F32), pltpu.VMEM((2, 224, 128), F32),
        pltpu.VMEM((ROWS * NB, 1024), BF), pltpu.VMEM((2, 336, 128), jnp.int32), pltpu.VMEM((128 + ROWS * NB, 512), F32),
        pltpu.VMEM((2, 224, 128), F32), pltpu.VMEM((2, ROWS, 128), F32),
    ]
    spec = pl.BlockSpec((NB, 64, 128), lambda i, l, m: (i, 0, 0))
    return conv_call(kernel, lens, meta, (src, own, other), shape((src.shape[0], 64, 128)), spec, scratch, after, cost)


def conv_grads(lens, meta, src, grad, after=(), cost=30):
    scratch = [
        pltpu.VMEM((512, 1024), F32), pltpu.VMEM((ROWS * NB, 512), BF), pltpu.VMEM((304, 128), F32), pltpu.VMEM((336, 128), F32),
        pltpu.VMEM((224, 128), F32), pltpu.VMEM((ROWS * NB, 1024), BF), pltpu.VMEM((336, 128), jnp.int32), pltpu.VMEM((336, 128), F32),
        pltpu.VMEM((336, 128), jnp.int32),
    ]
    spec = pl.BlockSpec((32, 8192), lambda i, l, m: (0, 0))
    return conv_call(conv_grad_kernel, lens, meta, (src, grad), [out_hbm(shape((32, 8192), F32)), out_hbm(shape((32, 8192)))], [spec, spec], scratch, after, cost)


INV_SQRT2 = 0.7071067811865476
INV_SQRT_2PI = 0.3989422804014327


def gelu_cdf(v):
    return 0.5 + 0.5 * lax.erf(v * INV_SQRT2)


def gelu_slope(v, cdf):
    return cdf + v * (jnp.exp(-0.5 * v * v) * INV_SQRT_2PI)


def normed(v):
    centred = v - jnp.mean(v, axis=-1, keepdims=True)
    scale = lax.rsqrt(jnp.mean(centred * centred, axis=-1, keepdims=True) + norm_eps)
    return centred * scale, scale


def norm_pull(unit, scale, gain, grad):
    grad_unit = grad * gain
    mean_grad = jnp.mean(grad_unit, axis=-1, keepdims=True)
    mean_both = jnp.mean(grad_unit * unit, axis=-1, keepdims=True)
    return scale * (grad_unit - mean_grad - unit * mean_both)


def column_sum(v):
    return jnp.sum(v, axis=0, keepdims=True)


def norm_one_kernel(c_ref, f_ref, vec_ref, act_ref, zero_ref, zero_out_ref, n_ref):
    for g in range(8):
        tile = slice(128 * g, 128 * g + 128)
        a, b = cross(f32(c_ref[2 * g]), f32(c_ref[2 * g + 1]))
        act_ref[0:64, tile] = a + vec_ref[0:1, tile]
        act_ref[64:128, tile] = b + vec_ref[0:1, tile]
    for i in range(4):
        rows = slice(32 * i, 32 * i + 32)
        act = act_ref[rows, :]
        zero = f32(f_ref[rows, :]) + act * gelu_cdf(act)
        zero_ref[rows, :] = zero
        zero_out_ref[rows, :] = zero
        n_ref[rows, :] = low(normed(zero)[0] * vec_ref[1:2, :] + vec_ref[2:3, :])


def norm_two_kernel(zero_ref, keep_ref, got_ref, vec_ref, one_ref, n_ref):
    for i in range(4):
        rows = slice(32 * i, 32 * i + 32)
        one = zero_ref[rows, :] + vec_ref[5:6, :] + keep_ref[rows, :] + f32(got_ref[rows, :])
        one_ref[rows, :] = one
        n_ref[rows, :] = low(normed(one)[0] * vec_ref[6:7, :] + vec_ref[7:8, :])


def norm_two_back_kernel(keep_ref, got_ref, got_y_ref, got_d_ref, one_ref, g_ref, vec_ref, grad_ref, low_ref, sum_ref):
    sums = [jnp.zeros((1, 1024), jnp.float32) for _ in range(4)]
    for i in range(4):
        rows = slice(32 * i, 32 * i + 32)
        grad = keep_ref[rows, :] + f32(got_ref[rows, :]) + f32(got_y_ref[rows, :]) + f32(got_d_ref[rows, :])
        unit, scale = normed(one_ref[rows, :])
        out = f32(g_ref[rows, :])
        total = out + norm_pull(unit, scale, vec_ref[6:7, :], grad)
        grad_ref[rows, :] = total
        low_ref[rows, :] = low(total)
        for k, v in enumerate((total, grad * unit, grad, out)):
            sums[k] = sums[k] + column_sum(v)
    for k in range(4):
        sum_ref[k : k + 1, :] = sums[k]


def norm_one_back_kernel(meta_ref, keep_ref, got_ref, zero_ref, act_ref, one_grad_ref, vec_ref, two_ref, qv_ref, up_ref, grad_ref, pack_ref, conv):
    c, x = meta_ref[3], meta_ref[2]
    sums = [jnp.zeros((1, 1024), jnp.float32) for _ in range(3)]
    for i in range(4):
        rows = slice(32 * i, 32 * i + 32)
        grad = keep_ref[rows, :] + f32(got_ref[rows, :])
        unit, scale = normed(zero_ref[rows, :])
        total = one_grad_ref[rows, :] + norm_pull(unit, scale, vec_ref[1:2, :], grad)
        grad_ref[rows, :] = total
        act = act_ref[rows, :]
        conv_grad = total * gelu_slope(act, gelu_cdf(act))
        conv[rows, :] = conv_grad
        for k, v in enumerate((conv_grad, grad * unit, grad)):
            sums[k] = sums[k] + column_sum(v)
    lane = lax.broadcasted_iota(jnp.int32, (1, 128), 1)
    for g in range(8):
        tile = slice(128 * g, 128 * g + 128)
        p, q = cross(conv[0:64, tile], conv[64:128, tile])
        pack_ref[2 * g, 0:64, :] = low(p)
        pack_ref[2 * g + 1, 0:64, :] = low(q)
        source = qv_ref[0:2, 128 * (g // 2) : 128 * (g // 2) + 128]
        even = jnp.where(lane < 64, source, 0.0) if g % 2 == 0 else jnp.where(lane < 64, turn(source), 0.0)
        heads = jnp.where(c == 0, even, turn(even))
        up_rows = []
        for k in range(4):
            piece = up_ref[0:1, 128 * (g // 2) : 128 * (g // 2) + 128]
            piece = pltpu.roll(piece, (128 - 32 * k) % 128, 1) if k else piece
            piece = jnp.where(lane < 32, piece, 0.0)
            piece = jnp.where(x == 0, piece, pltpu.roll(piece, 32, 1))
            piece = jnp.where(c == 0, piece, turn(piece))
            up_rows.append(jnp.where(meta_ref[1] == g % 2, piece, 0.0))
        all_rows = [sums[0][:, tile], sums[1][:, tile], sums[2][:, tile], heads[0:1], heads[1:2], two_ref[0:1, tile],
                    two_ref[1:2, tile], two_ref[2:3, tile], two_ref[3:4, tile], *up_rows, jnp.zeros((3, 128), jnp.float32)]
        block = jnp.concatenate(all_rows, axis=0)
        pack_ref[2 * g, 64:80, :] = low(block)
        pack_ref[2 * g + 1, 64:80, :] = low(turn(block))


def final_kernel(c_ref, grad_ref, o_ref):
    for g in range(8):
        tile = slice(128 * g, 128 * g + 128)
        a, b = cross(f32(c_ref[2 * g]), f32(c_ref[2 * g + 1]))
        o_ref[0:64, tile] = grad_ref[0:64, tile] + a
        o_ref[64:128, tile] = grad_ref[64:128, tile] + b


def related(lens_ref, block):
    row = lax.broadcasted_iota(jnp.int32, (128, 128), 0)
    col = lax.broadcasted_iota(jnp.int32, (128, 128), 1)
    first = jnp.zeros((128, 128), jnp.int32)
    last = jnp.full((128, 128), 128, jnp.int32)
    e = 0
    for i in range(4):
        e = e + lens_ref[block * 4 + i]
        first = jnp.maximum(first, jnp.where(row >= e, e, 0))
        last = jnp.minimum(last, jnp.where(row < e, e, 128))
    return (col >= first) & (col < last)


def head_probs(query, key, rel, mine):
    masked_query = jnp.where(mine, query, jnp.zeros_like(query))
    scores = dot_nt(masked_query, key) * score_scale
    scores = jnp.where(rel, scores, -1000000000.0)
    top = jnp.max(scores, axis=-1, keepdims=True)
    expd = jnp.exp(scores - top)
    return expd / jnp.sum(expd, axis=-1, keepdims=True)


def attn_places(meta_ref, pieces, wqkv, wo):
    own, along_x, along_y, diag_a, diag_b = pieces
    y, x, c = meta_ref[1], meta_ref[2], meta_ref[3]
    groups = [[], [], [], []]
    every, low_z, high_z = slice(0, 4), slice(0, 2), slice(2, 4)
    for dy, dx, zs, src in (
        (0, 0, every, own), (0, 1, every, along_x), (1, 0, every, along_y), (1, 1, low_z, diag_a), (1, 1, high_z, diag_b)
    ):
        yy, xx = y ^ dy, x ^ dx
        for i in range(8):
            place = wqkv.at[i % 3, zs, yy, c ^ (i // 3), xx] if i < 6 else wo.at[i - 6, zs, yy, xx]
            groups[i % 3 if i < 6 else 3].append((src.at[:, i], place))
    return groups


def attn_scratch():
    return [pltpu.VMEM((3, 4, 2, 2, 2, 32, 512), BF), pltpu.VMEM((2, 4, 2, 2, 32, 512), BF)]


def attn_fwd_kernel(
    meta_ref, lens_ref, n_ref, n_other_ref, own, along_x, along_y, diag_a, diag_b, bias_ref,
    q_ref, k_ref, v_ref, m_ref, keep_ref, send_ref, wqkv, wo, ready,
):
    n = jnp.concatenate([n_ref[...], n_other_ref[...]], axis=0)
    ready(0)
    q_ref[...] = low(dot(n, wqkv[0].reshape(1024, 512)) + bias_ref[0:1, :])
    ready(1)
    k_ref[...] = low(dot(n, wqkv[1].reshape(1024, 512)))
    ready(2)
    v_ref[...] = low(dot(n, wqkv[2].reshape(1024, 512)) + bias_ref[1:2, :])
    half = lax.broadcasted_iota(jnp.int32, (128, 128), 1) // 64
    for b in range(2):
        rel = related(lens_ref, meta_ref[0] ^ b)
        for p in range(4):
            at = (slice(128 * b, 128 * b + 128), slice(128 * p, 128 * p + 128))
            query, key, value = q_ref[at], k_ref[at], v_ref[at]
            outs = [dot(low(head_probs(query, key, rel, half == h)), value) for h in range(2)]
            m_ref[at] = low(jnp.where(half == 0, outs[0], outs[1]))
    mixed = m_ref[...]
    ready(3)
    for h in range(2):
        out = dot(mixed, wo[h].reshape(512, 512))
        keep_ref[:, 512 * h : 512 * h + 512] = out[0:128]
        send_ref[:, 512 * h : 512 * h + 512] = low(out[128:256])


def attn_bwd_kernel(
    meta_ref, lens_ref, g_ref, g_other_ref, q_ref, k_ref, v_ref, own, along_x, along_y, diag_a, diag_b,
    dq_ref, dk_ref, dv_ref, sum_ref, keep_ref, send_ref, wqkv, wo, ready,
):
    grad_in = jnp.concatenate([g_ref[...], g_other_ref[...]], axis=0)
    ready(3)
    mixed_grad = low(dot_nt(grad_in[:, 0:512], wo[0].reshape(512, 512)) + dot_nt(grad_in[:, 512:1024], wo[1].reshape(512, 512)))
    half = lax.broadcasted_iota(jnp.int32, (128, 128), 1) // 64
    for p in range(4):
        sums = []
        for b in range(2):
            rel = related(lens_ref, meta_ref[0] ^ b)
            at = (slice(128 * b, 128 * b + 128), slice(128 * p, 128 * p + 128))
            query, key, value = q_ref[at], k_ref[at], v_ref[at]
            grad = mixed_grad[128 * b : 128 * b + 128, 128 * p : 128 * p + 128]
            dqs, dks, dvs = [], [], []
            for h in range(2):
                probs = head_probs(query, key, rel, half == h)
                grad_h = jnp.where(half == h, grad, jnp.zeros_like(grad))
                prob_grad = dot_nt(grad_h, value)
                dvs.append(dot_tn(low(probs), grad))
                score_grad = probs * (prob_grad - jnp.sum(probs * prob_grad, axis=-1, keepdims=True))
                score_low = low(score_grad)
                dqs.append(dot(score_low, key) * score_scale)
                dks.append(dot_tn(score_low, query) * score_scale)
            dq = jnp.where(half == 0, dqs[0], dqs[1])
            dk = jnp.where(half == 0, dks[0], dks[1])
            dv = jnp.where(half == 0, dvs[0], dvs[1])
            dq_ref[at], dk_ref[at], dv_ref[at] = low(dq), low(dk), low(dv)
            sums.append((column_sum(dq), column_sum(dv)))
        sum_ref[0:1, 128 * p : 128 * p + 128] = sums[0][0] + sums[1][0]
        sum_ref[1:2, 128 * p : 128 * p + 128] = sums[0][1] + sums[1][1]
    for j in range(3):
        ready(j)
    out = dot_nt(dq_ref[...], wqkv[0].reshape(1024, 512))
    out += dot_nt(dk_ref[...], wqkv[1].reshape(1024, 512))
    out += dot_nt(dv_ref[...], wqkv[2].reshape(1024, 512))
    keep_ref[...] = out[0:128]
    send_ref[...] = low(out[128:256])


def term_plan(meta_ref, own, send_x, send_y, keep_a, keep_b, gqkv, go):
    y, x, c = meta_ref[1], meta_ref[2], meta_ref[3]
    plan = []
    for dy, dx in ((0, 0), (0, 1), (1, 0), (1, 1)):
        yy, xx = y ^ dy, x ^ dx
        for i in range(8):
            if dy == 0 and dx == 0:
                part = own.at[:, i]
            elif i < 4:
                part = send_x.at[dy, :, i] if dx == 1 else keep_a.at[:, i]
            else:
                part = send_y.at[dx, :, i - 4] if dy == 1 else keep_b.at[:, i - 4]
            plan.append((gqkv.at[i % 3, :, yy, c ^ (i // 3), xx] if i < 6 else go.at[i - 6, :, yy, xx], part))
    return plan


def attn_term_kernel(meta_ref, n_ref, n_other_ref, dq_ref, dk_ref, dv_ref, m_ref, g_ref, g_other_ref, own, send_x, send_y, keep_a, keep_b, gqkv, go, sems):
    plan = term_plan(meta_ref, own, send_x, send_y, keep_a, keep_b, gqkv, go)
    copies = [pltpu.make_async_copy(a, b, sems.at[k]) for k, (a, b) in enumerate(plan)]

    def leave(weight):
        for k, copy in enumerate(copies):
            if (k % 8 % 3 if k % 8 < 6 else 3) == weight:
                copy.start()

    columns = [slice(256 * z, 256 * z + 256) for z in range(4)]
    n = [jnp.concatenate([n_ref[:, cols], n_other_ref[:, cols]], axis=0) for cols in columns]
    for j, ref in enumerate((dq_ref, dk_ref, dv_ref)):
        for z in range(4):
            gqkv[j, z] = low(dot_tn(n[z], ref[...])).reshape(2, 2, 2, 32, 512)
        leave(j)
    grad = jnp.concatenate([g_ref[...], g_other_ref[...]], axis=0)
    for z in range(4):
        term = low(dot_tn(m_ref[:, 128 * z : 128 * z + 128], grad))
        for h in range(2):
            go[h, z] = term[:, 512 * h : 512 * h + 512].reshape(2, 2, 32, 512)
    leave(3)
    for copy in copies:
        copy.wait()


def ffn_plan(both, wu, wd):
    return [[(both.at[:, 0:256], wu)], [(both.at[:, 256:384], wd.at[0]), (both.at[:, 384:512], wd.at[1])]]


def ffn_scratch():
    return [pltpu.VMEM((4, 256, 512), BF), pltpu.VMEM((2, 4, 128, 512), BF)]


def ffn_kernel(*refs):
    n_refs, g_refs, bias_ref = refs[0:8], refs[8:16], refs[17]
    act_ref, ug_ref, keep_ref, send_ref, sum_ref, wu, wd, ready = refs[18:26]
    ready(0)
    total = jnp.zeros((1, 512), jnp.float32)
    for i in (4, 5, 6, 7, 0, 1, 2, 3):
        rows = slice(128 * i, 128 * i + 128)
        up_pre = dot(n_refs[i][...], wu[...].reshape(1024, 512)) + bias_ref[...]
        cdf = gelu_cdf(up_pre)
        act_ref[rows, :] = low(up_pre * cdf)
        if i == 4:
            ready(1)
        act_grad = dot_nt(g_refs[i][:, 0:512], wd[0].reshape(512, 512)) + dot_nt(g_refs[i][:, 512:1024], wd[1].reshape(512, 512))
        up_grad = act_grad * gelu_slope(up_pre, cdf)
        total = total + column_sum(up_grad)
        ug_ref[rows, :] = low(up_grad)
        back = dot_nt(low(up_grad), wu[...].reshape(1024, 512))
        if i >= 4:
            send_ref[128 * i - 512 : 128 * i - 384, :] = low(back)
        else:
            keep_ref[rows, :] = back
    sum_ref[...] = total


def ffn_out_kernel(act_ref, both_ref, keep_ref, send_ref, wd, ready):
    ready(0)
    for h in range(2):
        cols = slice(512 * h, 512 * h + 512)
        keep_ref[:, cols] = dot(act_ref[0:512, :], wd[h].reshape(512, 512))
        send_ref[:, cols] = low(dot(act_ref[512:1024, :], wd[h].reshape(512, 512)))


def half_sum_kernel(keep_ref, got_ref, own_ref, x_ref, y_ref, across_ref):
    own_ref[...] = keep_ref[0:128, :] + f32(got_ref[0:128, :])
    for i, ref in enumerate((x_ref, y_ref, across_ref), 1):
        rows = slice(128 * i, 128 * i + 128)
        ref[...] = low(keep_ref[rows, :] + f32(got_ref[rows, :]))


def ffn_terms(act, grads, normeds, up_grad, after, cost=20):
    def body(*refs):
        act_ref, g_refs, n_refs, u_ref, out_ref = refs[0], refs[1:9], refs[9:17], refs[17], refs[-1]
        n = jnp.concatenate([ref[...] for ref in n_refs], axis=0)
        out_ref[0, 0:256] = low(dot_tn(n, u_ref[...]))
        g = jnp.concatenate([ref[...] for ref in g_refs], axis=0)
        down = low(dot_tn(act_ref[...], g))
        out_ref[0, 256:384] = down[:, 0:512]
        out_ref[0, 384:512] = down[:, 512:1024]

    rows = pl.BlockSpec((128, 1024), lambda i: (0, 0))
    part = pl.BlockSpec((128, 256), lambda i: (0, i))
    return pl.pallas_call(
        body,
        grid=(4,),
        in_specs=[pl.BlockSpec((1024, 128), lambda i: (0, i))] + [rows] * 8 + [part] * 8
        + [pl.BlockSpec((1024, 512), lambda i: (0, 0))] + [ANY] * len(after),
        out_specs=pl.BlockSpec((1, 512, 512), lambda i: (i, 0, 0)),
        out_shape=out_hbm(shape((4, 512, 512))),
        compiler_params=pltpu.CompilerParams(vmem_limit_bytes=20 << 20),
        cost_estimate=estimate(20),
    )(act, grads[0], *[in_hbm(v) for v in grads[1:]], normeds[0], *[in_hbm(v) for v in normeds[1:]], up_grad, *after)


def fold_call(keep_a, keep_b, got_x, got_y, after, cost=3):
    def body(a_ref, b_ref, x_ref, y_ref, *refs):
        refs[-2][...] = low(f32(a_ref[...]) + f32(x_ref[0]))
        refs[-1][...] = low(f32(b_ref[...]) + f32(y_ref[0]))

    part = pl.BlockSpec((2, 4, 32, 512), lambda i: (i, 0, 0, 0))
    second = pl.BlockSpec((1, 2, 4, 32, 512), lambda i: (1, i, 0, 0, 0))
    return pl.pallas_call(
        body,
        grid=(2,),
        in_specs=[part, part, second, second] + [ANY] * len(after),
        out_specs=[part, part],
        out_shape=[out_hbm(shape((4, 4, 32, 512)))] * 2,
        compiler_params=pltpu.CompilerParams(vmem_limit_bytes=16 << 20),
        cost_estimate=estimate(cost),
    )(in_hbm(keep_a), in_hbm(keep_b), in_hbm(got_x), in_hbm(got_y), *after)


def join_call(own, got_x, got_y, last_a, last_b, after, cost=3):
    def body(own_ref, x_ref, y_ref, a_ref, b_ref, *refs):
        refs[-1][:, 0:4] = low(f32(own_ref[:, 0:4]) + f32(x_ref[0]) + f32(a_ref[...]))
        refs[-1][:, 4:8] = low(f32(own_ref[:, 4:8]) + f32(y_ref[0]) + f32(b_ref[...]))

    full = pl.BlockSpec((2, 8, 32, 512), lambda i: (i, 0, 0, 0))
    part = pl.BlockSpec((2, 4, 32, 512), lambda i: (i, 0, 0, 0))
    first = pl.BlockSpec((1, 2, 4, 32, 512), lambda i: (0, i, 0, 0, 0))
    return pl.pallas_call(
        body,
        grid=(2,),
        in_specs=[full, first, first, part, part] + [ANY] * len(after),
        out_specs=full,
        out_shape=out_hbm(shape((4, 8, 32, 512))),
        compiler_params=pltpu.CompilerParams(vmem_limit_bytes=16 << 20),
        cost_estimate=estimate(cost),
    )(in_hbm(own), in_hbm(got_x), in_hbm(got_y), in_hbm(last_a), in_hbm(last_b), *after)


def output_kernel(one_ref, keep_ref, got_ref, got_y_ref, got_d_ref, vec_ref, o_ref):
    got = f32(got_ref[...]) + f32(got_y_ref[...]) + f32(got_d_ref[...])
    o_ref[...] = low(one_ref[...] + keep_ref[...] + got + vec_ref[8:9, :])


def up_grad_kernel(got_ref, sum_ref, up_ref, down_ref):
    for z in range(4):
        for k in range(8):
            at = 128 * (8 * z + k)
            up_ref[:, at : at + 128] = f32(got_ref[k, :, 128 * z : 128 * z + 128])
    down_ref[:, 0:512] = f32(sum_ref[256:384])
    down_ref[:, 512:1024] = f32(sum_ref[384:512])


def qkv_grad_kernel(meta_ref, sum_ref, got_ref, q_ref, k_ref, v_ref, o_ref):
    c = meta_ref[3]
    for j, ref in enumerate((q_ref, k_ref, v_ref)):
        for t in range(4):
            tile = slice(128 * t, 128 * t + 128)
            mine, theirs = f32(sum_ref[j, :, tile]), f32(got_ref[3 + j, :, tile])
            a, b = cross(jnp.where(c == 0, mine, theirs), jnp.where(c == 0, theirs, mine))
            ref[:, 256 * t : 256 * t + 128] = a
            ref[:, 256 * t + 128 : 256 * t + 256] = b
    for h in range(2):
        o_ref[:, 512 * h : 512 * h + 512] = f32(sum_ref[6 + h])


def swap(v, axis):
    return lax.ppermute(v, axis, [(0, 1), (1, 0)])


def swap_across(v):
    return lax.ppermute(v, ("y", "x"), [(i, 3 - i) for i in range(4)])


def gather_z(v):
    return lax.all_gather(v, "z", axis=0, tiled=False)


def scatter_z(v):
    return lax.psum_scatter(v, "z", scatter_dimension=0, tiled=False)


def pick(v, index, axis):
    return lax.dynamic_index_in_dim(v, index, axis, keepdims=False)


def local(
    frames, lengths, cotangent, conv_kernel, conv_bias, norm_one_gain, norm_one_bias,
    query_weight, query_bias, key_weight, value_weight, value_bias, out_weight, out_bias,
    norm_two_gain, norm_two_bias, up_weight, up_bias, down_weight, down_bias,
):
    zi, yi, ci, xi = (lax.axis_index(a) for a in ("z", "y", "c", "x"))
    meta = jnp.stack([(zi * 2 + yi) * 2 + ci, yi, xi, ci]).astype(jnp.int32)
    row, row_f, half = shape((128, 1024)), shape((128, 1024), F32), shape((256, 512))
    groups, plane = ("z", "y", "c"), ("y", "c", "x")

    def spread_plane(own, along_x, along_y, across):
        four = (own, along_x, along_y, across)
        return (*four, *(swap(v, "c") for v in four))

    def half_sum(keep, send, saved, cost, after):
        return whole_call(
            half_sum_kernel, (keep, swap(send, "c")), [saved, VMEM], [row_f, row, row, row], [saved] + [VMEM] * 3, cost=cost, after=after
        )

    vectors = (conv_bias, norm_one_gain, norm_one_bias, query_bias, value_bias, out_bias, norm_two_gain, norm_two_bias, down_bias, up_bias)
    qkv_mine, qkv_theirs, out_part, small = whole_call(
        first_kernel, (lengths, *vectors, query_weight, key_weight, value_weight, out_weight), [None] * 15,
        [shape((3, 32, 512)), shape((3, 32, 512)), shape((2, 32, 512)), shape((16, 128), F32)], [VMEM] * 4, cost=0.05, after=(),
    )
    attn_part = jnp.concatenate([qkv_mine, swap(qkv_theirs, "c"), out_part], axis=0)
    attn_own = gather_z(attn_part)

    up_split, grad_out, grad_send = whole_call(
        ffn_prep_kernel, (lengths, up_weight, cotangent), [None] * 3, [shape((8, 32, 512)), row, row], [VMEM] * 3, cost=0.05, after=(qkv_mine,)
    )
    grad_y = swap(grad_send, "y")
    up_part = lax.all_to_all(up_split, plane, 0, 0, tiled=True)

    payload = whole_call(pack_kernel, (frames, small), [None, VMEM], shape((16, 80, 128)), VMEM, cost=0.05, after=(in_hbm(attn_part), in_hbm(grad_y)))
    got = lax.all_to_all(payload, groups, 0, 0, tiled=True)
    kernel_other = swap(conv_kernel, "x")
    grad_x = swap(tie(grad_send, kernel_other), "x")
    lens = got[:, 77, 0:4].astype(jnp.int32).reshape(64)
    ffn_part = jnp.concatenate([up_part.reshape(256, 512), down_weight[:, :512], down_weight[:, 512:]], axis=0)
    ffn_both = gather_z(ffn_part)
    conv_out = conv_pass(conv_fwd_kernel, lens, meta, got, conv_kernel, kernel_other, cost=30, after=(in_hbm(attn_own), in_hbm(grad_x)))
    conv_got = lax.all_to_all(conv_out, groups, 0, 0, tiled=True)

    grad_d = swap_across(tie(grad_send, kernel_other))
    grads_out = spread_plane(grad_out, grad_x, grad_y, grad_d)
    attn_own = attn_own
    attn_x, attn_y = swap(attn_own, "x"), swap(attn_own, "y")
    diag_a, diag_b = swap(attn_x[0:2], "y"), swap(attn_y[2:4], "x")
    attn_pieces = (attn_own, attn_x, attn_y, diag_a, diag_b)

    got_small = got[:, 64:80]
    got_small_other = swap(got_small, "x")
    vec, up_bias_own, qv_bias = whole_call(
        vector_kernel, (meta, got_small, got_small_other), [SMEM, VMEM, VMEM],
        [shape((16, 1024), F32), shape((1, 512), F32), shape((2, 512), F32)], [VMEM] * 3, cost=3, after=(conv_out,),
    )
    conv_act, hidden_zero, zero_saved, n_one = whole_call(
        norm_one_kernel, (conv_got, frames, vec), [VMEM, None, VMEM], [row_f, row_f, row_f, row], [None, VMEM, None, VMEM],
        cost=1, after=(*(in_hbm(v) for v in grads_out[3:]), in_hbm(attn_x), in_hbm(attn_y)),
    )
    n_one_other = swap(n_one, "c")

    def attn_copies(first):
        return lambda *refs: attn_places(refs[0], refs[first : first + 5], refs[-2], refs[-1])

    query, key, value, mixed, attn_keep, attn_send = whole_call(
        attn_fwd_kernel, (meta, lens, n_one, n_one_other, *attn_pieces, qv_bias), [SMEM, SMEM, VMEM, VMEM] + [ANY] * 5 + [VMEM],
        [half] * 4 + [row_f, row], [None] * 4 + [VMEM] * 2, attn_scratch(), plan=attn_copies(4), vmem=16, cost=8, after=(),
    )
    hidden_one, n_two = whole_call(
        norm_two_kernel, (hidden_zero, attn_keep, swap(attn_send, "c"), vec), [VMEM] * 4, [row_f, row], [VMEM] * 2,
        cost=0.1, after=(in_hbm(ffn_both),),
    )

    n_twos = spread_plane(n_two, swap(n_two, "x"), swap(n_two, "y"), swap_across(n_two))
    many, many_f, many_half = shape((1024, 512)), shape((512, 1024), F32), shape((512, 1024))
    activated, up_grad, back_keep, back_send, up_bias_term = whole_call(
        ffn_kernel, (*n_twos, *grads_out, ffn_both, up_bias_own), ([VMEM] + [None] * 7) * 2 + [ANY, VMEM],
        [many, many, many_f, many_half, shape((1, 512), F32)], [VMEM] * 5, ffn_scratch(),
        plan=lambda *refs: ffn_plan(refs[16], refs[-2], refs[-1]), vmem=20, cost=30,
    )
    two_own, two_x, two_y, two_across = half_sum(back_keep, back_send, VMEM, 0.05, ())
    ffn_keep, ffn_send = whole_call(
        ffn_out_kernel, (activated, ffn_both), [None, ANY], [many_f, many_half], [None, None], ffn_scratch()[1:],
        plan=lambda *refs: ffn_plan(refs[1], None, refs[-1])[1:], cost=1, after=(two_x,),
    )
    two_got = (swap(two_x, "x"), swap(two_y, "y"), swap_across(two_across))
    ffn_term = ffn_terms(activated, grads_out, n_twos, up_grad, (two_x,), 20)
    one_grad, attn_grad, two_sums = whole_call(
        norm_two_back_kernel, (two_own, *two_got, hidden_one, grad_out, vec), [VMEM] * 7, [row_f, row, shape((4, 1024), F32)],
        [None, VMEM, None], cost=5, after=(in_hbm(ffn_term), in_hbm(ffn_send)),
    )
    attn_grad_other = swap(attn_grad, "c")
    ffn_sum = scatter_z(ffn_term)
    dq, dk, dv, qv_sum, one_keep, one_send = whole_call(
        attn_bwd_kernel, (meta, lens, attn_grad, attn_grad_other, query, key, value, *attn_pieces),
        [SMEM, SMEM, VMEM, VMEM] + [None] * 3 + [ANY] * 5, [half] * 3 + [shape((2, 512), F32), row_f, row], [VMEM] * 6, attn_scratch(),
        plan=attn_copies(7), vmem=16, cost=70, after=(),
    )
    zero_grad, payload_back = whole_call(
        norm_one_back_kernel, (meta, one_keep, swap(one_send, "c"), zero_saved, conv_act, one_grad, vec, two_sums, qv_sum, up_bias_term),
        [SMEM, VMEM, VMEM, None, None, None, VMEM, None, VMEM, VMEM], [row_f, shape((16, 80, 128))], [None, VMEM],
        [pltpu.VMEM((128, 1024), F32)], cost=10, after=(),
    )
    grad_got = lax.all_to_all(payload_back, groups, 0, 0, tiled=True)
    out_own, out_x, out_y, out_across = half_sum(ffn_keep, ffn_send, None, 0.05, (payload_back,))

    piece, part = out_hbm(shape((4, 8, 32, 512))), out_hbm(shape((4, 4, 32, 512)))
    pair = out_hbm(shape((2, 4, 4, 32, 512)))
    term_own, term_x, term_y, keep_a, keep_b = whole_call(
        attn_term_kernel, (meta, n_one, n_one_other, dq, dk, dv, mixed, attn_grad, attn_grad_other),
        [SMEM, VMEM, VMEM] + [None] * 4 + [VMEM] * 2, [piece, pair, pair, part, part], [HBM] * 5,
        attn_scratch() + [pltpu.SemaphoreType.DMA((32,))], vmem=16, cost=1, after=(payload_back,),
    )
    got_x, got_y = swap(term_x, "x"), swap(term_y, "y")
    conv_back_out = conv_pass(conv_back_kernel, lens, meta, grad_got, conv_kernel, kernel_other, cost=10, after=(out_x,))
    send_a, send_b = fold_call(keep_a, keep_b, got_x, got_y, (conv_back_out,), 3)
    back_got = lax.all_to_all(conv_back_out, groups, 0, 0, tiled=True)
    out_got = (swap(tie(out_x, send_b), "x"), swap(tie(out_y, send_b), "y"), swap_across(tie(out_across, send_b)))
    kernel_keep, kernel_send = conv_grads(lens, meta, got, grad_got, cost=30, after=(conv_back_out,))
    last_a, last_b = swap(send_a, "y"), swap(send_b, "x")
    attn_half = join_call(term_own, got_x, got_y, last_a, last_b, (in_hbm(kernel_send), back_got, in_hbm(ffn_sum)), 3)
    attn_sum = scatter_z(attn_half)

    frames_grad = whole_call(final_kernel, (back_got, zero_grad), [VMEM, None], row_f, None, cost=0.05, after=(in_hbm(attn_half),))
    output = whole_call(
        output_kernel, (hidden_one, out_own, *out_got, vec), [VMEM, None] + [VMEM] * 4, row, None, cost=0.05, after=(in_hbm(attn_half),)
    )
    kernel_grad = kernel_keep + f32(swap(kernel_send, "x"))
    ffn_sum = tie(ffn_sum, attn_half)
    up_got = lax.all_to_all(ffn_sum[0:256].reshape(8, 32, 512), plane, 0, 0, tiled=True)
    up_weight_grad, down_weight_grad = whole_call(
        up_grad_kernel, (up_got, ffn_sum), [VMEM, None], [shape((32, 4096), F32), shape((128, 1024), F32)], [None] * 2, cost=0.05
    )
    small_sum = jnp.sum(f32(grad_got[:, 64:80, 0:64]), axis=0).reshape(16, 2, 32)
    small_grad = pick(small_sum, xi, 1) + swap(tie(pick(small_sum, 1 - xi, 1), send_a), "x")
    small_grads = [small_grad[i] for i in range(9)]
    attn_sum = tie(attn_sum, output, up_weight_grad, kernel_grad, small_grad, frames_grad)
    query_weight_grad, key_weight_grad, value_weight_grad, out_weight_grad = whole_call(
        qkv_grad_kernel, (meta, attn_sum, swap(attn_sum, "c")), [SMEM, None, VMEM], [shape((32, 1024), F32)] * 4, [None] * 4
    )

    return (
        output, frames_grad, kernel_grad, small_grads[0], small_grads[1], small_grads[2], query_weight_grad, small_grads[3],
        key_weight_grad, value_weight_grad, small_grads[4], out_weight_grad, small_grads[5], small_grads[6], small_grads[7],
        up_weight_grad, small_grad[9:13].reshape(128), down_weight_grad, small_grads[8],
    )


MATRICES_IN = (0, 1, 2, 3, 7, 9, 10, 12, 16, 18)
MATRICES_OUT = (0, 1, 2, 6, 8, 9, 11, 15, 17)


def solution(mesh):
    n_dp, n_fsdp = mesh.shape["dp"], mesh.shape["fsdp"]
    if n_fsdp == 2 and n_dp == GROUPS:
        axes = ("z", "y", "c", "x")
        mesh = Mesh(mesh.devices.reshape(n_dp // 4, 2, 2, n_fsdp), axes)
        body = local
    else:
        axes = ("dp", "fsdp")
        body = local_plain
    in_specs = tuple(P(axes, None) if i in MATRICES_IN else P(axes) for i in range(20))
    out_specs = tuple(P(axes, None) if i in MATRICES_OUT else P(axes) for i in range(19))
    return jax.shard_map(body, mesh=mesh, in_specs=in_specs, out_specs=out_specs, check_vma=False)
```
